32 devices in a mesh: dp: 16 (over z, y, x), fsdp: 2 (over core).
Axes of the slice: x: 2, y: 2, z: 4, core: 2. Of those that a mesh axis runs over, the one named last changes fastest.
Arguments:
- tokens: bfloat16 [32, 256, 768], P(('dp', 'fsdp')), may hold values from -6 to 6
- lengths: int32 [32], P(('dp', 'fsdp')), may hold values from 64 to 256, as said below
- cotangent: bfloat16 [32, 256, 768], P(('dp', 'fsdp')), may hold values from -6 to 6
- gain: bfloat16 [768], P('fsdp'), may hold values from 0.5 to 1.5
- w_in: bfloat16 [768, 3072], P('fsdp'), may hold values from -0.21875 to 0.21875
- conv_w: bfloat16 [4, 1536], P(None, 'fsdp'), may hold values from -3 to 3
- conv_b: bfloat16 [1536], P('fsdp'), may hold values from -1.5 to 1.5
- w_x: bfloat16 [1536, 80], P('fsdp'), may hold values from -0.15625 to 0.15625
- w_dt: bfloat16 [48, 1536], P(None, 'fsdp'), may hold values from -0.875 to 0.875
- dt_bias: bfloat16 [1536], P('fsdp'), may hold values from -6.875 to -2.296875
- a_log: bfloat16 [16, 1536], P(None, 'fsdp'), may hold values from 0 to 2.765625
- d_skip: bfloat16 [1536], P('fsdp'), may hold values from 0.5 to 1.5
- w_out: bfloat16 [1536, 768], P('fsdp'), may hold values from -0.15625 to 0.15625
Outputs:
- output: bfloat16 [32, 256, 768], P(('dp', 'fsdp'))
- input_grad: float32 [32, 256, 768], P(('dp', 'fsdp'))
- grad_gain: float32 [768], P('fsdp')
- grad_in: float32 [768, 3072], P('fsdp')
- grad_conv_w: float32 [4, 1536], P(None, 'fsdp')
- grad_conv_b: float32 [1536], P('fsdp')
- grad_x: float32 [1536, 80], P('fsdp')
- grad_dt: float32 [48, 1536], P(None, 'fsdp')
- grad_dt_bias: float32 [1536], P('fsdp')
- grad_a_log: float32 [16, 1536], P(None, 'fsdp')
- grad_skip: float32 [1536], P('fsdp')
- grad_out: float32 [1536, 768], P('fsdp')
The draws below stay inside these ranges and needn't reach their ends.
Inputs may be any that keep to these rules, and one draw needn't show every extreme that they name: A sequence's first lengths tokens are real and the rest padding; in every draw some sequence has 256 tokens and some has 64.
All inputs are finite; a program needn't handle non-finite values.
Results may differ from the reference program's by a relative error of at most 0.012.
Values may be sent and summed in bfloat16 or wider, within the bound.
A program may use at most 128 MiB of HBM per device.

```python
from functools import partial
import jax
import jax.numpy as jnp
from jax import lax

D_MODEL = 768
D_INNER = 1536
STATE = 16
RANK = 48
CONV = 4
LEN = 256
BLOCK = 64
SEQS = 32


def draw_lengths(key, part):
    key = jax.random.fold_in(key, 7)
    subkeys = jax.random.split(key, 2)
    length_span = LEN - LEN // 4 + 1
    uniform_ints = jax.random.randint(subkeys[0], (2, SEQS), 0, length_span)
    length_draw = jnp.min(uniform_ints, axis=0) + LEN // 4
    shuffled = jax.random.permutation(subkeys[1], SEQS)
    length_draw = length_draw.at[shuffled[0]].set(LEN)
    length_draw = length_draw.at[shuffled[1]].set(LEN // 4)
    return length_draw.astype(jnp.int32)


def levels(own_key, extent, shards, low, largest):
    def one(axis_at, blocks):
        heights = jax.random.uniform(jax.random.fold_in(jax.random.fold_in(own_key, 6), axis_at), (blocks,), jnp.float32, low / len(shards), largest / len(shards))
        return jnp.repeat(jnp.exp(heights), extent[axis_at] // blocks).reshape((-1,) + (1,) * (len(extent) - axis_at - 1))

    loudness = one(*shards[0])
    for cut in shards[1:]:
        loudness = loudness * one(*cut)
    return loudness


def scatter_about(stream_key, shape, deviation, most, cuts=(), kind=jnp.bfloat16):
    entries = jax.random.normal(stream_key, shape, jnp.float32) * deviation
    if len(cuts) > 0:
        entries = levels(stream_key, shape, cuts, -0.22, 0.18) * entries
    return jnp.clip(entries, min=-most, max=most).astype(kind)


def setup_inputs(seed: int = 0) -> dict:
    keys = jax.random.split(jax.random.key(seed), 14)
    return {
        "tokens": scatter_about(keys[0], (SEQS, LEN, D_MODEL), 1.0, 6.0, ((0, 32),)),
        "lengths": draw_lengths(jax.random.fold_in(keys[13], 71), 0),
        "cotangent": scatter_about(keys[2], (SEQS, LEN, D_MODEL), 1.0, 6.0, ((0, 32),)),
        "gain": jnp.clip(1.0 + 0.1 * jax.random.normal(keys[3], (D_MODEL,), jnp.float32), 0.5, 1.5).astype(jnp.bfloat16),
        "w_in": scatter_about(keys[4], (D_MODEL, 2 * D_INNER), D_MODEL ** -0.5, 0.21875, ((0, 2),)),
        "conv_w": scatter_about(keys[5], (CONV, D_INNER), CONV ** -0.5, 3.0, ((1, 2),)),
        "conv_b": scatter_about(keys[6], (D_INNER,), 0.3, 1.5, ((0, 2),)),
        "w_x": scatter_about(keys[7], (D_INNER, RANK + 2 * STATE), D_INNER ** -0.5, 0.15625, ((0, 2),)),
        "w_dt": scatter_about(keys[8], (RANK, D_INNER), RANK ** -0.5, 0.875, ((1, 2),)),
        "dt_bias": jnp.clip(-6.875 + 4.578125 * jax.random.uniform(keys[9], (D_INNER,), jnp.float32) ** levels(keys[9], (D_INNER,), ((0, 2),), -0.2, 0.2), -6.875, -2.296875).astype(jnp.bfloat16),
        "a_log": jnp.clip(2.765625 * jax.random.uniform(keys[10], (STATE, D_INNER), jnp.float32) ** levels(keys[10], (STATE, D_INNER), ((1, 2),), -0.2, 0.2), 0.0, 2.765625).astype(jnp.bfloat16),
        "d_skip": jnp.clip(0.5 + 1.0 * jax.random.uniform(keys[11], (D_INNER,), jnp.float32) ** levels(keys[11], (D_INNER,), ((0, 2),), -0.2, 0.2), 0.5, 1.5).astype(jnp.bfloat16),
        "w_out": scatter_about(keys[12], (D_INNER, D_MODEL), D_INNER ** -0.5, 0.15625, ((0, 2),)),
    }


@jax.custom_vjp
def low(v):
    return lax.optimization_barrier(v.astype(jnp.bfloat16)).astype(jnp.float32)

@jax.custom_vjp
def low_back(v):
    return v

def low_keep(v):
    return (low(v), None)

def low_pass(kept, grad):
    return (grad,)

def back_keep(v):
    return (v, None)

def back_low(kept, grad):
    return (low(grad),)
low.defvjp(low_keep, low_pass)
low_back.defvjp(back_keep, back_low)
epsilon = 1e-05
highest = lax.Precision.HIGHEST

def product(left, right):
    return jnp.dot(left, right, precision=highest, preferred_element_type=jnp.float32)

def scan_block(carried, pieces, decay_rate):

    def stepper(current, row_data):
        dt_row, x_row, b_row, c_row = row_data
        current = jnp.exp(dt_row[None, :] * decay_rate) * current + b_row[:, None] * (dt_row * x_row)[None, :]
        return (current, lax.optimization_barrier(jnp.sum(c_row[:, None] * current, axis=0)))
    return lax.scan(stepper, carried, pieces)

def mamba_layer(params, tokens, live):
    gain, w_in, conv_w, conv_b, w_x, w_dt, dt_bias, a_log, d_skip, w_out = params
    inv_rms = lax.rsqrt(lax.optimization_barrier(jnp.mean(tokens * tokens, axis=-1, keepdims=True)) + epsilon)
    normed = low(tokens * inv_rms * gain)
    joined = low_back(product(normed, w_in))
    inner_part = joined[:, :D_INNER]
    gate_part = joined[:, D_INNER:]
    padded = jnp.concatenate([jnp.zeros((CONV - 1, D_INNER), jnp.float32), inner_part], axis=0)
    convolved = conv_b + sum((conv_w[offset] * padded[offset:offset + LEN] for offset in range(CONV)))
    active = low(jax.nn.silu(convolved))
    projected = low(low_back(product(active, w_x)))
    rank_part = projected[:, :RANK]
    b_rows = projected[:, RANK:RANK + STATE]
    c_rows = projected[:, RANK + STATE:]
    step_size = jax.nn.softplus(low_back(product(rank_part, w_dt)) + dt_bias)
    decay_rate = -jnp.exp(a_log)
    blocks = LEN // BLOCK
    pieces = tuple((value.reshape(blocks, BLOCK, value.shape[-1]) for value in (step_size, active, b_rows, c_rows)))

    def block_step(carried, block_data):
        return jax.checkpoint(scan_block)(carried, block_data, decay_rate)
    unused, scan_out = lax.scan(block_step, jnp.zeros((STATE, D_INNER), jnp.float32), pieces)
    mixed = scan_out.reshape(LEN, D_INNER) + d_skip * active
    gated = low(mixed * jax.nn.silu(gate_part))
    branch = low_back(product(gated, w_out))
    return tokens + live[:, None] * branch

def reference(tokens, lengths, cotangent, gain, w_in, conv_w, conv_b, w_x, w_dt, dt_bias, a_log, d_skip, w_out):
    params = tuple((weight.astype(jnp.float32) for weight in (gain, w_in, conv_w, conv_b, w_x, w_dt, dt_bias, a_log, d_skip, w_out)))
    positions = jnp.arange(LEN, dtype=jnp.int32)

    def one_sequence(totals, sequence_data):
        sequence, length, incoming = sequence_data
        live = (positions < length).astype(jnp.float32)
        result, pullback = jax.vjp(partial(mamba_layer, live=live), params, sequence.astype(jnp.float32))
        weight_grads, token_grad = pullback(incoming.astype(jnp.float32))
        totals = tuple((running + grad_part for running, grad_part in zip(totals, weight_grads)))
        return (totals, (result.astype(jnp.bfloat16), token_grad))
    zeros_init = tuple((jnp.zeros_like(weight) for weight in params))
    totals, (output, input_grad) = lax.scan(one_sequence, zeros_init, (tokens, lengths, cotangent))
    grad_gain, grad_in, grad_conv_w, grad_conv_b, grad_x, grad_dt, grad_dt_bias, grad_a_log, grad_skip, grad_out = totals
    return (output, input_grad, grad_gain, grad_in, grad_conv_w, grad_conv_b, grad_x, grad_dt, grad_dt_bias, grad_a_log, grad_skip, grad_out)
```

```python
import functools
import jax
import jax.numpy as jnp
from jax import lax
from jax.experimental import pallas as pl
from jax.experimental.pallas import tpu as pltpu
from jax.sharding import PartitionSpec as P

F32 = jnp.float32
BF16 = jnp.bfloat16
EPS = 1e-05
STEPS = 16
LOG2E = 1.4426950408889634
VMEM = pl.BlockSpec(memory_space=pltpu.VMEM)
SMEM = pl.BlockSpec(memory_space=pltpu.SMEM)
MB = 2**20


def dot(left, right, over=(1, 0)):
    dims = (((over[0],), (over[1],)), ((), ()))
    return lax.dot_general(left, right, dims, preferred_element_type=F32)


def each(count, width, step):
    def run(index, carry):
        step(pl.ds(pl.multiple_of(index * width, width), width))
        return carry

    lax.fori_loop(0, count, run, 0)


def rows_of(block, size):
    return pl.ds(pl.multiple_of(block * size, size), size)


def compute_kernel(
    length_ref, tok, cot, gain, w_in, conv_w, conv_b, w_x, w_dt, dt_bias, a_log, d_skip, w_out,
    output, input_grad, normed, gated, d_branch, d_joined, g_gain, g_rows, g_dt, g_xt,
    inv, inner, gact, gslope, cslope, active, proj, cmat, bmat, spread, decay,
    step_s, drive, sigp, mixed, d_mixed, lam_b, d_decay, states, carry, lam_s, part_s,
    db, dc, d_pre_low, d_proj, d_conv, d_normed,
):
    T, D = tok.shape
    E = w_out.shape[0]
    N = a_log.shape[0]
    R = w_dt.shape[0]
    J = w_x.shape[1]
    K = conv_w.shape[0]
    NB = T // STEPS
    WIDE = STEPS * N
    PAD = 8

    def prepare(block, c):
        rows = rows_of(block, 64)
        x = tok[rows, :].astype(F32)
        scale = lax.rsqrt(jnp.mean(x * x, axis=1, keepdims=True) + EPS)
        inv[rows, :] = jnp.broadcast_to(scale, (64, 128))
        normed[rows, :] = (x * scale * gain[...].astype(F32)).astype(BF16)
        at = block * 64 + lax.broadcasted_iota(jnp.int32, (64, 1), 0)
        live = (at < length_ref[0]).astype(F32)
        d_branch[rows, :] = (live * cot[rows, :].astype(F32)).astype(BF16)
        return c

    lax.fori_loop(0, T // 64, prepare, 0)

    inner[pl.ds(0, PAD), :] = jnp.zeros((PAD, E), F32)

    def project_in(cols):
        inner[pl.ds(PAD, T), cols] = dot(normed[...], w_in[:, cols])

    each(E // 256, 256, project_in)

    def convolve(cols):
        taps = conv_w[:, cols].astype(F32)
        value = conv_b[:, cols].astype(F32) + sum(
            taps[k : k + 1] * inner[pl.ds(PAD - K + 1 + k, T), cols] for k in range(K)
        )
        sigma = jax.nn.sigmoid(value)
        active[:, cols] = (value * sigma).astype(BF16)
        cslope[:, cols] = sigma * (1.0 + value * (1.0 - sigma))

    each(E // 128, 128, convolve)

    def project_gate(index, c):
        source = pl.ds(pl.multiple_of(E + index * 256, 256), 256)
        cols = rows_of(index, 256)
        value = dot(normed[...], w_in[:, source])
        sigma = jax.nn.sigmoid(value)
        gact[:, cols] = value * sigma
        gslope[:, cols] = sigma * (1.0 + value * (1.0 - sigma))
        return c

    lax.fori_loop(0, E // 256, project_gate, 0)

    proj[...] = dot(active[...], w_x[...]).astype(BF16)

    row = lax.broadcasted_iota(jnp.int32, (J, WIDE), 0)
    col = lax.broadcasted_iota(jnp.int32, (J, WIDE), 1)
    at = lax.broadcasted_iota(jnp.int32, (T, WIDE), 0)
    to = lax.broadcasted_iota(jnp.int32, (T, WIDE), 1)
    diagonal = (at % STEPS == to // N).astype(F32)
    pick_b = (row == R + col % N).astype(BF16)
    pick_c = (row == R + N + col % N).astype(BF16)
    bmat[...] = (dot(proj[...], pick_b) * diagonal).astype(BF16)
    cmat[...] = (dot(proj[...], pick_c) * diagonal).astype(BF16)
    ones = jnp.ones((STEPS, 128), BF16)

    def spread_rows(source):
        def run(block, c):
            spread[rows_of(block, WIDE), :] = dot(source[rows_of(block, STEPS), :], ones, (0, 0))
            return c

        lax.fori_loop(0, NB, run, 0)

    spread_rows(bmat)

    def step_size(cols):
        pre = dot(proj[:, :R], w_dt[:, cols]) + dt_bias[:, cols].astype(F32)
        size = jnp.maximum(pre, 0.0) + jnp.log1p(jnp.exp(-jnp.abs(pre)))
        step_s[:, cols] = size
        sigp[:, cols] = jax.nn.sigmoid(pre)
        drive[:, cols] = size * active[:, cols].astype(F32)

    each(E // 256, 256, step_size)
    decay[...] = -jnp.exp(a_log[...].astype(F32)) * LOG2E

    states[pl.ds(0, N), :] = jnp.zeros((N, E), BF16)

    def scan_sum(block):
        rows = rows_of(block, STEPS)
        held = states[pl.ds(pl.multiple_of(block * WIDE + N, N), WIDE), :]
        mixed[rows, :] = dot(cmat[rows, :], held)

    def forward_block(block, state):
        scan_sum(jnp.maximum(block - 1, 0))
        rows = rows_of(block, STEPS)
        size, push = step_s[rows, :], drive[rows, :]
        for i in range(STEPS):
            t = block * STEPS + i
            b_row = spread[rows_of(t, N), :]
            b_row = jnp.concatenate([b_row] * (E // 128), axis=1)
            factor = jnp.exp2(jnp.broadcast_to(size[i : i + 1], (N, E)) * decay[...])
            state = factor * state + b_row * jnp.broadcast_to(push[i : i + 1], (N, E))
            states[rows_of(t + 1, N), :] = state.astype(BF16)
        return state

    lax.fori_loop(0, NB, forward_block, jnp.zeros((N, E), F32))
    scan_sum(NB - 1)

    def mix(cols):
        value = mixed[:, cols] + d_skip[:, cols].astype(F32) * active[:, cols].astype(F32)
        mixed[:, cols] = value
        gated[:, cols] = (value * gact[:, cols]).astype(BF16)

    each(E // 128, 128, mix)

    def project_out(cols):
        branch = dot(gated[...], w_out[:, cols])
        at = lax.broadcasted_iota(jnp.int32, (T, 1), 0)
        live = (at < length_ref[0]).astype(F32)
        output[:, cols] = (tok[:, cols].astype(F32) + live * branch).astype(BF16)

    each(D // 256, 256, project_out)

    def back_out(index, c):
        cols = rows_of(index, 256)
        d_gated = dot(d_branch[...], w_out[cols, :], (1, 1))
        d_value = d_gated * gact[:, cols]
        d_mixed[:, cols] = d_value
        to = pl.ds(pl.multiple_of(E + index * 256, 256), 256)
        d_joined[:, to] = (d_gated * mixed[:, cols] * gslope[:, cols]).astype(BF16)
        g_rows[pl.ds(N + K + 2, 1), cols] = jnp.sum(
            d_value * active[:, cols].astype(F32), axis=0, keepdims=True
        )
        return c

    lax.fori_loop(0, E // 256, back_out, 0)

    spread_rows(cmat)
    carry[...] = jnp.zeros((N, E), F32)
    g_rows[pl.ds(0, N), :] = jnp.zeros((N, E), F32)
    half = N // 2
    at = lax.broadcasted_iota(jnp.int32, (STEPS, STEPS * half), 0)
    to = lax.broadcasted_iota(jnp.int32, (STEPS, STEPS * half), 1)
    gather = (at == to // half).astype(BF16)
    CH = 256

    def backward_block(k, c):
        block = NB - 1 - k
        rows = rows_of(block, STEPS)
        for chunk in range(E // CH):
            cols = pl.ds(chunk * CH, CH)
            later, total = carry[:, cols], g_rows[pl.ds(0, N), cols]
            size, d_value = step_s[rows, cols], d_mixed[rows, cols]
            rate = decay[:, cols]
            for i in reversed(range(STEPS)):
                t = block * STEPS + i
                dt = jnp.broadcast_to(size[i : i + 1], (N, CH))
                c_row = spread[rows_of(t, N), :]
                c_row = jnp.concatenate([c_row] * (CH // 128), axis=1)
                lam = c_row * jnp.broadcast_to(d_value[i : i + 1], (N, CH)) + later
                lam_s[pl.ds(i * N, N), cols] = lam.astype(BF16)
                later = jnp.exp2(dt * rate) * lam
                weighted = later * states[rows_of(t, N), cols].astype(F32)
                total = total + weighted * dt
                part = weighted * rate
                part = part[:half] + part[half:]
                if i % 2 == 1:
                    odd = part
                else:
                    part_s[pl.ds(i * half, N), cols] = jnp.concatenate([part, odd], axis=0).astype(BF16)
            carry[:, cols] = later
            g_rows[pl.ds(0, N), cols] = total
            held = lam_s[:, cols]
            lam_b[rows, cols] = dot(bmat[rows, :], held)
            d_decay[rows, cols] = dot(gather, part_s[:, cols])
            b_part = dot(drive[rows, cols].astype(BF16), held, (1, 1))
            after = states[pl.ds(pl.multiple_of(block * WIDE + N, N), WIDE), cols]
            c_part = dot(d_value.astype(BF16), after, (1, 1))
            if chunk == 0:
                db[rows, :] = b_part
                dc[rows, :] = c_part
            else:
                db[rows, :] += b_part
                dc[rows, :] += c_part
        return c

    lax.fori_loop(0, NB, backward_block, 0)
    g_rows[pl.ds(0, N), :] = g_rows[pl.ds(0, N), :] * decay[...] * (1.0 / LOG2E)

    def back_step(cols):
        wide = active[:, cols].astype(F32)
        adjoint = lam_b[:, cols]
        d_pre = (wide * adjoint + d_decay[:, cols] * (1.0 / LOG2E)) * sigp[:, cols]
        g_rows[pl.ds(N + K + 1, 1), cols] = jnp.sum(d_pre, axis=0, keepdims=True)
        d_pre_low[:, cols] = d_pre.astype(BF16)
        d_mixed[:, cols] = d_mixed[:, cols] * d_skip[:, cols].astype(F32) + step_s[:, cols] * adjoint

    each(E // 128, 128, back_step)

    row = lax.broadcasted_iota(jnp.int32, (WIDE, N), 0)
    col = lax.broadcasted_iota(jnp.int32, (WIDE, N), 1)
    pick = (row % N == col).astype(BF16)
    d_proj[:, pl.ds(0, R)] = dot(d_pre_low[...], w_dt[...], (1, 1)).astype(BF16)
    d_proj[:, pl.ds(R, N)] = dot((db[...] * diagonal).astype(BF16), pick).astype(BF16)
    d_proj[:, pl.ds(R + N, N)] = dot((dc[...] * diagonal).astype(BF16), pick).astype(BF16)

    d_conv[pl.ds(T, PAD), :] = jnp.zeros((PAD, E), F32)

    def back_conv(cols):
        g_dt[:, cols] = dot(proj[:, :R], d_pre_low[:, cols], (0, 0))
        g_xt[:, cols] = dot(d_proj[...], active[:, cols], (0, 0))
        d_active = d_mixed[:, cols] + dot(d_proj[...], w_x[cols, :], (1, 1))
        d_value = d_active * cslope[:, cols]
        d_conv[pl.ds(0, T), cols] = d_value
        g_rows[pl.ds(N + K, 1), cols] = jnp.sum(d_value, axis=0, keepdims=True)
        taps = conv_w[:, cols].astype(F32)
        total = jnp.zeros_like(d_value)
        for k in range(K):
            g_rows[pl.ds(N + k, 1), cols] = jnp.sum(
                d_value * inner[pl.ds(PAD - K + 1 + k, T), cols], axis=0, keepdims=True
            )
            total = total + taps[k : k + 1] * d_conv[pl.ds(K - 1 - k, T), cols]
        d_joined[:, cols] = total.astype(BF16)

    each(E // 128, 128, back_conv)
    g_rows[pl.ds(N + K + 3, 1), :] = jnp.zeros((1, E), F32)

    def back_in(index, c):
        rows = rows_of(index, 256)
        d_normed[:, rows] = dot(d_joined[...], w_in[rows, :], (1, 1))
        return c

    lax.fori_loop(0, D // 256, back_in, 0)

    g_gain[...] = jnp.zeros((1, D), F32)

    def back_norm(block, c):
        rows = rows_of(block, 64)
        x = tok[rows, :].astype(F32)
        scale = inv[rows, pl.ds(0, 1)]
        d_value = d_normed[rows, :]
        g_gain[...] += jnp.sum(d_value * x * scale, axis=0, keepdims=True)
        d_scaled = d_value * gain[...].astype(F32)
        shared = jnp.mean(d_scaled * x, axis=1, keepdims=True)
        input_grad[rows, :] = (
            cot[rows, :].astype(F32) + scale * d_scaled - x * (scale * scale * scale) * shared
        )
        return c

    lax.fori_loop(0, T // 64, back_norm, 0)


def compute(length, tokens, cotangent, gain, w_in, conv_w, conv_b, w_x, w_dt, dt_bias, a_log, d_skip, w_out):
    T, D = tokens.shape
    E, N, R, J, K = w_out.shape[0], a_log.shape[0], w_dt.shape[0], w_x.shape[1], conv_w.shape[0]
    wide = STEPS * N
    full = pltpu.VMEM((T, E), F32)
    low = pltpu.VMEM((T, E), BF16)
    out = lambda shape, dtype=F32: jax.ShapeDtypeStruct(shape, dtype)
    return pl.pallas_call(
        compute_kernel,
        out_shape=[
            out((T, D), BF16), out((T, D)), out((T, D), BF16), out((T, E), BF16), out((T, D), BF16),
            out((T, 2 * E), BF16), out((1, D)), out((N + K + 4, E)), out((R, E)), out((J, E)),
        ],
        in_specs=[SMEM] + [VMEM] * 12,
        out_specs=[VMEM] * 10,
        scratch_shapes=[
            pltpu.VMEM((T, 128), F32), pltpu.VMEM((T + 8, E), F32), full, full, full, low,
            pltpu.VMEM((T, J), BF16), pltpu.VMEM((T, wide), BF16), pltpu.VMEM((T, wide), BF16),
            pltpu.VMEM((T * N, 128), F32), pltpu.VMEM((N, E), F32),
            full, full, full, full, full, full, full, pltpu.VMEM(((T + 1) * N, E), BF16),
            pltpu.VMEM((N, E), F32), pltpu.VMEM((wide, E), BF16), pltpu.VMEM((wide // 2, E), BF16),
            pltpu.VMEM((T, wide), F32), pltpu.VMEM((T, wide), F32), low, pltpu.VMEM((T, J), BF16),
            pltpu.VMEM((T + 8, E), F32), pltpu.VMEM((T, D), F32),
        ],
        compiler_params=pltpu.CompilerParams(vmem_limit_bytes=62 * MB),
        name="layer",
    )(length, tokens, cotangent, gain, w_in, conv_w, conv_b, w_x, w_dt, dt_bias, a_log, d_skip, w_out)


def gather(weights):
    axes = (0, 0, 1, 0, 0, 1, 0, 1, 0, 0)
    return [lax.all_gather(w, "fsdp", axis=a, tiled=True) for w, a in zip(weights, axes)]


def reduce_plain(normed, gated, d_branch, d_joined, g_gain, g_rows, g_dt, g_xt):
    N, K = g_rows.shape[0] - 8, 4
    big_in = lax.dot_general(normed, d_joined, (((0,), (0,)), ((), ())), preferred_element_type=F32)
    big_out = lax.dot_general(gated, d_branch, (((0,), (0,)), ((), ())), preferred_element_type=F32)
    rows = jnp.concatenate([g_rows, g_dt, g_xt], axis=0)

    def scatter(value, axis):
        return lax.psum_scatter(value, "fsdp", scatter_dimension=axis, tiled=True)

    own = (
        scatter(big_in.astype(BF16), 0), scatter(big_out.astype(BF16), 0),
        scatter(rows, 1), scatter(g_gain[0], 0),
    )
    own_in, own_out, own_rows, own_gain = lax.psum(own, "dp")
    return own_in.astype(F32), own_out.astype(F32), own_rows, own_gain


def body(
    tokens, lengths, cotangent, gain, w_in, conv_w, conv_b, w_x, w_dt, dt_bias, a_log, d_skip, w_out
):
    weights = gather((gain, w_in, conv_w, conv_b, w_x, w_dt, dt_bias, a_log, d_skip, w_out))
    weights = [w.reshape(1, -1) if w.ndim == 1 else w for w in weights]
    output, input_grad, *parts = compute(lengths, tokens[0], cotangent[0], *weights)
    own_in, own_out, rows, own_gain = reduce_plain(*parts)
    N, K, R = a_log.shape[0], conv_w.shape[0], w_dt.shape[0]
    M = N + K + 4
    return (
        output[None], input_grad[None], own_gain, own_in, rows[N : N + K], rows[N + K],
        rows[M + R :].T, rows[M : M + R], rows[N + K + 1], rows[:N], rows[N + K + 2], own_out,
    )


def solution(mesh):
    seq, row, col, one = P(("dp", "fsdp"), None, None), P("fsdp", None), P(None, "fsdp"), P("fsdp")
    return jax.shard_map(
        body,
        mesh=mesh,
        in_specs=(seq, P(("dp", "fsdp")), seq, one, row, col, one, row, col, one, col, one, row),
        out_specs=(seq, seq, one, row, col, one, row, col, one, col, one, row),
        check_vma=False,
    )
```

```python
import functools
import types

import jax
import jax.numpy as jnp
from jax import lax
from jax.experimental import pallas as pl
from jax.experimental.pallas import tpu as pltpu
from jax.sharding import PartitionSpec as P

F32 = jnp.float32
BF16 = jnp.bfloat16
EPS = 1e-05
STEPS = 16
CHUNK = 256
PAD = 8
LOG2E = 1.4426950408889634
MB = 2**20
VMEM = pl.BlockSpec(memory_space=pltpu.VMEM)
SMEM = pl.BlockSpec(memory_space=pltpu.SMEM)
ANY = pl.BlockSpec(memory_space=pl.ANY)
MESH = pl.DeviceIdType.MESH


def dot(left, right, over=(1, 0)):
    dims = (((over[0],), (over[1],)), ((), ()))
    return lax.dot_general(left, right, dims, preferred_element_type=F32)


def span(index, size):
    return pl.ds(pl.multiple_of(index * size, size), size)


def repeat(count, step):
    def run(index, carry):
        step(index)
        return carry

    lax.fori_loop(0, count, run, 0)


def row_plan(s):
    bias = s.N + s.K
    return types.SimpleNamespace(conv=s.N, bias=bias, dt_bias=bias + 1, skip=bias + 2, gain=bias + 3)


def start_norm(s):
    def run(block):
        rows = span(block, 64)
        x = s.tok[rows, :].astype(F32)
        scale = lax.rsqrt(jnp.mean(x * x, axis=1, keepdims=True) + EPS)
        s.inv[rows, :] = jnp.broadcast_to(scale, (64, 128))
        at = block * 64 + lax.broadcasted_iota(jnp.int32, (64, 1), 0)
        live = (at < s.length[0]).astype(F32)
        s.d_branch[rows, :] = (live * s.cot[rows, :].astype(F32)).astype(BF16)

    repeat(s.T // 64, run)


def norm(s):
    def run(block):
        rows = span(block, 64)
        x = s.tok[rows, :].astype(F32)
        s.normed[rows, :] = (x * s.inv[rows, pl.ds(0, 1)] * s.gain[...]).astype(BF16)

    repeat(s.T // 64, run)


def project_inner(s, first, count):
    at = row_plan(s)

    def run(index):
        cols = span(first + index, 256)
        s.inner[pl.ds(PAD, s.T), cols] = dot(s.normed[...], s.w_in[:, cols])

    repeat(count, run)

    def convolve(index):
        cols = span(2 * first + index, 128)
        value = s.small[pl.ds(at.bias, 1), cols] + sum(
            s.small[pl.ds(at.conv + k, 1), cols] * s.inner[pl.ds(PAD - s.K + 1 + k, s.T), cols]
            for k in range(s.K)
        )
        sigma = jax.nn.sigmoid(value)
        s.active[:, cols] = (value * sigma).astype(BF16)
        s.cslope[:, cols] = sigma * (1.0 + value * (1.0 - sigma))

    repeat(2 * count, convolve)


def project_gate(s, first, count):
    def run(index):
        cols = span(first + index, 256)
        source = pl.ds(pl.multiple_of(s.E + (first + index) * 256, 256), 256)
        value = dot(s.normed[...], s.w_in[:, source])
        sigma = jax.nn.sigmoid(value)
        s.gact[:, cols] = value * sigma
        s.gslope[:, cols] = sigma * (1.0 + value * (1.0 - sigma))

    repeat(count, run)


def diagonal(s):
    wide = STEPS * s.N
    at = lax.broadcasted_iota(jnp.int32, (s.T, wide), 0)
    to = lax.broadcasted_iota(jnp.int32, (s.T, wide), 1)
    return (at % STEPS == to // s.N).astype(F32)


def spread_rows(s, source):
    ones = jnp.ones((STEPS, 128), BF16)
    wide = STEPS * s.N

    def run(block):
        s.spread[span(block, wide), :] = dot(source[span(block, STEPS), :], ones, (0, 0))

    repeat(s.T // STEPS, run)


def scan_inputs(s):
    wide = STEPS * s.N
    at = row_plan(s)
    s.proj[...] = dot(s.active[...], s.w_x[...]).astype(BF16)
    row = lax.broadcasted_iota(jnp.int32, (s.J, wide), 0)
    col = lax.broadcasted_iota(jnp.int32, (s.J, wide), 1)
    mask = diagonal(s)
    pick_b = (row == s.R + col % s.N).astype(BF16)
    pick_c = (row == s.R + s.N + col % s.N).astype(BF16)
    s.bmat[...] = (dot(s.proj[...], pick_b) * mask).astype(BF16)
    s.cmat[...] = (dot(s.proj[...], pick_c) * mask).astype(BF16)
    spread_rows(s, s.bmat)

    def run(index):
        cols = span(index, 256)
        pre = dot(s.proj[:, : s.R], s.w_dt[:, cols]) + s.small[pl.ds(at.dt_bias, 1), cols]
        size = jnp.maximum(pre, 0.0) + jnp.log1p(jnp.exp(-jnp.abs(pre)))
        s.step[:, cols] = size
        s.sigp[:, cols] = jax.nn.sigmoid(pre)
        s.drive[:, cols] = size * s.active[:, cols].astype(F32)

    repeat(s.E // 256, run)
    s.decay[...] = -jnp.exp(s.small[pl.ds(0, s.N), :]) * LOG2E


def forward_scan(s):
    N, E, wide = s.N, s.E, STEPS * s.N
    s.states[pl.ds(0, N), :] = jnp.zeros((N, E), BF16)

    def scan_sum(block):
        rows = span(block, STEPS)
        held = s.states[pl.ds(pl.multiple_of(block * wide + N, N), wide), :]
        s.mixed[rows, :] = dot(s.cmat[rows, :], held)

    def run(block, state):
        scan_sum(jnp.maximum(block - 1, 0))
        rows = span(block, STEPS)
        size, push = s.step[rows, :], s.drive[rows, :]
        for i in range(STEPS):
            t = block * STEPS + i
            b_row = s.spread[span(t, N), :]
            b_row = jnp.concatenate([b_row] * (E // 128), axis=1)
            factor = jnp.exp2(jnp.broadcast_to(size[i : i + 1], (N, E)) * s.decay[...])
            state = factor * state + b_row * jnp.broadcast_to(push[i : i + 1], (N, E))
            s.states[span(t + 1, N), :] = state.astype(BF16)
        return state

    lax.fori_loop(0, s.T // STEPS, run, jnp.zeros((N, E), F32))
    scan_sum(s.T // STEPS - 1)


def mix(s):
    at = row_plan(s)

    def run(index):
        cols = span(index, 128)
        value = s.mixed[pl.ds(0, s.T), cols] + s.small[pl.ds(at.skip, 1), cols] * s.active[:, cols].astype(F32)
        s.mixed[pl.ds(0, s.T), cols] = value
        s.gated[:, cols] = (value * s.gact[:, cols]).astype(BF16)

    repeat(s.E // 128, run)


def back_out(s):
    at = row_plan(s)

    def run(index):
        cols = span(index, 256)
        d_gated = dot(s.d_branch[...], s.w_out[cols, :], (1, 1))
        d_value = d_gated * s.gact[:, cols]
        s.d_mixed[:, cols] = d_value
        s.d_gate[:, cols] = (d_gated * s.mixed[pl.ds(0, s.T), cols] * s.gslope[:, cols]).astype(BF16)
        s.rows[pl.ds(at.skip, 1), cols] = jnp.sum(
            d_value * s.active[:, cols].astype(F32), axis=0, keepdims=True
        )

    repeat(s.E // 256, run)


def project_out(s):
    def run(index):
        cols = span(index, 256)
        branch = dot(s.gated[...], s.w_out[:, cols])
        at = lax.broadcasted_iota(jnp.int32, (s.T, 1), 0)
        live = (at < s.length[0]).astype(F32)
        s.output[:, cols] = (s.tok[:, cols].astype(F32) + live * branch).astype(BF16)

    repeat(s.D // 256, run)


def backward_scan(s, between=None):
    N, E, wide, half = s.N, s.E, STEPS * s.N, s.N // 2
    blocks = s.T // STEPS
    spread_rows(s, s.cmat)
    s.carry[...] = jnp.zeros((N, E), F32)
    s.rows[pl.ds(0, N), :] = jnp.zeros((N, E), F32)
    at = lax.broadcasted_iota(jnp.int32, (STEPS, STEPS * half), 0)
    to = lax.broadcasted_iota(jnp.int32, (STEPS, STEPS * half), 1)
    gather = (at == to // half).astype(BF16)

    def run(k):
        block = blocks - 1 - k
        rows = span(block, STEPS)
        for chunk in range(E // CHUNK):
            cols = pl.ds(chunk * CHUNK, CHUNK)
            later, total = s.carry[:, cols], s.rows[pl.ds(0, N), cols]
            size, d_value = s.step[rows, cols], s.d_mixed[rows, cols]
            rate = s.decay[:, cols]
            for i in reversed(range(STEPS)):
                t = block * STEPS + i
                dt = jnp.broadcast_to(size[i : i + 1], (N, CHUNK))
                c_row = s.spread[span(t, N), :]
                c_row = jnp.concatenate([c_row] * (CHUNK // 128), axis=1)
                lam = c_row * jnp.broadcast_to(d_value[i : i + 1], (N, CHUNK)) + later
                s.lam[pl.ds(i * N, N), cols] = lam.astype(BF16)
                later = jnp.exp2(dt * rate) * lam
                weighted = later * s.states[span(t, N), cols].astype(F32)
                total = total + weighted * dt
                part = weighted * rate
                part = part[:half] + part[half:]
                if i % 2 == 1:
                    odd = part
                else:
                    s.part[pl.ds(i * half, N), cols] = jnp.concatenate([part, odd], axis=0).astype(BF16)
            s.carry[:, cols] = later
            s.rows[pl.ds(0, N), cols] = total
            held = s.lam[:, cols]
            s.gact[rows, cols] = dot(s.bmat[rows, :], held)
            s.gslope[rows, cols] = dot(gather, s.part[:, cols])
            b_part = dot(s.drive[rows, cols].astype(BF16), held, (1, 1))
            after = s.states[pl.ds(pl.multiple_of(block * wide + N, N), wide), cols]
            c_part = dot(d_value.astype(BF16), after, (1, 1))
            if chunk == 0:
                s.db[rows, :] = b_part
                s.dc[rows, :] = c_part
            else:
                s.db[rows, :] += b_part
                s.dc[rows, :] += c_part
        if between is not None:
            between(k)

    repeat(blocks, run)
    s.rows[pl.ds(0, N), :] = s.rows[pl.ds(0, N), :] * s.decay[...] * (1.0 / LOG2E)


def back_step(s):
    at = row_plan(s)

    def run(index):
        cols = span(index, 128)
        wide = s.active[:, cols].astype(F32)
        adjoint = s.gact[:, cols]
        d_pre = (wide * adjoint + s.gslope[:, cols] * (1.0 / LOG2E)) * s.sigp[:, cols]
        s.rows[pl.ds(at.dt_bias, 1), cols] = jnp.sum(d_pre, axis=0, keepdims=True)
        s.d_pre_low[:, cols] = d_pre.astype(BF16)
        s.d_mixed[:, cols] = (
            s.d_mixed[:, cols] * s.small[pl.ds(at.skip, 1), cols] + s.step[:, cols] * adjoint
        )

    repeat(s.E // 128, run)


def back_proj(s):
    wide = STEPS * s.N
    row = lax.broadcasted_iota(jnp.int32, (wide, s.N), 0)
    col = lax.broadcasted_iota(jnp.int32, (wide, s.N), 1)
    pick = (row % s.N == col).astype(BF16)
    mask = diagonal(s)
    s.d_proj[:, pl.ds(0, s.R)] = dot(s.d_pre_low[...], s.w_dt[...], (1, 1)).astype(BF16)
    s.d_proj[:, pl.ds(s.R, s.N)] = dot((s.db[...] * mask).astype(BF16), pick).astype(BF16)
    s.d_proj[:, pl.ds(s.R + s.N, s.N)] = dot((s.dc[...] * mask).astype(BF16), pick).astype(BF16)


def back_conv(s):
    at = row_plan(s)
    s.mixed[pl.ds(s.T, PAD), :] = jnp.zeros((PAD, s.E), F32)
    first = at.gain + 1

    def run(index):
        cols = span(index, 128)
        s.rows[pl.ds(first, s.R), cols] = dot(s.proj[:, : s.R], s.d_pre_low[:, cols], (0, 0))
        s.rows[pl.ds(first + s.R, s.J), cols] = dot(s.d_proj[...], s.active[:, cols], (0, 0))
        d_active = s.d_mixed[:, cols] + dot(s.d_proj[...], s.w_x[cols, :], (1, 1))
        d_value = d_active * s.cslope[:, cols]
        s.mixed[pl.ds(0, s.T), cols] = d_value
        s.rows[pl.ds(at.bias, 1), cols] = jnp.sum(d_value, axis=0, keepdims=True)
        total = jnp.zeros_like(d_value)
        for k in range(s.K):
            s.rows[pl.ds(at.conv + k, 1), cols] = jnp.sum(
                d_value * s.inner[pl.ds(PAD - s.K + 1 + k, s.T), cols], axis=0, keepdims=True
            )
            taps = s.small[pl.ds(at.conv + k, 1), cols]
            total = total + taps * s.mixed[pl.ds(s.K - 1 - k, s.T), cols]
        s.d_inner[:, cols] = total.astype(BF16)

    repeat(s.E // 128, run)


def back_in(s):
    def run(index):
        rows = span(index, 256)
        s.d_normed[:, rows] = dot(s.d_inner[...], s.w_in[rows, pl.ds(0, s.E)], (1, 1)) + dot(
            s.d_gate[...], s.w_in[rows, pl.ds(s.E, s.E)], (1, 1)
        )

    repeat(s.D // 256, run)


def back_norm(s):
    s.d_gain[...] = jnp.zeros((1, s.D), F32)

    def run(block):
        rows = span(block, 64)
        x = s.tok[rows, :].astype(F32)
        scale = s.inv[rows, pl.ds(0, 1)]
        d_value = s.d_normed[rows, :]
        s.d_gain[...] += jnp.sum(d_value * x * scale, axis=0, keepdims=True)
        d_scaled = d_value * s.gain[...]
        shared = jnp.mean(d_scaled * x, axis=1, keepdims=True)
        s.input_grad[rows, :] = (
            s.cot[rows, :].astype(F32) + scale * d_scaled - x * (scale * scale * scale) * shared
        )

    repeat(s.T // 64, run)


def sizes(tokens, w_out, a_log, w_dt, w_x, conv_w):
    return dict(
        T=tokens.shape[0], D=tokens.shape[1], E=w_out.shape[0], N=a_log.shape[0],
        R=w_dt.shape[0], J=w_x.shape[1], K=conv_w.shape[0],
    )


def scratch_plan(z):
    T, D, E, N, R, J, K = (z[n] for n in "TDENRJK")
    wide = STEPS * N
    full, low = ((T, E), F32), ((T, E), BF16)
    padded = ((T + PAD, E), F32)
    count = N + K + 4
    return dict(
        inv=((T, 128), F32), gain=((1, D), F32), small=((count, E), F32), inner=padded, gact=full, gslope=full,
        cslope=full, active=low, proj=((T, J), BF16), bmat=((T, wide), BF16), cmat=((T, wide), BF16),
        spread=((T * N, 128), F32), decay=((N, E), F32), step=full, drive=full, sigp=full,
        mixed=padded, d_mixed=full, states=(((T + 1) * N, E), BF16), carry=((N, E), F32),
        lam=((wide, E), BF16), part=((wide // 2, E), BF16), db=((T, wide), F32), dc=((T, wide), F32),
        d_pre_low=low, d_proj=((T, J), BF16), d_normed=((T, D), F32), d_gain=((1, D), F32),
    )


def plain_kernel(z, names, *refs):
    s = types.SimpleNamespace(**z, **dict(zip(names, refs)))
    at = row_plan(s)
    s.small[pl.ds(0, s.N), :] = s.a_log[...].astype(F32)
    s.small[pl.ds(at.conv, s.K), :] = s.conv_w[...].astype(F32)
    s.small[pl.ds(at.bias, 1), :] = s.conv_b[...].astype(F32)
    s.small[pl.ds(at.dt_bias, 1), :] = s.dt_bias[...].astype(F32)
    s.small[pl.ds(at.skip, 1), :] = s.d_skip[...].astype(F32)
    s.gain[...] = s.gain_in[...].astype(F32)
    s.rows[...] = jnp.zeros(s.rows.shape, F32)
    s.inner[pl.ds(0, PAD), :] = jnp.zeros((PAD, s.E), F32)
    for step in (start_norm, norm):
        step(s)
    project_inner(s, 0, s.E // 256)
    project_gate(s, 0, s.E // 256)
    for step in (scan_inputs, forward_scan, mix, project_out, back_out):
        step(s)
    backward_scan(s)
    for step in (back_step, back_proj, back_conv, back_in, back_norm):
        step(s)
    s.g_gain[...] = s.d_gain[...]


def plain_layer(length, tokens, cotangent, gain, w_in, conv_w, conv_b, w_x, w_dt, dt_bias, a_log, d_skip, w_out):
    z = sizes(tokens, w_out, a_log, w_dt, w_x, conv_w)
    T, D, E, N, R, J, K = (z[n] for n in "TDENRJK")
    plan = scratch_plan(z)
    ins = ("length", "tok", "cot", "gain_in", "w_in", "conv_w", "conv_b", "w_x", "w_dt", "dt_bias", "a_log", "d_skip", "w_out")
    outs = dict(
        output=((T, D), BF16), input_grad=((T, D), F32), normed=((T, D), BF16), gated=((T, E), BF16),
        d_branch=((T, D), BF16), d_inner=((T, E), BF16), d_gate=((T, E), BF16), g_gain=((1, D), F32),
        rows=((N + K + 4 + R + J, E), F32),
    )
    names = list(ins) + list(outs) + list(plan)
    return pl.pallas_call(
        functools.partial(plain_kernel, z, names),
        out_shape=[jax.ShapeDtypeStruct(*spec) for spec in outs.values()],
        in_specs=[SMEM] + [VMEM] * 12,
        out_specs=[VMEM] * len(outs),
        scratch_shapes=[pltpu.VMEM(*spec) for spec in plan.values()],
        compiler_params=pltpu.CompilerParams(vmem_limit_bytes=60 * MB),
        name="plain_layer",
    )(length, tokens, cotangent, gain, w_in, conv_w, conv_b, w_x, w_dt, dt_bias, a_log, d_skip, w_out)


def plain_body(tokens, lengths, cotangent, *shards):
    axes = (0, 0, 1, 0, 0, 1, 0, 1, 0, 0)
    weights = [lax.all_gather(w, "fsdp", axis=a, tiled=True) for w, a in zip(shards, axes)]
    weights = [w.reshape(1, -1) if w.ndim == 1 else w for w in weights]
    output, input_grad, normed, gated, d_branch, d_inner, d_gate, g_gain, rows = plain_layer(
        lengths, tokens[0], cotangent[0], *weights
    )
    big_in = dot(normed, jnp.concatenate([d_inner, d_gate], axis=1), (0, 0))
    big_out = dot(gated, d_branch, (0, 0))

    def scatter(value, axis):
        return lax.psum_scatter(value, "fsdp", scatter_dimension=axis, tiled=True)

    own = (
        scatter(big_in.astype(BF16), 0), scatter(big_out.astype(BF16), 0),
        scatter(rows, 1), scatter(g_gain[0], 0),
    )
    own_in, own_out, rows, own_gain = lax.psum(own, "dp")
    N, K, R = shards[7].shape[0], shards[2].shape[0], shards[5].shape[0]
    M = N + K + 4
    return (
        output[None], input_grad[None], own_gain, own_in.astype(F32), rows[N : N + K], rows[N + K],
        rows[M + R :].T, rows[M : M + R], rows[N + K + 1], rows[:N], rows[N + K + 2], own_out.astype(F32),
    )


ORDERS = ((0, 1, 2, 3), (1, 0, 2, 3), (2, 0, 1, 3))
LEVELS = 4
PIECES = 2**LEVELS
GATHERS = 10
SWAPS = 6


def packed_rows(s):
    return s.N + s.K + 4


class Sum:
    def __init__(self, s, sem, order, acc, recv, out, first, piece):
        self.s, self.sem, self.order, self.piece = s, sem, order, piece
        self.acc, self.recv, self.out = acc, recv, out
        self.first, self.first_recv = first * PIECES * piece, first * (PIECES - 1) * piece
        self.bit = [lax.rem(s.dp // 2**b, 2) for b in order]

    def partner(self, level):
        b = self.order[level]
        return (self.s.dp + (1 - 2 * self.bit[level]) * 2**b, self.s.me)

    def rows(self, level, mine):
        start = 0
        for above in range(level):
            start = start + self.bit[above] * (PIECES >> (above + 1))
        bit = self.bit[level] if mine else 1 - self.bit[level]
        start = start + bit * (PIECES >> (level + 1))
        count = (PIECES >> (level + 1)) * self.piece
        return pl.multiple_of(self.first + start * self.piece, 16), count

    def landing(self, level):
        start = self.first_recv + (PIECES - (PIECES >> level)) * self.piece
        return start, (PIECES >> (level + 1)) * self.piece

    def reduce_copy(self, level):
        return self.s.remote(
            self.acc.at[pl.ds(*self.rows(level, False)), :],
            self.recv.at[pl.ds(*self.landing(level)), :],
            self.sem + level, self.partner(level),
        )

    def spread_copy(self, level, mine=True):
        rows = pl.ds(*self.rows(level, mine))
        return self.s.remote(
            self.out.at[rows, :], self.out.at[rows, :], self.sem + LEVELS + level, self.partner(level)
        )

    def start(self):
        self.reduce_copy(0).start()

    def reduce(self, level):
        self.reduce_copy(level).wait_recv()
        start, count = self.rows(level, True)
        landed = self.landing(level)[0]
        last = level == LEVELS - 1
        target = self.out if last else self.acc

        def add(index):
            here = pl.ds(pl.multiple_of(start + index * self.piece, 16), self.piece)
            there = pl.ds(pl.multiple_of(landed + index * self.piece, 16), self.piece)
            target[here, :] = (self.acc[here, :].astype(F32) + self.recv[there, :].astype(F32)).astype(BF16)

        repeat(count // self.piece, add)
        if last:
            self.spread_copy(level).start()
        else:
            self.reduce_copy(level + 1).start()

    def spread(self, level):
        self.spread_copy(level, False).wait_recv()
        if level > 0:
            self.spread_copy(level - 1).start()

    def finish(self):
        for level in range(LEVELS):
            self.reduce_copy(level).wait_send()
            self.spread_copy(level).wait_send()


def fused_kernel(z, names, *refs):
    s = types.SimpleNamespace(**z, **dict(zip(names, refs)))
    D, E = s.D, s.E
    DH, EH = D // 2, E // 2
    at = row_plan(s)
    count = packed_rows(s)
    s.dp, s.me = lax.axis_index("dp"), lax.axis_index("fsdp")
    other = 1 - s.me
    peer = (s.dp, other)

    def remote(src, dst, sem, device):
        return pltpu.make_async_remote_copy(
            src_ref=src, dst_ref=dst, send_sem=s.send.at[sem], recv_sem=s.recv_sem.at[sem],
            device_id=device, device_id_type=MESH,
        )

    s.remote = remote
    units = []
    for unit in range(3):
        for color in range(3):
            index = 3 * unit + color
            units.append(
                Sum(s, GATHERS + SWAPS + 2 * LEVELS * index, ORDERS[color], s.acc, s.recv, s.out, index, 16)
            )
    units.append(Sum(s, GATHERS + SWAPS + 2 * LEVELS * 9, ORDERS[0], s.acc_rows, s.recv_rows, s.out_rows, 0, 32))

    barrier = pltpu.get_barrier_semaphore()
    pl.semaphore_signal(barrier, inc=1, device_id=peer, device_id_type=MESH)
    for level in range(LEVELS):
        pl.semaphore_signal(barrier, inc=1, device_id=units[0].partner(level), device_id_type=MESH)

    mine_d, mine_e = span(s.me, DH), span(s.me, EH)
    theirs_d, theirs_e = span(other, DH), span(other, EH)
    local_in = pltpu.make_async_copy(s.w_in_own, s.w_in.at[mine_d, :], s.local.at[0])
    local_out = pltpu.make_async_copy(s.w_out_own, s.w_out.at[mine_e, :], s.local.at[1])
    local_in.start()
    local_out.start()
    s.pack[pl.ds(0, s.N), :] = s.a_log[...].astype(F32)
    s.pack[pl.ds(at.conv, s.K), :] = s.conv_w[...].astype(F32)
    s.pack[pl.ds(at.bias, 1), :] = s.conv_b[...].astype(F32)
    s.pack[pl.ds(at.dt_bias, 1), :] = s.dt_bias[...].astype(F32)
    s.pack[pl.ds(at.skip, 1), :] = s.d_skip[...].astype(F32)
    s.pack[pl.ds(at.gain, 1), :] = jnp.zeros((1, EH), F32)
    s.pack[pl.ds(at.gain, 1), pl.ds(0, DH)] = s.gain_own[...].astype(F32)
    pl.semaphore_wait(barrier, LEVELS + 1)

    width = 2 * E // 6
    gathers = [remote(s.pack, s.pack_in, 0, peer)]
    for j in range(6):
        cols = pl.ds(j * width, width)
        gathers.append(remote(s.w_in_own.at[:, cols], s.w_in.at[mine_d, cols], 1 + j, peer))
    gathers.append(remote(s.w_x_own, s.w_x.at[mine_e, :], 7, peer))
    gathers.append(remote(s.w_dt_own, s.w_dt_in, 8, peer))
    gathers.append(remote(s.w_out_own, s.w_out.at[mine_e, :], 9, peer))
    for copy in gathers:
        copy.start()

    swaps = [
        remote(s.normed.at[:, theirs_d], s.normed_in, GATHERS, peer),
        remote(s.d_branch, s.d_branch_in, GATHERS + 1, peer),
        remote(s.gated.at[:, theirs_e], s.gated_in, GATHERS + 2, peer),
        remote(s.d_gate, s.d_gate_in, GATHERS + 3, peer),
        remote(s.d_inner, s.d_inner_in, GATHERS + 4, peer),
        remote(s.rows.at[:, theirs_e], s.rows_in, GATHERS + 5, peer),
    ]

    start_norm(s)
    swaps[1].start()
    s.w_x[mine_e, :] = s.w_x_own[...]
    s.w_dt[:, mine_e] = s.w_dt_own[...]
    s.small[:, mine_e] = s.pack[...]
    s.gain[:, mine_d] = s.pack[pl.ds(at.gain, 1), pl.ds(0, DH)]
    s.inner[pl.ds(0, PAD), :] = jnp.zeros((PAD, E), F32)
    gathers[0].wait_recv()
    s.small[:, theirs_e] = s.pack_in[...]
    s.gain[:, theirs_d] = s.pack_in[pl.ds(at.gain, 1), pl.ds(0, DH)]
    norm(s)
    swaps[0].start()
    local_in.wait()
    for j in range(3):
        gathers[1 + j].wait_recv()
        project_inner(s, 2 * j, 2)
    gathers[7].wait_recv()
    gathers[8].wait_recv()
    s.w_dt[:, theirs_e] = s.w_dt_in[...]
    scan_inputs(s)
    for j in range(3):
        gathers[4 + j].wait_recv()
        project_gate(s, 2 * j, 2)
    forward_scan(s)
    mix(s)
    swaps[2].start()
    local_out.wait()
    gathers[9].wait_recv()
    back_out(s)
    swaps[3].start()
    project_out(s)

    def product(left, left_in, right, right_in, shift, cols, across):
        own = pl.ds(pl.multiple_of(shift + cols.start, 128), cols.size)
        total = dot(left[:, own], right[:, across], (0, 0)) + dot(left_in[:, cols], right_in[:, across], (0, 0))
        return total.astype(BF16)

    def grad_out(color):
        cols = pl.ds(256 * color, 256)
        s.acc[pl.ds(256 * color, 256), :] = product(
            s.gated, s.gated_in, s.d_branch, s.d_branch_in, s.me * EH, cols, pl.ds(0, D)
        )

    def grad_in(unit, color, right, right_in):
        first = 256 * (3 * unit + color)
        parts = (((0, 256, 0),), ((256, 128, 0), (0, 128, EH)), ((128, 256, EH),))[color]
        for start, size, across in parts:
            s.acc[pl.ds(first, size), :] = product(
                s.normed, s.normed_in, right, right_in, s.me * DH, pl.ds(start, size), pl.ds(across, EH)
            )
            first += size

    swaps[1].wait_recv()
    swaps[2].wait_recv()
    for color in range(3):
        grad_out(color)
        units[color].start()
    swaps[0].wait_recv()
    swaps[3].wait_recv()
    for color in range(3):
        grad_in(1, color, s.d_gate, s.d_gate_in)
        units[3 + color].start()

    def event(unit, step):
        members = units[9:] if unit == 3 else units[3 * unit : 3 * unit + 3]
        for member in members:
            if step < LEVELS:
                member.reduce(step)
            else:
                member.spread(2 * LEVELS - 1 - step)

    schedule = {6: (0, 0), 10: (1, 0), 12: (0, 1), 14: (1, 1), 15: (0, 2)}

    def between(k):
        for when, what in schedule.items():
            pl.when(k == when)(functools.partial(event, *what))

    s.rows[pl.ds(at.gain, 1), :] = jnp.zeros((1, E), F32)
    backward_scan(s, between)
    event(1, 2)
    back_step(s)
    event(0, 3)
    back_proj(s)
    event(1, 3)
    back_conv(s)
    swaps[4].start()
    event(0, 4)
    event(1, 4)
    back_in(s)
    event(0, 5)
    event(1, 5)
    back_norm(s)
    s.rows[pl.ds(at.gain, 1), pl.ds(0, DH)] = s.d_gain[:, pl.ds(0, DH)]
    s.rows[pl.ds(at.gain, 1), pl.ds(EH, DH)] = s.d_gain[:, pl.ds(DH, DH)]
    swaps[5].start()
    swaps[4].wait_recv()
    for color in range(3):
        grad_in(2, color, s.d_inner, s.d_inner_in)
        units[6 + color].start()
    swaps[5].wait_recv()
    total = s.rows.shape[0]
    s.acc_rows[...] = jnp.zeros(s.acc_rows.shape, BF16)
    for part in range(3):
        own = pl.ds(pl.multiple_of(s.me * EH + 256 * part, 128), 256)
        value = s.rows[:, own] + s.rows_in[:, pl.ds(256 * part, 256)]
        value = jnp.concatenate([value, jnp.zeros((160 - total, 256), F32)], axis=0)
        s.acc_rows[pl.ds(160 * part, 160), :] = value.astype(BF16)
    units[9].start()
    event(0, 6)
    event(1, 6)
    event(2, 0)
    event(3, 0)
    event(0, 7)
    event(1, 7)
    for step in range(1, 2 * LEVELS):
        event(2, step)
        event(3, step)
    for copy in gathers + swaps:
        copy.wait_send()
    for unit in units:
        unit.finish()


def fused_layer(length, tokens, cotangent, gain, w_in, conv_w, conv_b, w_x, w_dt, dt_bias, a_log, d_skip, w_out):
    z = sizes(tokens, jax.ShapeDtypeStruct((2 * w_out.shape[0], w_out.shape[1]), BF16), a_log, w_dt, w_x, conv_w)
    T, D, E, N, R, J, K = (z[n] for n in "TDENRJK")
    DH, EH = D // 2, E // 2
    total = N + K + 4 + R + J
    names = ("length", "tok", "cot", "gain_own", "w_in_own", "conv_w", "conv_b", "w_x_own", "w_dt_own", "dt_bias", "a_log", "d_skip", "w_out_own")
    outs = dict(
        output=((T, D), BF16), input_grad=((T, D), F32), out=((9 * 256, D), BF16), out_rows=((512, 256), BF16)
    )
    plan = scratch_plan(z)
    plan.update(
        w_in=((D, 2 * E), BF16), w_out=((E, D), BF16), w_x=((E, J), BF16), w_dt=((R, E), BF16),
        pack=((N + K + 4, EH), F32), pack_in=((N + K + 4, EH), F32), w_dt_in=((R, EH), BF16),
        normed=((T, D), BF16), gated=((T, E), BF16), d_branch=((T, D), BF16), d_inner=((T, E), BF16),
        d_gate=((T, E), BF16), rows=((total, E), F32), normed_in=((T, DH), BF16), d_branch_in=((T, D), BF16),
        gated_in=((T, EH), BF16), d_gate_in=((T, E), BF16), d_inner_in=((T, E), BF16), rows_in=((total, EH), F32),
        acc=((9 * 256, D), BF16), recv=((9 * 240, D), BF16), acc_rows=((512, 256), BF16), recv_rows=((480, 256), BF16),
    )
    sems = GATHERS + SWAPS + 2 * LEVELS * 10
    names = list(names) + list(outs) + list(plan) + ["local", "send", "recv_sem"]
    specs = [SMEM] + [VMEM] * 12
    specs[4] = specs[12] = ANY
    return pl.pallas_call(
        functools.partial(fused_kernel, z, names),
        out_shape=[jax.ShapeDtypeStruct(*spec) for spec in outs.values()],
        in_specs=specs,
        out_specs=[VMEM] * len(outs),
        scratch_shapes=[pltpu.VMEM(*spec) for spec in plan.values()]
        + [pltpu.SemaphoreType.DMA((2,)), pltpu.SemaphoreType.DMA((sems,)), pltpu.SemaphoreType.DMA((sems,))],
        compiler_params=pltpu.CompilerParams(collective_id=0, has_side_effects=True, vmem_limit_bytes=63 * MB),
        name="layer",
    )(length, tokens, cotangent, gain, w_in, conv_w, conv_b, w_x, w_dt, dt_bias, a_log, d_skip, w_out)


def finish_kernel(N, K, R, J, out, out_rows, output_in, grad_in_in, output, input_grad, *grads):
    g_gain, g_in, g_conv_w, g_conv_b, g_x, g_dt, g_dt_bias, g_a_log, g_skip, g_out = grads
    output[...] = output_in[...]
    input_grad[...] = grad_in_in[...]
    DH, D = g_in.shape[0], out.shape[1]
    g_out[...] = out[pl.ds(0, D), :].astype(F32)
    for place, unit in enumerate((2, 1)):
        for half in range(2):
            g_in[:, pl.ds((2 * place + half) * D, D)] = out[pl.ds(unit * D + half * DH, DH), :].astype(F32)
    M = N + K + 4
    for part in range(3):
        value = out_rows[pl.ds(160 * part, 160), :].astype(F32)
        cols = pl.ds(256 * part, 256)
        g_a_log[:, cols] = value[:N]
        g_conv_w[:, cols] = value[N : N + K]
        g_conv_b[:, cols] = value[N + K : N + K + 1]
        g_dt_bias[:, cols] = value[N + K + 1 : N + K + 2]
        g_skip[:, cols] = value[N + K + 2 : N + K + 3]
        row = value[N + K + 3 : N + K + 4]
        if part == 0:
            g_gain[:, pl.ds(0, 256)] = row
        elif part == 1:
            g_gain[:, pl.ds(256, DH - 256)] = row[:, : DH - 256]
        g_dt[:, cols] = value[M : M + R]
        turned = jnp.concatenate([value[M + R : M + R + J], jnp.zeros((128 - J, 256), F32)], axis=0).T
        g_x[cols, :] = turned[:, :J]


def fused_body(tokens, lengths, cotangent, *shards):
    shards = [w.reshape(1, -1) if w.ndim == 1 else w for w in shards]
    output, input_grad, out, out_rows = fused_layer(lengths, tokens[0], cotangent[0], *shards)
    gain, w_in, conv_w, conv_b, w_x, w_dt, dt_bias, a_log, d_skip, w_out = shards
    results = pl.pallas_call(
        functools.partial(finish_kernel, a_log.shape[0], conv_w.shape[0], w_dt.shape[0], w_x.shape[1]),
        out_shape=[jax.ShapeDtypeStruct(x.shape, x.dtype) for x in (output, input_grad)]
        + [jax.ShapeDtypeStruct(w.shape, F32) for w in shards],
        in_specs=[VMEM] * 4,
        out_specs=[VMEM] * 12,
        compiler_params=pltpu.CompilerParams(vmem_limit_bytes=60 * MB),
        name="finish",
    )(out, out_rows, output, input_grad)
    output, input_grad, *grads = results
    vectors = (0, 3, 6, 8)
    grads = [g.reshape(-1) if i in vectors else g for i, g in enumerate(grads)]
    return (output[None], input_grad[None], *grads)


def solution(mesh):
    seq, row, col, one = P(("dp", "fsdp"), None, None), P("fsdp", None), P(None, "fsdp"), P("fsdp")
    fused = mesh.shape["dp"] == PIECES and mesh.shape["fsdp"] == 2
    return jax.shard_map(
        fused_body if fused else plain_body,
        mesh=mesh,
        in_specs=(seq, P(("dp", "fsdp")), seq, one, row, col, one, row, col, one, col, one, row),
        out_specs=(seq, seq, one, row, col, one, row, col, one, col, one, row),
        check_vma=False,
    )
```

```python
import functools
import types

import jax
import jax.numpy as jnp
from jax import lax
from jax.experimental import pallas as pl
from jax.experimental.pallas import tpu as pltpu
from jax.sharding import PartitionSpec as P

F32 = jnp.float32
BF16 = jnp.bfloat16
EPS = 1e-05
STEPS = 16
CHUNK = 256
PAD = 8
LOG2E = 1.4426950408889634
MB = 2**20
VMEM = pl.BlockSpec(memory_space=pltpu.VMEM)
SMEM = pl.BlockSpec(memory_space=pltpu.SMEM)
ANY = pl.BlockSpec(memory_space=pl.ANY)
MESH = pl.DeviceIdType.MESH


def dot(left, right, over=(1, 0)):
    dims = (((over[0],), (over[1],)), ((), ()))
    return lax.dot_general(left, right, dims, preferred_element_type=F32)


def span(index, size):
    return pl.ds(pl.multiple_of(index * size, size), size)


def repeat(count, step):
    def run(index, carry):
        step(index)
        return carry

    lax.fori_loop(0, count, run, 0)


def row_plan(s):
    bias = s.N + s.K
    return types.SimpleNamespace(conv=s.N, bias=bias, dt_bias=bias + 1, skip=bias + 2, gain=bias + 3)


def start_norm(s):
    def run(block):
        rows = span(block, 64)
        x = s.tok[rows, :].astype(F32)
        scale = lax.rsqrt(jnp.mean(x * x, axis=1, keepdims=True) + EPS)
        s.inv[rows, :] = jnp.broadcast_to(scale, (64, 128))
        at = block * 64 + lax.broadcasted_iota(jnp.int32, (64, 1), 0)
        live = (at < s.length[0]).astype(F32)
        s.d_branch[rows, :] = (live * s.cot[rows, :].astype(F32)).astype(BF16)

    repeat(s.T // 64, run)


def norm(s):
    def run(block):
        rows = span(block, 64)
        x = s.tok[rows, :].astype(F32)
        s.normed[rows, :] = (x * s.inv[rows, pl.ds(0, 1)] * s.gain[...]).astype(BF16)

    repeat(s.T // 64, run)


def project_inner(s, first, count):
    at = row_plan(s)

    def run(index):
        cols = span(first + index, 256)
        s.inner[pl.ds(PAD, s.T), cols] = dot(s.normed[...], s.w_in[:, cols])

    repeat(count, run)

    def convolve(index):
        cols = span(2 * first + index, 128)
        value = s.small[pl.ds(at.bias, 1), cols] + sum(
            s.small[pl.ds(at.conv + k, 1), cols] * s.inner[pl.ds(PAD - s.K + 1 + k, s.T), cols]
            for k in range(s.K)
        )
        sigma = jax.nn.sigmoid(value)
        s.active[:, cols] = (value * sigma).astype(BF16)
        s.cslope[:, cols] = sigma * (1.0 + value * (1.0 - sigma))

    repeat(2 * count, convolve)


def project_gate(s, first, count):
    def run(index):
        cols = span(first + index, 256)
        source = pl.ds(pl.multiple_of(s.E + (first + index) * 256, 256), 256)
        value = dot(s.normed[...], s.w_in[:, source])
        sigma = jax.nn.sigmoid(value)
        s.gact[:, cols] = value * sigma
        s.gslope[:, cols] = sigma * (1.0 + value * (1.0 - sigma))

    repeat(count, run)


def diagonal(s):
    wide = STEPS * s.N
    at = lax.broadcasted_iota(jnp.int32, (s.T, wide), 0)
    to = lax.broadcasted_iota(jnp.int32, (s.T, wide), 1)
    return (at % STEPS == to // s.N).astype(F32)


def spread_rows(s):
    N, J, wide = s.N, s.J, STEPS * s.N
    state = lax.broadcasted_iota(jnp.int32, (N, J), 0)
    col = lax.broadcasted_iota(jnp.int32, (N, J), 1)
    mask = jnp.logical_or(col == s.R + state, col == s.R + N + state).astype(F32)
    row = lax.broadcasted_iota(jnp.int32, (J, 256), 0)
    lane = lax.broadcasted_iota(jnp.int32, (J, 256), 1)
    first = jnp.logical_and(row < s.R + N, lane < 128)
    last = jnp.logical_and(row >= s.R + N, lane >= 128)
    ones = jnp.logical_or(first, last).astype(BF16)

    def run(block):
        rows = s.proj[span(block, STEPS), :].astype(F32)
        parts = [(jnp.broadcast_to(rows[i : i + 1], (N, J)) * mask).astype(BF16) for i in range(STEPS)]
        s.spread[span(block, wide), :] = dot(jnp.concatenate(parts, axis=0), ones)

    repeat(s.T // STEPS, run)


def scan_inputs(s):
    wide = STEPS * s.N
    at = row_plan(s)
    s.proj[...] = dot(s.active[...], s.w_xt[...], (1, 1)).astype(BF16)
    row = lax.broadcasted_iota(jnp.int32, (s.J, wide), 0)
    col = lax.broadcasted_iota(jnp.int32, (s.J, wide), 1)
    mask = diagonal(s)
    pick_b = (row == s.R + col % s.N).astype(BF16)
    pick_c = (row == s.R + s.N + col % s.N).astype(BF16)
    s.bmat[...] = (dot(s.proj[...], pick_b) * mask).astype(BF16)
    s.cmat[...] = (dot(s.proj[...], pick_c) * mask).astype(BF16)
    spread_rows(s)

    def run(index):
        cols = span(index, 256)
        pre = dot(s.proj[:, : s.R], s.w_dt[:, cols]) + s.small[pl.ds(at.dt_bias, 1), cols]
        size = jnp.maximum(pre, 0.0) + jnp.log1p(jnp.exp(-jnp.abs(pre)))
        s.step[:, cols] = size
        s.sigp[:, cols] = jax.nn.sigmoid(pre)

    repeat(s.E // 256, run)
    s.decay[...] = -jnp.exp(s.small[pl.ds(0, s.N), :]) * LOG2E


def forward_scan(s):
    N, E, wide = s.N, s.E, STEPS * s.N
    s.states[pl.ds(0, N), :] = jnp.zeros((N, E), BF16)

    def scan_sum(block):
        rows = span(block, STEPS)
        held = s.states[pl.ds(pl.multiple_of(block * wide + N, N), wide), :]
        s.mixed[rows, :] = dot(s.cmat[rows, :], held)

    def run(block, state):
        scan_sum(jnp.maximum(block - 1, 0))
        rows = span(block, STEPS)
        size = s.step[rows, :]
        push = size * s.active[rows, :].astype(F32)
        for i in range(STEPS):
            t = block * STEPS + i
            b_row = s.spread[span(t, N), pl.ds(0, 128)]
            b_row = jnp.concatenate([b_row] * (E // 128), axis=1)
            factor = jnp.exp2(jnp.broadcast_to(size[i : i + 1], (N, E)) * s.decay[...])
            state = factor * state + b_row * jnp.broadcast_to(push[i : i + 1], (N, E))
            s.states[span(t + 1, N), :] = state.astype(BF16)
        return state

    lax.fori_loop(0, s.T // STEPS, run, jnp.zeros((N, E), F32))
    scan_sum(s.T // STEPS - 1)


def mix(s):
    at = row_plan(s)

    def run(index):
        cols = span(index, 128)
        value = s.mixed[pl.ds(0, s.T), cols] + s.small[pl.ds(at.skip, 1), cols] * s.active[:, cols].astype(F32)
        s.mixed[pl.ds(0, s.T), cols] = value
        s.gated[:, cols] = (value * s.gact[:, cols]).astype(BF16)

    repeat(s.E // 128, run)


def back_out(s):
    at = row_plan(s)

    def run(index):
        cols = span(index, 256)
        d_gated = dot(s.d_branch[...], s.w_out[cols, :], (1, 1))
        d_value = d_gated * s.gact[:, cols]
        s.d_mixed[:, cols] = d_value
        s.d_gate[:, cols] = (d_gated * s.mixed[pl.ds(0, s.T), cols] * s.gslope[:, cols]).astype(BF16)
        s.rows[pl.ds(at.skip, 1), cols] = jnp.sum(
            d_value * s.active[:, cols].astype(F32), axis=0, keepdims=True
        )

    repeat(s.E // 256, run)


def project_out(s):
    def run(index):
        cols = span(index, 256)
        branch = dot(s.gated[...], s.w_out[:, cols])
        at = lax.broadcasted_iota(jnp.int32, (s.T, 1), 0)
        live = (at < s.length[0]).astype(F32)
        s.output[:, cols] = (s.tok[:, cols].astype(F32) + live * branch).astype(BF16)

    repeat(s.D // 256, run)


def backward_scan(s, between=None):
    N, E, wide, half = s.N, s.E, STEPS * s.N, s.N // 2
    blocks = s.T // STEPS
    s.carry[...] = jnp.zeros((N, E), F32)
    s.rows[pl.ds(0, N), :] = jnp.zeros((N, E), F32)
    at = lax.broadcasted_iota(jnp.int32, (STEPS, STEPS * half), 0)
    to = lax.broadcasted_iota(jnp.int32, (STEPS, STEPS * half), 1)
    gather = (at == to // half).astype(BF16)

    def run(k):
        block = blocks - 1 - k
        rows = span(block, STEPS)
        for chunk in range(E // CHUNK):
            cols = pl.ds(chunk * CHUNK, CHUNK)
            later, total = s.carry[:, cols], s.rows[pl.ds(0, N), cols]
            size, d_value = s.step[rows, cols], s.d_mixed[rows, cols]
            rate = s.decay[:, cols]
            for i in reversed(range(STEPS)):
                t = block * STEPS + i
                dt = jnp.broadcast_to(size[i : i + 1], (N, CHUNK))
                c_row = s.spread[span(t, N), pl.ds(128, 128)]
                c_row = jnp.concatenate([c_row] * (CHUNK // 128), axis=1)
                lam = c_row * jnp.broadcast_to(d_value[i : i + 1], (N, CHUNK)) + later
                s.lam[pl.ds(i * N, N), cols] = lam.astype(BF16)
                later = jnp.exp2(dt * rate) * lam
                weighted = later * s.states[span(t, N), cols].astype(F32)
                total = total + weighted * dt
                part = weighted * rate
                part = part[:half] + part[half:]
                if i % 2 == 1:
                    odd = part
                else:
                    s.part[pl.ds(i * half, N), cols] = jnp.concatenate([part, odd], axis=0).astype(BF16)
            s.carry[:, cols] = later
            s.rows[pl.ds(0, N), cols] = total
            held = s.lam[:, cols]
            s.gact[rows, cols] = dot(s.bmat[rows, :], held)
            s.gslope[rows, cols] = dot(gather, s.part[:, cols])
            drive = (size * s.active[rows, cols].astype(F32)).astype(BF16)
            b_part = dot(drive, held, (1, 1))
            after = s.states[pl.ds(pl.multiple_of(block * wide + N, N), wide), cols]
            c_part = dot(d_value.astype(BF16), after, (1, 1))
            if chunk == 0:
                s.db[rows, :] = b_part
                s.dc[rows, :] = c_part
            else:
                s.db[rows, :] += b_part
                s.dc[rows, :] += c_part
        if between is not None:
            between(k)

    repeat(blocks, run)
    s.rows[pl.ds(0, N), :] = s.rows[pl.ds(0, N), :] * s.decay[...] * (1.0 / LOG2E)


def back_step(s):
    at = row_plan(s)

    def run(index):
        cols = span(index, 128)
        wide = s.active[:, cols].astype(F32)
        adjoint = s.gact[:, cols]
        d_pre = (wide * adjoint + s.gslope[:, cols] * (1.0 / LOG2E)) * s.sigp[:, cols]
        s.rows[pl.ds(at.dt_bias, 1), cols] = jnp.sum(d_pre, axis=0, keepdims=True)
        s.d_pre_low[:, cols] = d_pre.astype(BF16)
        s.d_mixed[:, cols] = (
            s.d_mixed[:, cols] * s.small[pl.ds(at.skip, 1), cols] + s.step[:, cols] * adjoint
        )

    repeat(s.E // 128, run)


def back_proj(s):
    wide = STEPS * s.N
    row = lax.broadcasted_iota(jnp.int32, (wide, s.N), 0)
    col = lax.broadcasted_iota(jnp.int32, (wide, s.N), 1)
    pick = (row % s.N == col).astype(BF16)
    mask = diagonal(s)
    s.d_proj[:, pl.ds(0, s.R)] = dot(s.d_pre_low[...], s.w_dt[...], (1, 1)).astype(BF16)
    s.d_proj[:, pl.ds(s.R, s.N)] = dot((s.db[...] * mask).astype(BF16), pick).astype(BF16)
    s.d_proj[:, pl.ds(s.R + s.N, s.N)] = dot((s.dc[...] * mask).astype(BF16), pick).astype(BF16)


def back_conv(s):
    at = row_plan(s)
    s.mixed[pl.ds(s.T, PAD), :] = jnp.zeros((PAD, s.E), F32)
    first = at.gain + 1

    def run(index):
        cols = span(index, 128)
        s.rows[pl.ds(first, s.R), cols] = dot(s.proj[:, : s.R], s.d_pre_low[:, cols], (0, 0))
        s.rows[pl.ds(first + s.R, s.J), cols] = dot(s.d_proj[...], s.active[:, cols], (0, 0))
        d_active = s.d_mixed[:, cols] + dot(s.d_proj[...], s.w_xt[:, cols])
        d_value = d_active * s.cslope[:, cols]
        s.mixed[pl.ds(0, s.T), cols] = d_value
        s.rows[pl.ds(at.bias, 1), cols] = jnp.sum(d_value, axis=0, keepdims=True)
        total = jnp.zeros_like(d_value)
        for k in range(s.K):
            s.rows[pl.ds(at.conv + k, 1), cols] = jnp.sum(
                d_value * s.inner[pl.ds(PAD - s.K + 1 + k, s.T), cols], axis=0, keepdims=True
            )
            taps = s.small[pl.ds(at.conv + k, 1), cols]
            total = total + taps * s.mixed[pl.ds(s.K - 1 - k, s.T), cols]
        s.d_inner[:, cols] = total.astype(BF16)

    repeat(s.E // 128, run)


def back_in(s):
    def run(index):
        rows = span(index, 256)
        s.d_normed[:, rows] = dot(s.d_inner[...], s.w_in[rows, pl.ds(0, s.E)], (1, 1)) + dot(
            s.d_gate[...], s.w_in[rows, pl.ds(s.E, s.E)], (1, 1)
        )

    repeat(s.D // 256, run)


def back_norm(s):
    s.d_gain[...] = jnp.zeros((1, s.D), F32)

    def run(block):
        rows = span(block, 64)
        x = s.tok[rows, :].astype(F32)
        scale = s.inv[rows, pl.ds(0, 1)]
        d_value = s.d_normed[rows, :]
        s.d_gain[...] += jnp.sum(d_value * x * scale, axis=0, keepdims=True)
        d_scaled = d_value * s.gain[...]
        shared = jnp.mean(d_scaled * x, axis=1, keepdims=True)
        s.input_grad[rows, :] = (
            s.cot[rows, :].astype(F32) + scale * d_scaled - x * (scale * scale * scale) * shared
        )

    repeat(s.T // 64, run)


def sizes(tokens, w_out, a_log, w_dt, w_xt, conv_w):
    return dict(
        T=tokens.shape[0], D=tokens.shape[1], E=w_out.shape[0], N=a_log.shape[0],
        R=w_dt.shape[0], J=w_xt.shape[0], K=conv_w.shape[0],
    )


def scratch_plan(z):
    T, D, E, N, R, J, K = (z[n] for n in "TDENRJK")
    wide = STEPS * N
    full, low = ((T, E), F32), ((T, E), BF16)
    padded = ((T + PAD, E), F32)
    count = N + K + 4
    return dict(
        inv=((T, 128), F32), gain=((1, D), F32), small=((count, E), F32), inner=padded, gact=full, gslope=full,
        cslope=full, active=low, proj=((T, J), BF16), bmat=((T, wide), BF16), cmat=((T, wide), BF16),
        spread=((T * N, 256), F32), decay=((N, E), F32), step=full, sigp=full,
        mixed=padded, d_mixed=full, states=(((T + 1) * N, E), BF16), carry=((N, E), F32),
        lam=((wide, E), BF16), part=((wide // 2, E), BF16), db=((T, wide), F32), dc=((T, wide), F32),
        d_pre_low=low, d_proj=((T, J), BF16), d_normed=((T, D), F32), d_gain=((1, D), F32),
    )


def plain_kernel(z, names, *refs):
    s = types.SimpleNamespace(**z, **dict(zip(names, refs)))
    at = row_plan(s)
    s.small[pl.ds(0, s.N), :] = s.a_log[...].astype(F32)
    s.small[pl.ds(at.conv, s.K), :] = s.conv_w[...].astype(F32)
    s.small[pl.ds(at.bias, 1), :] = s.conv_b[...].astype(F32)
    s.small[pl.ds(at.dt_bias, 1), :] = s.dt_bias[...].astype(F32)
    s.small[pl.ds(at.skip, 1), :] = s.d_skip[...].astype(F32)
    s.gain[...] = s.gain_in[...].astype(F32)
    s.rows[...] = jnp.zeros(s.rows.shape, F32)
    s.inner[pl.ds(0, PAD), :] = jnp.zeros((PAD, s.E), F32)
    for step in (start_norm, norm):
        step(s)
    project_inner(s, 0, s.E // 256)
    project_gate(s, 0, s.E // 256)
    for step in (scan_inputs, forward_scan, mix, project_out, back_out):
        step(s)
    backward_scan(s)
    for step in (back_step, back_proj, back_conv, back_in, back_norm):
        step(s)
    s.g_gain[...] = s.d_gain[...]


def plain_layer(length, tokens, cotangent, gain, w_in, conv_w, conv_b, w_xt, w_dt, dt_bias, a_log, d_skip, w_out):
    z = sizes(tokens, w_out, a_log, w_dt, w_xt, conv_w)
    T, D, E, N, R, J, K = (z[n] for n in "TDENRJK")
    plan = scratch_plan(z)
    ins = ("length", "tok", "cot", "gain_in", "w_in", "conv_w", "conv_b", "w_xt", "w_dt", "dt_bias", "a_log", "d_skip", "w_out")
    outs = dict(
        output=((T, D), BF16), input_grad=((T, D), F32), normed=((T, D), BF16), gated=((T, E), BF16),
        d_branch=((T, D), BF16), d_inner=((T, E), BF16), d_gate=((T, E), BF16), g_gain=((1, D), F32),
        rows=((N + K + 4 + R + J, E), F32),
    )
    names = list(ins) + list(outs) + list(plan)
    return pl.pallas_call(
        functools.partial(plain_kernel, z, names),
        out_shape=[jax.ShapeDtypeStruct(*spec) for spec in outs.values()],
        in_specs=[SMEM] + [VMEM] * 12,
        out_specs=[VMEM] * len(outs),
        scratch_shapes=[pltpu.VMEM(*spec) for spec in plan.values()],
        compiler_params=pltpu.CompilerParams(vmem_limit_bytes=60 * MB),
        name="plain_layer",
    )(length, tokens, cotangent, gain, w_in, conv_w, conv_b, w_xt, w_dt, dt_bias, a_log, d_skip, w_out)


def plain_body(tokens, lengths, cotangent, *shards):
    axes = (0, 0, 1, 0, 0, 1, 0, 1, 0, 0)
    weights = [lax.all_gather(w, "fsdp", axis=a, tiled=True) for w, a in zip(shards, axes)]
    weights = [w.reshape(1, -1) if w.ndim == 1 else w for w in weights]
    weights[4] = weights[4].T
    output, input_grad, normed, gated, d_branch, d_inner, d_gate, g_gain, rows = plain_layer(
        lengths, tokens[0], cotangent[0], *weights
    )
    big_in = dot(normed, jnp.concatenate([d_inner, d_gate], axis=1), (0, 0))
    big_out = dot(gated, d_branch, (0, 0))

    def scatter(value, axis):
        return lax.psum_scatter(value, "fsdp", scatter_dimension=axis, tiled=True)

    own = (
        scatter(big_in.astype(BF16), 0), scatter(big_out.astype(BF16), 0),
        scatter(rows, 1), scatter(g_gain[0], 0),
    )
    own_in, own_out, rows, own_gain = lax.psum(own, "dp")
    N, K, R = shards[7].shape[0], shards[2].shape[0], shards[5].shape[0]
    M = N + K + 4
    return (
        output[None], input_grad[None], own_gain, own_in.astype(F32), rows[N : N + K], rows[N + K],
        rows[M + R :].T, rows[M : M + R], rows[N + K + 1], rows[:N], rows[N + K + 2], own_out.astype(F32),
    )


ORDERS = (
    (0, 1, 2, 3), (1, 0, 3, 2), (3, 1, 0, 2), (0, 1, 2, 3), (1, 0, 3, 2),
    (2, 0, 1, 3), (1, 0, 3, 2), (2, 0, 1, 3), (0, 1, 2, 3), (1, 0, 2, 3),
)
DURING = {
    5: ((0, 0), (1, 0)), 10: ((3, 0), (4, 0), (2, 0), (5, 0)), 12: ((1, 1),), 13: ((0, 1),),
    15: ((4, 1), (3, 1)), 17: ((1, 2), (0, 2)), 18: ((5, 1), (2, 1), (3, 2), (4, 2)), 19: ((1, 3), (0, 3)),
}
AFTER = (
    (5, 2), (2, 2), (3, 3), (4, 3), (1, 4), (0, 4), (6, 0), (8, 0), (7, 0), (5, 3), (2, 3), (3, 4), (4, 4), (9, 0),
    (6, 1), (0, 5), (1, 5), (8, 1), (7, 1), (5, 4), (2, 4), (3, 5), (9, 1), (0, 6), (4, 5), (1, 6), (7, 2), (2, 5),
    (5, 5), (6, 2), (8, 2), (9, 2), (3, 6), (7, 3), (6, 3), (8, 3), (0, 7), (9, 3), (6, 4), (7, 4), (4, 6), (1, 7),
    (8, 4), (9, 4), (5, 6), (2, 6), (6, 5), (8, 5), (7, 5), (9, 5), (3, 7), (4, 7), (5, 7), (6, 6), (8, 6), (7, 6),
    (9, 6), (6, 7), (8, 7), (2, 7), (7, 7), (9, 7),
)
LEVELS = 4
PIECES = 2**LEVELS
GATHERS = 10
SWAPS = 6


def packed_rows(s):
    return s.N + s.K + 4


class Sum:
    def __init__(self, s, sem, order, acc, recv, out, first, piece):
        self.s, self.sem, self.order, self.piece = s, sem, order, piece
        self.acc, self.recv, self.out = acc, recv, out
        self.first, self.first_recv = first * PIECES * piece, first * (PIECES - 1) * piece
        self.bit = [lax.rem(s.dp // 2**b, 2) for b in order]

    def partner(self, level):
        b = self.order[level]
        return (self.s.dp + (1 - 2 * self.bit[level]) * 2**b, self.s.me)

    def rows(self, level, mine):
        start = 0
        for above in range(level):
            start = start + self.bit[above] * (PIECES >> (above + 1))
        bit = self.bit[level] if mine else 1 - self.bit[level]
        start = start + bit * (PIECES >> (level + 1))
        count = (PIECES >> (level + 1)) * self.piece
        return pl.multiple_of(self.first + start * self.piece, 16), count

    def landing(self, level):
        start = self.first_recv + (PIECES - (PIECES >> level)) * self.piece
        return start, (PIECES >> (level + 1)) * self.piece

    def reduce_copy(self, level):
        return self.s.remote(
            self.acc.at[pl.ds(*self.rows(level, False)), :],
            self.recv.at[pl.ds(*self.landing(level)), :],
            self.sem + level, self.partner(level),
        )

    def spread_copy(self, level, mine=True):
        rows = pl.ds(*self.rows(level, mine))
        return self.s.remote(
            self.out.at[rows, :], self.out.at[rows, :], self.sem + LEVELS + level, self.partner(level)
        )

    def start(self):
        self.reduce_copy(0).start()

    def reduce(self, level):
        self.reduce_copy(level).wait_recv()
        start, count = self.rows(level, True)
        landed = self.landing(level)[0]
        last = level == LEVELS - 1
        target = self.out if last else self.acc

        def add(index):
            here = pl.ds(pl.multiple_of(start + index * self.piece, 16), self.piece)
            there = pl.ds(pl.multiple_of(landed + index * self.piece, 16), self.piece)
            target[here, :] = (self.acc[here, :].astype(F32) + self.recv[there, :].astype(F32)).astype(BF16)

        repeat(count // self.piece, add)
        if last:
            self.spread_copy(level).start()
        else:
            self.reduce_copy(level + 1).start()

    def spread(self, level):
        self.spread_copy(level, False).wait_recv()
        if level > 0:
            self.spread_copy(level - 1).start()

    def finish(self):
        for level in range(LEVELS):
            self.reduce_copy(level).wait_send()
            self.spread_copy(level).wait_send()


def fused_kernel(z, names, *refs):
    s = types.SimpleNamespace(**z, **dict(zip(names, refs)))
    D, E = s.D, s.E
    DH, EH = D // 2, E // 2
    at = row_plan(s)
    count = packed_rows(s)
    s.dp, s.me = lax.axis_index("dp"), lax.axis_index("fsdp")
    other = 1 - s.me
    peer = (s.dp, other)

    def remote(src, dst, sem, device):
        return pltpu.make_async_remote_copy(
            src_ref=src, dst_ref=dst, send_sem=s.send.at[sem], recv_sem=s.recv_sem.at[sem],
            device_id=device, device_id_type=MESH,
        )

    s.remote = remote
    units = []
    for unit in range(3):
        for color in range(3):
            index = 3 * unit + color
            units.append(
                Sum(s, GATHERS + SWAPS + 2 * LEVELS * index, ORDERS[index], s.acc, s.recv, s.out, index, 16)
            )
    units.append(Sum(s, GATHERS + SWAPS + 2 * LEVELS * 9, ORDERS[9], s.acc_rows, s.recv_rows, s.out_rows, 0, 32))

    barrier = pltpu.get_barrier_semaphore()
    pl.semaphore_signal(barrier, inc=1, device_id=peer, device_id_type=MESH)
    for level in range(LEVELS):
        pl.semaphore_signal(barrier, inc=1, device_id=units[0].partner(level), device_id_type=MESH)

    mine_d, mine_e = span(s.me, DH), span(s.me, EH)
    theirs_d, theirs_e = span(other, DH), span(other, EH)
    local_in = pltpu.make_async_copy(s.w_in_own, s.w_in.at[mine_d, :], s.local.at[0])
    local_out = pltpu.make_async_copy(s.w_out_own, s.w_out.at[mine_e, :], s.local.at[1])
    local_in.start()
    local_out.start()
    s.pack[pl.ds(0, s.N), :] = s.a_log[...].astype(F32)
    s.pack[pl.ds(at.conv, s.K), :] = s.conv_w[...].astype(F32)
    s.pack[pl.ds(at.bias, 1), :] = s.conv_b[...].astype(F32)[None, :]
    s.pack[pl.ds(at.dt_bias, 1), :] = s.dt_bias[...].astype(F32)[None, :]
    s.pack[pl.ds(at.skip, 1), :] = s.d_skip[...].astype(F32)[None, :]
    s.pack[pl.ds(at.gain, 1), :] = jnp.zeros((1, EH), F32)
    s.pack[pl.ds(at.gain, 1), pl.ds(0, DH)] = s.gain_own[...].astype(F32)[None, :]
    pl.semaphore_wait(barrier, LEVELS + 1)

    width = 2 * E // 6
    gathers = [remote(s.pack, s.pack_in, 0, peer)]
    for j in range(6):
        cols = pl.ds(j * width, width)
        gathers.append(remote(s.w_in_own.at[:, cols], s.w_in.at[mine_d, cols], 1 + j, peer))
    gathers.append(remote(s.w_xt_own, s.w_xt_in, 7, peer))
    gathers.append(remote(s.w_dt_own, s.w_dt_in, 8, peer))
    gathers.append(remote(s.w_out_own, s.w_out.at[mine_e, :], 9, peer))
    for copy in gathers:
        copy.start()

    swaps = [
        remote(s.normed.at[:, theirs_d], s.normed_in, GATHERS, peer),
        remote(s.d_branch, s.d_branch_in, GATHERS + 1, peer),
        remote(s.gated.at[:, theirs_e], s.gated_in, GATHERS + 2, peer),
        remote(s.d_gate, s.d_gate_in, GATHERS + 3, peer),
        remote(s.d_inner, s.d_inner_in, GATHERS + 4, peer),
        remote(s.rows.at[:, theirs_e], s.rows_in, GATHERS + 5, peer),
    ]

    start_norm(s)
    swaps[1].start()
    s.w_xt[:, mine_e] = s.w_xt_own[...]
    s.w_dt[:, mine_e] = s.w_dt_own[...]
    s.small[:, mine_e] = s.pack[...]
    s.gain[:, mine_d] = s.pack[pl.ds(at.gain, 1), pl.ds(0, DH)]
    s.inner[pl.ds(0, PAD), :] = jnp.zeros((PAD, E), F32)
    gathers[0].wait_recv()
    s.small[:, theirs_e] = s.pack_in[...]
    s.gain[:, theirs_d] = s.pack_in[pl.ds(at.gain, 1), pl.ds(0, DH)]
    norm(s)
    swaps[0].start()
    local_in.wait()
    for j in range(3):
        gathers[1 + j].wait_recv()
        project_inner(s, 2 * j, 2)
    gathers[7].wait_recv()
    gathers[8].wait_recv()
    s.w_dt[:, theirs_e] = s.w_dt_in[...]
    s.w_xt[:, theirs_e] = s.w_xt_in[...]
    scan_inputs(s)
    for j in range(3):
        gathers[4 + j].wait_recv()
        project_gate(s, 2 * j, 2)
    forward_scan(s)
    mix(s)
    swaps[2].start()
    local_out.wait()
    gathers[9].wait_recv()
    back_out(s)
    swaps[3].start()
    project_out(s)

    def product(left, left_in, right, right_in, shift, cols, across):
        own = pl.ds(pl.multiple_of(shift + cols.start, 128), cols.size)
        total = dot(left[:, own], right[:, across], (0, 0)) + dot(left_in[:, cols], right_in[:, across], (0, 0))
        return total.astype(BF16)

    def grad_out(color):
        cols = pl.ds(256 * color, 256)
        s.acc[pl.ds(256 * color, 256), :] = product(
            s.gated, s.gated_in, s.d_branch, s.d_branch_in, s.me * EH, cols, pl.ds(0, D)
        )

    def grad_in(unit, color, right, right_in):
        first = 256 * (3 * unit + color)
        parts = (((0, 256, 0),), ((256, 128, 0), (0, 128, EH)), ((128, 256, EH),))[color]
        for start, size, across in parts:
            s.acc[pl.ds(first, size), :] = product(
                s.normed, s.normed_in, right, right_in, s.me * DH, pl.ds(start, size), pl.ds(across, EH)
            )
            first += size

    swaps[1].wait_recv()
    swaps[2].wait_recv()
    for color in range(3):
        grad_out(color)
        units[color].start()
    swaps[0].wait_recv()
    swaps[3].wait_recv()
    for color in range(3):
        grad_in(1, color, s.d_gate, s.d_gate_in)
        units[3 + color].start()

    def carry_on(events):
        for index, step in events:
            if step < LEVELS:
                units[index].reduce(step)
            else:
                units[index].spread(2 * LEVELS - 1 - step)

    def between(k):
        for when, events in DURING.items():
            if when < s.T // STEPS:
                pl.when(k == when)(functools.partial(carry_on, events))

    def phase(number, step):
        step(s)
        carry_on(DURING.get(number, ()))

    s.rows[pl.ds(at.gain, 1), :] = jnp.zeros((1, E), F32)
    backward_scan(s, between)
    phase(16, back_step)
    phase(17, back_proj)
    back_conv(s)
    swaps[4].start()
    carry_on(DURING.get(18, ()))
    phase(19, back_in)
    phase(20, back_norm)
    s.rows[pl.ds(at.gain, 1), pl.ds(0, DH)] = s.d_gain[:, pl.ds(0, DH)]
    s.rows[pl.ds(at.gain, 1), pl.ds(EH, DH)] = s.d_gain[:, pl.ds(DH, DH)]
    swaps[5].start()
    swaps[4].wait_recv()
    for color in range(3):
        grad_in(2, color, s.d_inner, s.d_inner_in)
        units[6 + color].start()
    swaps[5].wait_recv()
    total = s.rows.shape[0]
    s.acc_rows[...] = jnp.zeros(s.acc_rows.shape, BF16)
    for part in range(3):
        own = pl.ds(pl.multiple_of(s.me * EH + 256 * part, 128), 256)
        value = s.rows[:, own] + s.rows_in[:, pl.ds(256 * part, 256)]
        value = jnp.concatenate([value, jnp.zeros((160 - total, 256), F32)], axis=0)
        s.acc_rows[pl.ds(160 * part, 160), :] = value.astype(BF16)
    units[9].start()
    carry_on(AFTER)
    for copy in gathers + swaps:
        copy.wait_send()
    for unit in units:
        unit.finish()


def fused_layer(length, tokens, cotangent, gain, w_in, conv_w, conv_b, w_xt, w_dt, dt_bias, a_log, d_skip, w_out):
    z = sizes(tokens, jax.ShapeDtypeStruct((2 * w_out.shape[0], w_out.shape[1]), BF16), a_log, w_dt, w_xt, conv_w)
    T, D, E, N, R, J, K = (z[n] for n in "TDENRJK")
    DH, EH = D // 2, E // 2
    total = N + K + 4 + R + J
    names = ("length", "tok", "cot", "gain_own", "w_in_own", "conv_w", "conv_b", "w_xt_own", "w_dt_own", "dt_bias", "a_log", "d_skip", "w_out_own")
    outs = dict(
        output=((T, D), BF16), input_grad=((T, D), F32), out=((9 * 256, D), BF16), out_rows=((512, 256), BF16)
    )
    plan = scratch_plan(z)
    plan.update(
        w_in=((D, 2 * E), BF16), w_out=((E, D), BF16), w_xt=((J, E), BF16), w_dt=((R, E), BF16),
        pack=((N + K + 4, EH), F32), pack_in=((N + K + 4, EH), F32), w_dt_in=((R, EH), BF16), w_xt_in=((J, EH), BF16),
        normed=((T, D), BF16), gated=((T, E), BF16), d_branch=((T, D), BF16), d_inner=((T, E), BF16),
        d_gate=((T, E), BF16), rows=((total, E), F32), normed_in=((T, DH), BF16), d_branch_in=((T, D), BF16),
        gated_in=((T, EH), BF16), d_gate_in=((T, E), BF16), d_inner_in=((T, E), BF16), rows_in=((total, EH), F32),
        acc=((9 * 256, D), BF16), recv=((9 * 240, D), BF16), acc_rows=((512, 256), BF16), recv_rows=((480, 256), BF16),
    )
    sems = GATHERS + SWAPS + 2 * LEVELS * 10
    names = list(names) + list(outs) + list(plan) + ["local", "send", "recv_sem"]
    specs = [SMEM] + [VMEM] * 12
    specs[4] = specs[12] = ANY
    return pl.pallas_call(
        functools.partial(fused_kernel, z, names),
        out_shape=[jax.ShapeDtypeStruct(*spec) for spec in outs.values()],
        in_specs=specs,
        out_specs=[VMEM] * len(outs),
        scratch_shapes=[pltpu.VMEM(*spec) for spec in plan.values()]
        + [pltpu.SemaphoreType.DMA((2,)), pltpu.SemaphoreType.DMA((sems,)), pltpu.SemaphoreType.DMA((sems,))],
        compiler_params=pltpu.CompilerParams(collective_id=0, has_side_effects=True, vmem_limit_bytes=63 * MB),
        name="layer",
    )(length, tokens, cotangent, gain, w_in, conv_w, conv_b, w_xt, w_dt, dt_bias, a_log, d_skip, w_out)


def finish_kernel(N, K, R, J, *refs):
    out, out_rows, output_in, input_grad_in, output, input_grad = refs[:6]
    g_gain, g_in, g_conv_w, g_conv_b, g_xt, g_dt, g_dt_bias, g_a_log, g_skip, g_out = refs[6:16]
    low, wide, kept, kept_wide, sem_in, sem_out = refs[16:]
    DH, D = g_in.shape[0], out.shape[1]
    size = 128
    count = out.shape[0] // size
    reads, writes = [], []
    for index in range(count):
        rows = pl.ds(index * size, size)
        reads.append(pltpu.make_async_copy(out.at[rows, :], low.at[rows, :], sem_in.at[index]))
        unit, first = index * size // D, index * size % D
        if unit == 0:
            target = g_out.at[pl.ds(first, size), :]
        else:
            place = (2 - unit) * 2 + first // DH
            target = g_in.at[pl.ds(first % DH, size), pl.ds(place * D, D)]
        writes.append(pltpu.make_async_copy(wide.at[rows, :], target, sem_out.at[index]))
    for index, (source, held, target) in enumerate(
        ((input_grad_in, kept_wide, input_grad), (output_in, kept, output))
    ):
        reads.append(pltpu.make_async_copy(source, held, sem_in.at[count + index]))
        writes.append(pltpu.make_async_copy(held, target, sem_out.at[count + index]))
    for copy in reads:
        copy.start()
    M = N + K + 4
    for part in range(3):
        value = out_rows[pl.ds(160 * part, 160), :].astype(F32)
        cols = pl.ds(256 * part, 256)
        g_a_log[:, cols] = value[:N]
        g_conv_w[:, cols] = value[N : N + K]
        g_conv_b[cols] = value[N + K]
        g_dt_bias[cols] = value[N + K + 1]
        g_skip[cols] = value[N + K + 2]
        if part == 0:
            g_gain[pl.ds(0, 256)] = value[N + K + 3]
        elif part == 1:
            g_gain[pl.ds(256, DH - 256)] = value[N + K + 3, : DH - 256]
        g_dt[:, cols] = value[M : M + R]
        g_xt[:, cols] = value[M + R : M + R + J]
    for index in range(count):
        rows = pl.ds(index * size, size)
        reads[index].wait()
        wide[rows, :] = low[rows, :].astype(F32)
        writes[index].start()
    for index in range(count, count + 2):
        reads[index].wait()
        writes[index].start()
    for copy in writes:
        copy.wait()


def fused_body(tokens, lengths, cotangent, *shards):
    shards = list(shards)
    shards[4] = shards[4].T
    output, input_grad, out, out_rows = fused_layer(lengths, tokens[0], cotangent[0], *shards)
    gain, w_in, conv_w, conv_b, w_xt, w_dt, dt_bias, a_log, d_skip, w_out = shards
    chunks = out.shape[0] // 128
    specs = [VMEM] * 12
    specs[0] = specs[1] = specs[3] = specs[11] = ANY
    results = pl.pallas_call(
        functools.partial(finish_kernel, a_log.shape[0], conv_w.shape[0], w_dt.shape[0], w_xt.shape[0]),
        out_shape=[jax.ShapeDtypeStruct(x.shape, x.dtype) for x in (output, input_grad)]
        + [jax.ShapeDtypeStruct(w.shape, F32) for w in shards],
        in_specs=[ANY, VMEM, ANY, ANY],
        out_specs=specs,
        scratch_shapes=[
            pltpu.VMEM(out.shape, BF16), pltpu.VMEM(out.shape, F32), pltpu.VMEM(output.shape, BF16),
            pltpu.VMEM(output.shape, F32), pltpu.SemaphoreType.DMA((chunks + 2,)),
            pltpu.SemaphoreType.DMA((chunks + 2,)),
        ],
        compiler_params=pltpu.CompilerParams(vmem_limit_bytes=60 * MB),
        name="finish",
    )(out, out_rows, output, input_grad)
    output, input_grad, *grads = results
    grads[4] = grads[4].T
    return (output[None], input_grad[None], *grads)


def solution(mesh):
    seq, row, col, one = P(("dp", "fsdp"), None, None), P("fsdp", None), P(None, "fsdp"), P("fsdp")
    fused = mesh.shape["dp"] == PIECES and mesh.shape["fsdp"] == 2
    return jax.shard_map(
        fused_body if fused else plain_body,
        mesh=mesh,
        in_specs=(seq, P(("dp", "fsdp")), seq, one, row, col, one, row, col, one, col, one, row),
        out_specs=(seq, seq, one, row, col, one, row, col, one, col, one, row),
        check_vma=False,
    )
```

```python
import functools
import types

import jax
import jax.numpy as jnp
from jax import lax
from jax.experimental import pallas as pl
from jax.experimental.pallas import tpu as pltpu
from jax.sharding import PartitionSpec as P

F32 = jnp.float32
BF16 = jnp.bfloat16
EPS = 1e-05
STEPS = 16
CHUNK = 256
PAD = 8
LOG2E = 1.4426950408889634
MB = 2**20
VMEM = pl.BlockSpec(memory_space=pltpu.VMEM)
SMEM = pl.BlockSpec(memory_space=pltpu.SMEM)
ANY = pl.BlockSpec(memory_space=pl.ANY)
MESH = pl.DeviceIdType.MESH


def dot(left, right, over=(1, 0)):
    dims = (((over[0],), (over[1],)), ((), ()))
    return lax.dot_general(left, right, dims, preferred_element_type=F32)


def span(index, size):
    return pl.ds(pl.multiple_of(index * size, size), size)


def repeat(count, step, unroll=1):
    def run(index, carry):
        step(index)
        return carry

    lax.fori_loop(0, count, run, 0, unroll=min(unroll, count))


def row_plan(s):
    bias = s.N + s.K
    return types.SimpleNamespace(conv=s.N, bias=bias, dt_bias=bias + 1, skip=bias + 2, gain=bias + 3)


def start_norm(s):
    def run(block):
        rows = span(block, 64)
        x = s.tok[rows, :].astype(F32)
        scale = lax.rsqrt(jnp.mean(x * x, axis=1, keepdims=True) + EPS)
        s.inv[rows, :] = jnp.broadcast_to(scale, (64, 128))
        at = block * 64 + lax.broadcasted_iota(jnp.int32, (64, 1), 0)
        live = (at < s.length[0]).astype(F32)
        s.d_branch[rows, :] = (live * s.cot[rows, :].astype(F32)).astype(BF16)

    repeat(s.T // 64, run, 4)


def norm(s):
    def run(block):
        rows = span(block, 64)
        x = s.tok[rows, :].astype(F32)
        s.normed[rows, :] = (x * s.inv[rows, pl.ds(0, 1)] * s.gain[...]).astype(BF16)

    repeat(s.T // 64, run, 4)


def project_inner(s, first, count):
    at = row_plan(s)

    def run(index):
        cols = span(first + index, 256)
        s.inner[pl.ds(PAD, s.T), cols] = dot(s.normed[...], s.w_in[:, cols])

    repeat(count, run, 6)

    def convolve(index):
        cols = span(2 * first + index, 128)
        value = s.small[pl.ds(at.bias, 1), cols] + sum(
            s.small[pl.ds(at.conv + k, 1), cols] * s.inner[pl.ds(PAD - s.K + 1 + k, s.T), cols]
            for k in range(s.K)
        )
        sigma = jax.nn.sigmoid(value)
        s.active[:, cols] = (value * sigma).astype(BF16)
        s.cslope[:, cols] = sigma * (1.0 + value * (1.0 - sigma))

    repeat(2 * count, convolve, 4)


def project_gate(s, first, count):
    def run(index):
        cols = span(first + index, 256)
        source = pl.ds(pl.multiple_of(s.E + (first + index) * 256, 256), 256)
        value = dot(s.normed[...], s.w_in[:, source])
        sigma = jax.nn.sigmoid(value)
        s.gact[:, cols] = value * sigma
        s.gslope[:, cols] = sigma * (1.0 + value * (1.0 - sigma))

    repeat(count, run, 6)


def diagonal(s):
    wide = STEPS * s.N
    at = lax.broadcasted_iota(jnp.int32, (s.T, wide), 0)
    to = lax.broadcasted_iota(jnp.int32, (s.T, wide), 1)
    return (at % STEPS == to // s.N).astype(F32)


def spread_rows(s):
    N, J, wide = s.N, s.J, STEPS * s.N
    state = lax.broadcasted_iota(jnp.int32, (N, J), 0)
    col = lax.broadcasted_iota(jnp.int32, (N, J), 1)
    mask = jnp.logical_or(col == s.R + state, col == s.R + N + state).astype(F32)
    row = lax.broadcasted_iota(jnp.int32, (J, 256), 0)
    lane = lax.broadcasted_iota(jnp.int32, (J, 256), 1)
    first = jnp.logical_and(row < s.R + N, lane < 128)
    last = jnp.logical_and(row >= s.R + N, lane >= 128)
    ones = jnp.logical_or(first, last).astype(BF16)

    def run(block):
        rows = s.proj[span(block, STEPS), :].astype(F32)
        parts = [(jnp.broadcast_to(rows[i : i + 1], (N, J)) * mask).astype(BF16) for i in range(STEPS)]
        s.spread[span(block, wide), :] = dot(jnp.concatenate(parts, axis=0), ones)

    repeat(s.T // STEPS, run, 4)


def scan_inputs(s):
    wide = STEPS * s.N
    at = row_plan(s)
    s.proj[...] = dot(s.active[...], s.w_xt[...], (1, 1)).astype(BF16)
    row = lax.broadcasted_iota(jnp.int32, (s.J, wide), 0)
    col = lax.broadcasted_iota(jnp.int32, (s.J, wide), 1)
    mask = diagonal(s)
    pick_b = (row == s.R + col % s.N).astype(BF16)
    pick_c = (row == s.R + s.N + col % s.N).astype(BF16)
    s.bmat[...] = (dot(s.proj[...], pick_b) * mask).astype(BF16)
    s.cmat[...] = (dot(s.proj[...], pick_c) * mask).astype(BF16)
    spread_rows(s)

    def run(index):
        cols = span(index, 256)
        pre = dot(s.proj[:, : s.R], s.w_dt[:, cols]) + s.small[pl.ds(at.dt_bias, 1), cols]
        size = jnp.maximum(pre, 0.0) + jnp.log1p(jnp.exp(-jnp.abs(pre)))
        s.step[:, cols] = size
        s.sigp[:, cols] = jax.nn.sigmoid(pre)

    repeat(s.E // 256, run, 6)
    s.decay[...] = -jnp.exp(s.small[pl.ds(0, s.N), :]) * LOG2E


def forward_scan(s):
    N, E, wide = s.N, s.E, STEPS * s.N
    s.states[pl.ds(0, N), :] = jnp.zeros((N, E), BF16)

    def scan_sum(block):
        rows = span(block, STEPS)
        held = s.states[pl.ds(pl.multiple_of(block * wide + N, N), wide), :]
        s.mixed[rows, :] = dot(s.cmat[rows, :], held)

    def run(block, state):
        scan_sum(jnp.maximum(block - 1, 0))
        rows = span(block, STEPS)
        size = s.step[rows, :]
        push = size * s.active[rows, :].astype(F32)
        for i in range(STEPS):
            t = block * STEPS + i
            b_row = s.spread[span(t, N), pl.ds(0, 128)]
            b_row = jnp.concatenate([b_row] * (E // 128), axis=1)
            factor = jnp.exp2(jnp.broadcast_to(size[i : i + 1], (N, E)) * s.decay[...])
            state = factor * state + b_row * jnp.broadcast_to(push[i : i + 1], (N, E))
            s.states[span(t + 1, N), :] = state.astype(BF16)
        return state

    lax.fori_loop(0, s.T // STEPS, run, jnp.zeros((N, E), F32))
    scan_sum(s.T // STEPS - 1)


def mix(s):
    at = row_plan(s)

    def run(index):
        cols = span(index, 128)
        value = s.mixed[pl.ds(0, s.T), cols] + s.small[pl.ds(at.skip, 1), cols] * s.active[:, cols].astype(F32)
        s.mixed[pl.ds(0, s.T), cols] = value
        s.gated[:, cols] = (value * s.gact[:, cols]).astype(BF16)

    repeat(s.E // 128, run, 2)


def back_out(s):
    at = row_plan(s)

    def run(index):
        cols = span(index, 256)
        d_gated = dot(s.d_branch[...], s.w_out[cols, :], (1, 1))
        d_value = d_gated * s.gact[:, cols]
        s.d_mixed[:, cols] = d_value
        s.d_gate[:, cols] = (d_gated * s.mixed[pl.ds(0, s.T), cols] * s.gslope[:, cols]).astype(BF16)
        s.rows[pl.ds(at.skip, 1), cols] = jnp.sum(
            d_value * s.active[:, cols].astype(F32), axis=0, keepdims=True
        )

    repeat(s.E // 256, run, 6)


def project_out(s):
    def run(index):
        cols = span(index, 256)
        branch = dot(s.gated[...], s.w_out[:, cols])
        at = lax.broadcasted_iota(jnp.int32, (s.T, 1), 0)
        live = (at < s.length[0]).astype(F32)
        s.output[:, cols] = (s.tok[:, cols].astype(F32) + live * branch).astype(BF16)

    repeat(s.D // 256, run, 3)


def backward_scan(s, between=None):
    N, E, wide, half = s.N, s.E, STEPS * s.N, s.N // 2
    blocks = s.T // STEPS
    s.carry[...] = jnp.zeros((N, E), F32)
    s.rows[pl.ds(0, N), :] = jnp.zeros((N, E), F32)
    at = lax.broadcasted_iota(jnp.int32, (STEPS, STEPS * half), 0)
    to = lax.broadcasted_iota(jnp.int32, (STEPS, STEPS * half), 1)
    gather = (at == to // half).astype(BF16)

    def run(k):
        block = blocks - 1 - k
        rows = span(block, STEPS)
        for chunk in range(E // CHUNK):
            cols = pl.ds(chunk * CHUNK, CHUNK)
            later, total = s.carry[:, cols], s.rows[pl.ds(0, N), cols]
            size, d_value = s.step[rows, cols], s.d_mixed[rows, cols]
            rate = s.decay[:, cols]
            for i in reversed(range(STEPS)):
                t = block * STEPS + i
                dt = jnp.broadcast_to(size[i : i + 1], (N, CHUNK))
                c_row = s.spread[span(t, N), pl.ds(128, 128)]
                c_row = jnp.concatenate([c_row] * (CHUNK // 128), axis=1)
                lam = c_row * jnp.broadcast_to(d_value[i : i + 1], (N, CHUNK)) + later
                s.lam[pl.ds(i * N, N), cols] = lam.astype(BF16)
                later = jnp.exp2(dt * rate) * lam
                weighted = later * s.states[span(t, N), cols].astype(F32)
                total = total + weighted * dt
                part = weighted * rate
                part = part[:half] + part[half:]
                if i % 2 == 1:
                    odd = part
                else:
                    s.part[pl.ds(i * half, N), cols] = jnp.concatenate([part, odd], axis=0).astype(BF16)
            s.carry[:, cols] = later
            s.rows[pl.ds(0, N), cols] = total
            held = s.lam[:, cols]
            s.gact[rows, cols] = dot(s.bmat[rows, :], held)
            s.gslope[rows, cols] = dot(gather, s.part[:, cols])
            drive = (size * s.active[rows, cols].astype(F32)).astype(BF16)
            b_part = dot(drive, held, (1, 1))
            after = s.states[pl.ds(pl.multiple_of(block * wide + N, N), wide), cols]
            c_part = dot(d_value.astype(BF16), after, (1, 1))
            if chunk == 0:
                s.db[rows, :] = b_part
                s.dc[rows, :] = c_part
            else:
                s.db[rows, :] += b_part
                s.dc[rows, :] += c_part
        if between is not None:
            between(k)

    repeat(blocks, run)
    s.rows[pl.ds(0, N), :] = s.rows[pl.ds(0, N), :] * s.decay[...] * (1.0 / LOG2E)


def back_step(s):
    at = row_plan(s)

    def run(index):
        cols = span(index, 128)
        wide = s.active[:, cols].astype(F32)
        adjoint = s.gact[:, cols]
        d_pre = (wide * adjoint + s.gslope[:, cols] * (1.0 / LOG2E)) * s.sigp[:, cols]
        s.rows[pl.ds(at.dt_bias, 1), cols] = jnp.sum(d_pre, axis=0, keepdims=True)
        s.d_pre_low[:, cols] = d_pre.astype(BF16)
        s.d_mixed[:, cols] = (
            s.d_mixed[:, cols] * s.small[pl.ds(at.skip, 1), cols] + s.step[:, cols] * adjoint
        )

    repeat(s.E // 128, run)


def back_proj(s):
    wide = STEPS * s.N
    row = lax.broadcasted_iota(jnp.int32, (wide, s.N), 0)
    col = lax.broadcasted_iota(jnp.int32, (wide, s.N), 1)
    pick = (row % s.N == col).astype(BF16)
    mask = diagonal(s)
    s.d_proj[:, pl.ds(0, s.R)] = dot(s.d_pre_low[...], s.w_dt[...], (1, 1)).astype(BF16)
    s.d_proj[:, pl.ds(s.R, s.N)] = dot((s.db[...] * mask).astype(BF16), pick).astype(BF16)
    s.d_proj[:, pl.ds(s.R + s.N, s.N)] = dot((s.dc[...] * mask).astype(BF16), pick).astype(BF16)


def back_conv(s, part, count):
    at = row_plan(s)
    s.mixed[pl.ds(s.T, PAD), :] = jnp.zeros((PAD, s.E), F32)
    first = at.gain + 1

    def run(index):
        cols = span(part + index, 128)
        s.rows[pl.ds(first, s.R), cols] = dot(s.proj[:, : s.R], s.d_pre_low[:, cols], (0, 0))
        s.rows[pl.ds(first + s.R, s.J), cols] = dot(s.d_proj[...], s.active[:, cols], (0, 0))
        d_active = s.d_mixed[:, cols] + dot(s.d_proj[...], s.w_xt[:, cols])
        d_value = d_active * s.cslope[:, cols]
        s.mixed[pl.ds(0, s.T), cols] = d_value
        s.rows[pl.ds(at.bias, 1), cols] = jnp.sum(d_value, axis=0, keepdims=True)
        total = jnp.zeros_like(d_value)
        for k in range(s.K):
            s.rows[pl.ds(at.conv + k, 1), cols] = jnp.sum(
                d_value * s.inner[pl.ds(PAD - s.K + 1 + k, s.T), cols], axis=0, keepdims=True
            )
            taps = s.small[pl.ds(at.conv + k, 1), cols]
            total = total + taps * s.mixed[pl.ds(s.K - 1 - k, s.T), cols]
        s.d_inner[:, cols] = total.astype(BF16)

    repeat(count, run, 6)


def back_in(s):
    def run(index):
        rows = span(index, 256)
        s.d_normed[:, rows] = dot(s.d_inner[...], s.w_in[rows, pl.ds(0, s.E)], (1, 1)) + dot(
            s.d_gate[...], s.w_in[rows, pl.ds(s.E, s.E)], (1, 1)
        )

    repeat(s.D // 256, run, 3)


def back_norm(s):
    s.d_gain[...] = jnp.zeros((1, s.D), F32)

    def run(block):
        rows = span(block, 64)
        x = s.tok[rows, :].astype(F32)
        scale = s.inv[rows, pl.ds(0, 1)]
        d_value = s.d_normed[rows, :]
        s.d_gain[...] += jnp.sum(d_value * x * scale, axis=0, keepdims=True)
        d_scaled = d_value * s.gain[...]
        shared = jnp.mean(d_scaled * x, axis=1, keepdims=True)
        s.input_grad[rows, :] = (
            s.cot[rows, :].astype(F32) + scale * d_scaled - x * (scale * scale * scale) * shared
        )

    repeat(s.T // 64, run, 4)


def sizes(tokens, w_out, a_log, w_dt, w_xt, conv_w):
    return dict(
        T=tokens.shape[0], D=tokens.shape[1], E=w_out.shape[0], N=a_log.shape[0],
        R=w_dt.shape[0], J=w_xt.shape[0], K=conv_w.shape[0],
    )


def scratch_plan(z):
    T, D, E, N, R, J, K = (z[n] for n in "TDENRJK")
    wide = STEPS * N
    full, low = ((T, E), F32), ((T, E), BF16)
    padded = ((T + PAD, E), F32)
    count = N + K + 4
    return dict(
        inv=((T, 128), F32), gain=((1, D), F32), small=((count, E), F32), inner=padded, gact=full, gslope=full,
        cslope=full, active=low, proj=((T, J), BF16), bmat=((T, wide), BF16), cmat=((T, wide), BF16),
        spread=((T * N, 256), F32), decay=((N, E), F32), step=full, sigp=full,
        mixed=padded, d_mixed=full, states=(((T + 1) * N, E), BF16), carry=((N, E), F32),
        lam=((wide, E), BF16), part=((wide // 2, E), BF16), db=((T, wide), F32), dc=((T, wide), F32),
        d_pre_low=low, d_proj=((T, J), BF16), d_normed=((T, D), F32), d_gain=((1, D), F32),
    )


def plain_kernel(z, names, *refs):
    s = types.SimpleNamespace(**z, **dict(zip(names, refs)))
    at = row_plan(s)
    s.small[pl.ds(0, s.N), :] = s.a_log[...].astype(F32)
    s.small[pl.ds(at.conv, s.K), :] = s.conv_w[...].astype(F32)
    s.small[pl.ds(at.bias, 1), :] = s.conv_b[...].astype(F32)
    s.small[pl.ds(at.dt_bias, 1), :] = s.dt_bias[...].astype(F32)
    s.small[pl.ds(at.skip, 1), :] = s.d_skip[...].astype(F32)
    s.gain[...] = s.gain_in[...].astype(F32)
    s.rows[...] = jnp.zeros(s.rows.shape, F32)
    s.inner[pl.ds(0, PAD), :] = jnp.zeros((PAD, s.E), F32)
    for step in (start_norm, norm):
        step(s)
    project_inner(s, 0, s.E // 256)
    project_gate(s, 0, s.E // 256)
    for step in (scan_inputs, forward_scan, mix, project_out, back_out):
        step(s)
    backward_scan(s)
    back_step(s)
    back_proj(s)
    back_conv(s, 0, s.E // 128)
    back_in(s)
    back_norm(s)
    s.g_gain[...] = s.d_gain[...]


def plain_layer(length, tokens, cotangent, gain, w_in, conv_w, conv_b, w_xt, w_dt, dt_bias, a_log, d_skip, w_out):
    z = sizes(tokens, w_out, a_log, w_dt, w_xt, conv_w)
    T, D, E, N, R, J, K = (z[n] for n in "TDENRJK")
    plan = scratch_plan(z)
    ins = ("length", "tok", "cot", "gain_in", "w_in", "conv_w", "conv_b", "w_xt", "w_dt", "dt_bias", "a_log", "d_skip", "w_out")
    outs = dict(
        output=((T, D), BF16), input_grad=((T, D), F32), normed=((T, D), BF16), gated=((T, E), BF16),
        d_branch=((T, D), BF16), d_inner=((T, E), BF16), d_gate=((T, E), BF16), g_gain=((1, D), F32),
        rows=((N + K + 4 + R + J, E), F32),
    )
    names = list(ins) + list(outs) + list(plan)
    return pl.pallas_call(
        functools.partial(plain_kernel, z, names),
        out_shape=[jax.ShapeDtypeStruct(*spec) for spec in outs.values()],
        in_specs=[SMEM] + [VMEM] * 12,
        out_specs=[VMEM] * len(outs),
        scratch_shapes=[pltpu.VMEM(*spec) for spec in plan.values()],
        compiler_params=pltpu.CompilerParams(vmem_limit_bytes=60 * MB),
        name="plain_layer",
    )(length, tokens, cotangent, gain, w_in, conv_w, conv_b, w_xt, w_dt, dt_bias, a_log, d_skip, w_out)


def plain_body(tokens, lengths, cotangent, *shards):
    axes = (0, 0, 1, 0, 0, 1, 0, 1, 0, 0)
    weights = [lax.all_gather(w, "fsdp", axis=a, tiled=True) for w, a in zip(shards, axes)]
    weights = [w.reshape(1, -1) if w.ndim == 1 else w for w in weights]
    weights[4] = weights[4].T
    output, input_grad, normed, gated, d_branch, d_inner, d_gate, g_gain, rows = plain_layer(
        lengths, tokens[0], cotangent[0], *weights
    )
    big_in = dot(normed, jnp.concatenate([d_inner, d_gate], axis=1), (0, 0))
    big_out = dot(gated, d_branch, (0, 0))

    def scatter(value, axis):
        return lax.psum_scatter(value, "fsdp", scatter_dimension=axis, tiled=True)

    own = (
        scatter(big_in.astype(BF16), 0), scatter(big_out.astype(BF16), 0),
        scatter(rows, 1), scatter(g_gain[0], 0),
    )
    own_in, own_out, rows, own_gain = lax.psum(own, "dp")
    N, K, R = shards[7].shape[0], shards[2].shape[0], shards[5].shape[0]
    M = N + K + 4
    return (
        output[None], input_grad[None], own_gain, own_in.astype(F32), rows[N : N + K], rows[N + K],
        rows[M + R :].T, rows[M : M + R], rows[N + K + 1], rows[:N], rows[N + K + 2], own_out.astype(F32),
    )


ORDERS = (
    ((3,), (0,), (1,), (2,)),
    ((2,), (1,), (0,), (3,)),
    ((0,), (2,), (1,), (3,)),
    ((0, 1), (2, 3)),
    ((0,), (1,), (2,), (3,)),
    ((1,), (0,), (2,), (3,)),
    ((1,), (0,), (2, 3)),
    ((0,), (1,), (2, 3)),
    ((2,), (0, 1), (3,)),
    ((1,), (0,), (2, 3)),
)
DURING = {
    6: ((2, 0),),
    9: ((0, 0), (1, 0), (3, 0)),
    11: ((2, 1), (5, 0)),
    13: ((3, 1), (4, 0), (1, 1)),
    14: ((2, 2),),
    15: ((0, 1),),
    17: ((5, 1), (4, 1), (3, 2)),
    18: ((2, 3), (1, 2), (0, 2)),
    19: ((5, 2),),
    20: ((4, 2),),
    21: ((2, 4),),
    22: ((1, 3), (0, 3), (3, 3)),
}
AFTER = (
    (5, 3), (6, 0), (7, 0), (8, 0), (2, 5), (4, 3), (0, 4), (1, 4), (5, 4), (6, 1), (9, 0), (2, 6),
    (7, 1), (4, 4), (5, 5), (1, 5), (8, 1), (9, 1), (6, 2), (0, 5), (7, 2), (4, 5), (1, 6), (8, 2),
    (2, 7), (9, 2), (4, 6), (5, 6), (6, 3), (0, 6), (7, 3), (1, 7), (5, 7), (8, 3), (4, 7), (9, 3),
    (7, 4), (6, 4), (8, 4), (9, 4), (6, 5), (0, 7), (7, 5), (8, 5), (9, 5),
)
PIECES = 16
FIRST, SECOND = 0, 2
GATHERS = 10
SWAPS = 7
COPIES = 12


def packed_rows(s):
    return s.N + s.K + 4


class Sum:
    def __init__(self, s, number, stages, acc, recv, out, result, first, piece):
        self.s, self.stages, self.piece, self.steps = s, stages, piece, 2 * len(stages)
        self.sem = GATHERS + SWAPS + COPIES * number
        self.acc, self.recv, self.out = acc, recv, out
        self.first, self.landed = first * PIECES * piece, first * (PIECES - 1) * piece
        self.bits = [[lax.rem(s.dp // 2**b, 2) for b in stage] for stage in stages]
        whole = pl.ds(self.first, PIECES * piece)
        self.leave = pltpu.make_async_copy(out.at[whole, :], result.at[whole, :], s.local.at[6 + number])
        self.plan = []
        start, count, landing, sem = 0, PIECES, 0, self.sem
        for stage, bits in zip(stages, self.bits):
            group = 2 ** len(stage)
            count //= group
            others = []
            for flip in range(1, group):
                device, place = s.dp, 0
                for j, (b, bit) in enumerate(zip(stage, bits)):
                    flipped = flip // 2**j % 2
                    device = device + flipped * (1 - 2 * bit) * 2**b
                    place = place + (flipped + (1 - 2 * flipped) * bit) * 2**j
                others.append(((device, s.me), start + place * count, landing, sem))
                landing, sem = landing + count, sem + 2
            for j, bit in enumerate(bits):
                start = start + bit * 2**j * count
            self.plan.append((others, start, count))

    def rows(self, start, count):
        return pl.ds(pl.multiple_of(self.first + start * self.piece, 16), count * self.piece)

    def reduce_copies(self, level):
        others, _, count = self.plan[level]
        return [
            self.s.remote(
                self.acc.at[self.rows(theirs, count), :],
                self.recv.at[pl.ds(self.landed + landing * self.piece, count * self.piece), :], sem, device,
            )
            for device, theirs, landing, sem in others
        ]

    def spread_copies(self, level, sent=True):
        others, mine, count = self.plan[level]
        copies = []
        for device, theirs, _, sem in others:
            rows = self.rows(mine if sent else theirs, count)
            copies.append(self.s.remote(self.out.at[rows, :], self.out.at[rows, :], sem + 1, device))
        return copies

    def start(self):
        for copy in self.reduce_copies(0):
            copy.start()

    def carry_on(self, step):
        levels = len(self.stages)
        if step < levels:
            self.reduce(step)
            following = self.spread_copies(step) if step == levels - 1 else self.reduce_copies(step + 1)
        else:
            level = self.steps - 1 - step
            for copy in self.spread_copies(level, False):
                copy.wait_recv()
            following = self.spread_copies(level - 1) if level > 0 else [self.leave]
        for copy in following:
            copy.start()

    def reduce(self, level):
        for copy in self.reduce_copies(level):
            copy.wait_recv()
        others, mine, count = self.plan[level]
        target = self.out if level == len(self.stages) - 1 else self.acc

        def add(index):
            here = self.rows(mine + index, 1)
            total = self.acc[here, :].astype(F32)
            for _, _, landing, _ in others:
                there = pl.ds(pl.multiple_of(self.landed + (landing + index) * self.piece, 16), self.piece)
                total = total + self.recv[there, :].astype(F32)
            target[here, :] = total.astype(BF16)

        repeat(count, add)

    def finish(self):
        for level in range(len(self.stages)):
            for copy in self.reduce_copies(level) + self.spread_copies(level):
                copy.wait_send()
        self.leave.wait()


def fused_kernel(z, names, *refs):
    s = types.SimpleNamespace(**z, **dict(zip(names, refs)))
    D, E = s.D, s.E
    DH, EH = D // 2, E // 2
    at = row_plan(s)
    count = packed_rows(s)
    s.dp, s.me = lax.axis_index("dp"), lax.axis_index("fsdp")
    other = 1 - s.me
    peer = (s.dp, other)

    def remote(src, dst, sem, device):
        return pltpu.make_async_remote_copy(
            src_ref=src, dst_ref=dst, send_sem=s.send.at[sem], recv_sem=s.recv_sem.at[sem],
            device_id=device, device_id_type=MESH,
        )

    s.remote = remote
    units = [Sum(s, i, ORDERS[i], s.acc, s.recv, s.out, s.out_to, i, 16) for i in range(9)]
    units.append(Sum(s, 9, ORDERS[9], s.acc_rows, s.recv_rows, s.out_rows, s.out_rows_to, 0, 32))

    barrier = pltpu.get_barrier_semaphore()
    pl.semaphore_signal(barrier, inc=1, device_id=peer, device_id_type=MESH)
    partners = {}
    for unit in units:
        for stage, (others, _, _) in zip(unit.stages, unit.plan):
            for flip, other_one in enumerate(others):
                partners[(stage, flip)] = other_one[0]
    greeted = {}
    for (stage, flip), device in partners.items():
        greeted[tuple(sorted(b for j, b in enumerate(stage) if (flip + 1) // 2**j % 2))] = device
    for device in greeted.values():
        pl.semaphore_signal(barrier, inc=1, device_id=device, device_id_type=MESH)

    mine_d, mine_e = span(s.me, DH), span(s.me, EH)
    theirs_d, theirs_e = span(other, DH), span(other, EH)
    local_in = pltpu.make_async_copy(s.w_in_own, s.w_in.at[mine_d, :], s.local.at[0])
    local_out = pltpu.make_async_copy(s.w_out_own, s.w_out.at[mine_e, :], s.local.at[1])
    local_tok = pltpu.make_async_copy(s.tok_own, s.tok, s.local.at[2])
    local_cot = pltpu.make_async_copy(s.cot_own, s.cot, s.local.at[3])
    for copy in (local_tok, local_cot, local_in, local_out):
        copy.start()
    s.pack[pl.ds(0, s.N), :] = s.a_log[...].astype(F32)
    s.pack[pl.ds(at.conv, s.K), :] = s.conv_w[...].astype(F32)
    s.pack[pl.ds(at.bias, 1), :] = s.conv_b[...].astype(F32)[None, :]
    s.pack[pl.ds(at.dt_bias, 1), :] = s.dt_bias[...].astype(F32)[None, :]
    s.pack[pl.ds(at.skip, 1), :] = s.d_skip[...].astype(F32)[None, :]
    s.pack[pl.ds(at.gain, 1), :] = jnp.zeros((1, EH), F32)
    s.pack[pl.ds(at.gain, 1), pl.ds(0, DH)] = s.gain_own[...].astype(F32)[None, :]
    pl.semaphore_wait(barrier, len(greeted) + 1)

    width = 2 * E // 6
    gathers = [remote(s.pack, s.pack_in, 0, peer)]
    for j in range(6):
        cols = pl.ds(j * width, width)
        gathers.append(remote(s.w_in_own.at[:, cols], s.w_in.at[mine_d, cols], 1 + j, peer))
    gathers.append(remote(s.w_xt_own, s.w_xt_in, 7, peer))
    gathers.append(remote(s.w_dt_own, s.w_dt_in, 8, peer))
    gathers.append(remote(s.w_out_own, s.w_out.at[mine_e, :], 9, peer))
    for j in (0, 1, 2, 3, 7, 8, 4, 5, 6, 9):
        gathers[j].start()

    swaps = [
        remote(s.normed.at[:, theirs_d], s.normed_in, GATHERS, peer),
        remote(s.d_branch, s.d_branch_in, GATHERS + 1, peer),
        remote(s.gated.at[:, theirs_e], s.gated_in, GATHERS + 2, peer),
        remote(s.d_gate, s.d_gate_in, GATHERS + 3, peer),
        remote(s.d_inner.at[:, pl.ds(0, EH)], s.d_inner_in.at[:, pl.ds(0, EH)], GATHERS + 4, peer),
        remote(s.d_inner.at[:, pl.ds(EH, EH)], s.d_inner_in.at[:, pl.ds(EH, EH)], GATHERS + 5, peer),
        remote(s.rows.at[:, theirs_e], s.rows_in, GATHERS + 6, peer),
    ]

    local_tok.wait()
    local_cot.wait()
    start_norm(s)
    swaps[1].start()
    s.w_xt[:, mine_e] = s.w_xt_own[...]
    s.w_dt[:, mine_e] = s.w_dt_own[...]
    s.small[:, mine_e] = s.pack[...]
    s.gain[:, mine_d] = s.pack[pl.ds(at.gain, 1), pl.ds(0, DH)]
    s.inner[pl.ds(0, PAD), :] = jnp.zeros((PAD, E), F32)
    gathers[0].wait_recv()
    s.small[:, theirs_e] = s.pack_in[...]
    s.gain[:, theirs_d] = s.pack_in[pl.ds(at.gain, 1), pl.ds(0, DH)]
    norm(s)
    swaps[0].start()
    local_in.wait()
    for j in range(3):
        gathers[1 + j].wait_recv()
        project_inner(s, 2 * j, 2)
    gathers[7].wait_recv()
    gathers[8].wait_recv()
    s.w_dt[:, theirs_e] = s.w_dt_in[...]
    s.w_xt[:, theirs_e] = s.w_xt_in[...]
    scan_inputs(s)
    for j in range(3):
        gathers[4 + j].wait_recv()
        project_gate(s, 2 * j, 2)
    forward_scan(s)
    mix(s)
    swaps[2].start()
    local_out.wait()
    gathers[9].wait_recv()
    back_out(s)
    swaps[3].start()
    def product(left, left_in, right, right_in, shift, cols, across):
        own = pl.ds(pl.multiple_of(shift + cols.start, 128), cols.size)
        total = dot(left[:, own], right[:, across], (0, 0)) + dot(left_in[:, cols], right_in[:, across], (0, 0))
        return total.astype(BF16)

    def grad_out(color):
        cols = pl.ds(256 * color, 256)
        s.acc[pl.ds(256 * color, 256), :] = product(
            s.gated, s.gated_in, s.d_branch, s.d_branch_in, s.me * EH, cols, pl.ds(0, D)
        )

    def grad_in(unit, color, right, right_in):
        first = 256 * (3 * unit + color)
        parts = (((0, 256, 0),), ((256, 128, 0), (0, 128, EH)), ((128, 256, EH),))[color]
        for start, size, across in parts:
            s.acc[pl.ds(first, size), :] = product(
                s.normed, s.normed_in, right, right_in, s.me * DH, pl.ds(start, size), pl.ds(across, EH)
            )
            first += size

    def carry_on(events):
        for index, step in events:
            units[index].carry_on(step)

    def first_sums():
        swaps[1].wait_recv()
        swaps[2].wait_recv()
        for color in range(3):
            grad_out(color)
            units[color].start()

    def second_sums():
        swaps[0].wait_recv()
        swaps[3].wait_recv()
        for color in range(3):
            grad_in(1, color, s.d_gate, s.d_gate_in)
            units[3 + color].start()

    def between(k):
        pl.when(k == FIRST)(first_sums)
        pl.when(k == SECOND)(second_sums)
        for when, events in DURING.items():
            if when < s.T // STEPS:
                pl.when(k == when)(functools.partial(carry_on, events))

    def phase(number, step):
        step(s)
        carry_on(DURING.get(number, ()))

    s.rows[pl.ds(at.gain, 1), :] = jnp.zeros((1, E), F32)
    backward_scan(s, between)
    phase(16, back_step)
    phase(17, back_proj)
    back_conv(s, 0, 6)
    swaps[4].start()
    back_conv(s, 6, 6)
    swaps[5].start()
    carry_on(DURING.get(18, ()))
    phase(19, back_in)
    for color in range(3):
        if color < 2:
            swaps[4 + color].wait_recv()
        grad_in(2, color, s.d_inner, s.d_inner_in)
        units[6 + color].start()
    carry_on(DURING.get(20, ()))
    back_norm(s)
    s.rows[pl.ds(at.gain, 1), pl.ds(0, DH)] = s.d_gain[:, pl.ds(0, DH)]
    s.rows[pl.ds(at.gain, 1), pl.ds(EH, DH)] = s.d_gain[:, pl.ds(DH, DH)]
    swaps[6].start()
    leaving = [pltpu.make_async_copy(s.input_grad, s.input_grad_to, s.local.at[5])]
    leaving[0].start()
    carry_on(DURING.get(21, ()))
    project_out(s)
    leaving.append(pltpu.make_async_copy(s.output, s.output_to, s.local.at[4]))
    leaving[1].start()
    carry_on(DURING.get(22, ()))
    swaps[6].wait_recv()
    total = s.rows.shape[0]
    s.acc_rows[...] = jnp.zeros(s.acc_rows.shape, BF16)
    for part in range(3):
        own = pl.ds(pl.multiple_of(s.me * EH + 256 * part, 128), 256)
        value = s.rows[:, own] + s.rows_in[:, pl.ds(256 * part, 256)]
        value = jnp.concatenate([value, jnp.zeros((160 - total, 256), F32)], axis=0)
        s.acc_rows[pl.ds(160 * part, 160), :] = value.astype(BF16)
    units[9].start()
    carry_on(AFTER)
    for copy in leaving:
        copy.wait()
    for copy in gathers + swaps:
        copy.wait_send()
    for unit in units:
        unit.finish()


def fused_layer(length, tokens, cotangent, gain, w_in, conv_w, conv_b, w_xt, w_dt, dt_bias, a_log, d_skip, w_out):
    z = sizes(tokens, jax.ShapeDtypeStruct((2 * w_out.shape[0], w_out.shape[1]), BF16), a_log, w_dt, w_xt, conv_w)
    T, D, E, N, R, J, K = (z[n] for n in "TDENRJK")
    DH, EH = D // 2, E // 2
    total = N + K + 4 + R + J
    names = ("length", "tok_own", "cot_own", "gain_own", "w_in_own", "conv_w", "conv_b", "w_xt_own", "w_dt_own", "dt_bias", "a_log", "d_skip", "w_out_own")
    outs = dict(
        output_to=((T, D), BF16), input_grad_to=((T, D), F32), out_to=((9 * 256, D), BF16), out_rows_to=((512, 256), BF16)
    )
    plan = scratch_plan(z)
    plan.update(
        w_in=((D, 2 * E), BF16), w_out=((E, D), BF16), w_xt=((J, E), BF16), w_dt=((R, E), BF16),
        pack=((N + K + 4, EH), F32), pack_in=((N + K + 4, EH), F32), w_dt_in=((R, EH), BF16), w_xt_in=((J, EH), BF16),
        normed=((T, D), BF16), gated=((T, E), BF16), d_branch=((T, D), BF16), d_inner=((T, E), BF16),
        d_gate=((T, E), BF16), rows=((total, E), F32), normed_in=((T, DH), BF16), d_branch_in=((T, D), BF16),
        gated_in=((T, EH), BF16), d_gate_in=((T, E), BF16), d_inner_in=((T, E), BF16), rows_in=((total, EH), F32),
        tok=((T, D), BF16), cot=((T, D), BF16), output=((T, D), BF16), input_grad=((T, D), F32),
        out=((9 * 256, D), BF16), out_rows=((512, 256), BF16),
        acc=((9 * 256, D), BF16), recv=((9 * 240, D), BF16), acc_rows=((512, 256), BF16), recv_rows=((480, 256), BF16),
    )
    sems = GATHERS + SWAPS + COPIES * 10
    names = list(names) + list(outs) + list(plan) + ["local", "send", "recv_sem"]
    specs = [SMEM] + [VMEM] * 12
    specs[1] = specs[2] = specs[4] = specs[12] = ANY
    return pl.pallas_call(
        functools.partial(fused_kernel, z, names),
        out_shape=[jax.ShapeDtypeStruct(*spec) for spec in outs.values()],
        in_specs=specs,
        out_specs=[ANY] * len(outs),
        scratch_shapes=[pltpu.VMEM(*spec) for spec in plan.values()]
        + [pltpu.SemaphoreType.DMA((16,)), pltpu.SemaphoreType.DMA((sems,)), pltpu.SemaphoreType.DMA((sems,))],
        compiler_params=pltpu.CompilerParams(collective_id=0, has_side_effects=True, vmem_limit_bytes=63 * MB),
        name="layer",
    )(length, tokens, cotangent, gain, w_in, conv_w, conv_b, w_xt, w_dt, dt_bias, a_log, d_skip, w_out)


def finish_kernel(N, K, R, J, *refs):
    out, out_rows, output_in, input_grad_in, output, input_grad = refs[:6]
    targets = refs[6:16]
    g_in, g_out = targets[1], targets[9]
    low, wide, rows_low, kept, kept_wide, *small = refs[16:29]
    sem_in, sem_out = refs[29:]
    g_gain, g_conv_w, g_conv_b, g_xt, g_dt, g_dt_bias, g_a_log, g_skip = small
    DH, D = g_in.shape[0], out.shape[1]
    count = out.shape[0] // DH
    reads, writes = [], []

    def through(source, held, held_out, target):
        index = len(reads)
        reads.append(pltpu.make_async_copy(source, held, sem_in.at[index]))
        writes.append(pltpu.make_async_copy(held_out, target, sem_out.at[index]))

    for index in range(count):
        rows = pl.ds(index * DH, DH)
        unit, half = index // 2, index % 2
        if unit == 0:
            target = g_out.at[pl.ds(half * DH, DH), :]
        else:
            target = g_in.at[:, pl.ds(((2 - unit) * 2 + half) * D, D)]
        through(out.at[rows, :], low.at[rows, :], wide.at[rows, :], target)
    through(input_grad_in, kept_wide, kept_wide, input_grad)
    through(output_in, kept, kept, output)
    read_rows = pltpu.make_async_copy(out_rows, rows_low, sem_in.at[count + 2])
    read_rows.start()
    for copy in reads:
        copy.start()
    read_rows.wait()
    M = N + K + 4
    for part in range(3):
        value = rows_low[pl.ds(160 * part, 160), :].astype(F32)
        cols = pl.ds(256 * part, 256)
        g_a_log[:, cols] = value[:N]
        g_conv_w[:, cols] = value[N : N + K]
        g_conv_b[cols] = value[N + K]
        g_dt_bias[cols] = value[N + K + 1]
        g_skip[cols] = value[N + K + 2]
        if part == 0:
            g_gain[pl.ds(0, 256)] = value[N + K + 3]
        elif part == 1:
            g_gain[pl.ds(256, DH - 256)] = value[N + K + 3, : DH - 256]
        g_dt[:, cols] = value[M : M + R]
        g_xt[:, cols] = value[M + R : M + R + J]
    for index, held in enumerate(small):
        target = targets[(0, 2, 3, 4, 5, 6, 7, 8)[index]]
        writes.append(pltpu.make_async_copy(held, target, sem_out.at[count + 2 + index]))
        writes[-1].start()
    for index in range(count + 2):
        reads[index].wait()
        if index < count:
            rows = pl.ds(index * DH, DH)
            wide[rows, :] = low[rows, :].astype(F32)
        writes[index].start()
    for copy in writes:
        copy.wait()


def fused_body(tokens, lengths, cotangent, *shards):
    shards = list(shards)
    shards[4] = shards[4].T
    output, input_grad, out, out_rows = fused_layer(lengths, tokens[0], cotangent[0], *shards)
    gain, w_in, conv_w, conv_b, w_xt, w_dt, dt_bias, a_log, d_skip, w_out = shards
    kept = [out, jax.ShapeDtypeStruct(out.shape, F32), out_rows, output, input_grad]
    grads = [jax.ShapeDtypeStruct(w.shape, F32) for w in shards]
    small = [g for i, g in enumerate(grads) if i not in (1, 9)]
    results = pl.pallas_call(
        functools.partial(finish_kernel, a_log.shape[0], conv_w.shape[0], w_dt.shape[0], w_xt.shape[0]),
        out_shape=[jax.ShapeDtypeStruct(x.shape, x.dtype) for x in (output, input_grad)] + grads,
        in_specs=[ANY] * 4,
        out_specs=[ANY] * 12,
        scratch_shapes=[pltpu.VMEM(x.shape, x.dtype) for x in kept + small]
        + [pltpu.SemaphoreType.DMA((16,)), pltpu.SemaphoreType.DMA((24,))],
        compiler_params=pltpu.CompilerParams(vmem_limit_bytes=60 * MB),
        name="finish",
    )(out, out_rows, output, input_grad)
    output, input_grad, *grads = results
    grads[4] = grads[4].T
    return (output[None], input_grad[None], *grads)


def solution(mesh):
    seq, row, col, one = P(("dp", "fsdp"), None, None), P("fsdp", None), P(None, "fsdp"), P("fsdp")
    fused = mesh.shape["dp"] == PIECES and mesh.shape["fsdp"] == 2
    return jax.shard_map(
        fused_body if fused else plain_body,
        mesh=mesh,
        in_specs=(seq, P(("dp", "fsdp")), seq, one, row, col, one, row, col, one, col, one, row),
        out_specs=(seq, seq, one, row, col, one, row, col, one, col, one, row),
        check_vma=False,
    )
```

```python
import functools
import types

import jax
import jax.numpy as jnp
from jax import lax
from jax.experimental import pallas as pl
from jax.experimental.pallas import tpu as pltpu
from jax.sharding import PartitionSpec as P

F32 = jnp.float32
BF16 = jnp.bfloat16
EPS = 1e-05
STEPS = 16
CHUNK = 256
PAD = 8
LOG2E = 1.4426950408889634
MB = 2**20
VMEM = pl.BlockSpec(memory_space=pltpu.VMEM)
SMEM = pl.BlockSpec(memory_space=pltpu.SMEM)
ANY = pl.BlockSpec(memory_space=pl.ANY)
MESH = pl.DeviceIdType.MESH


def dot(left, right, over=(1, 0)):
    dims = (((over[0],), (over[1],)), ((), ()))
    return lax.dot_general(left, right, dims, preferred_element_type=F32)


def span(index, size):
    return pl.ds(pl.multiple_of(index * size, size), size)


def repeat(count, step, unroll=1):
    def run(index, carry):
        step(index)
        return carry

    lax.fori_loop(0, count, run, 0, unroll=min(unroll, count))


def row_plan(s):
    bias = s.N + s.K
    return types.SimpleNamespace(conv=s.N, bias=bias, dt_bias=bias + 1, skip=bias + 2, gain=bias + 3)


def start_norm(s):
    def run(block):
        rows = span(block, 64)
        x = s.tok[rows, :].astype(F32)
        scale = lax.rsqrt(jnp.mean(x * x, axis=1, keepdims=True) + EPS)
        s.inv[rows, :] = jnp.broadcast_to(scale, (64, 128))
        at = block * 64 + lax.broadcasted_iota(jnp.int32, (64, 1), 0)
        live = (at < s.length[0]).astype(F32)
        s.d_branch[rows, :] = (live * s.cot[rows, :].astype(F32)).astype(BF16)

    repeat(s.T // 64, run, 4)


def norm(s):
    def run(block):
        rows = span(block, 64)
        x = s.tok[rows, :].astype(F32)
        s.normed[rows, :] = (x * s.inv[rows, pl.ds(0, 1)] * s.gain[...]).astype(BF16)

    repeat(s.T // 64, run, 4)


def project_inner(s, first, count):
    at = row_plan(s)

    def run(index):
        cols = span(first + index, 256)
        s.inner[pl.ds(PAD, s.T), cols] = dot(s.normed[...], s.w_in[:, cols])

    repeat(count, run, 6)

    def convolve(index):
        cols = span(2 * first + index, 128)
        value = s.small[pl.ds(at.bias, 1), cols] + sum(
            s.small[pl.ds(at.conv + k, 1), cols] * s.inner[pl.ds(PAD - s.K + 1 + k, s.T), cols]
            for k in range(s.K)
        )
        sigma = jax.nn.sigmoid(value)
        s.active[:, cols] = (value * sigma).astype(BF16)
        s.cslope[:, cols] = sigma * (1.0 + value * (1.0 - sigma))

    repeat(2 * count, convolve, 4)


def project_gate(s, first, count):
    def run(index):
        cols = span(first + index, 256)
        source = pl.ds(pl.multiple_of(s.E + (first + index) * 256, 256), 256)
        value = dot(s.normed[...], s.w_in[:, source])
        sigma = jax.nn.sigmoid(value)
        s.gact[:, cols] = value * sigma
        s.gslope[:, cols] = sigma * (1.0 + value * (1.0 - sigma))

    repeat(count, run, 6)


def diagonal(s):
    wide = STEPS * s.N
    at = lax.broadcasted_iota(jnp.int32, (s.T, wide), 0)
    to = lax.broadcasted_iota(jnp.int32, (s.T, wide), 1)
    return (at % STEPS == to // s.N).astype(F32)


def spread_rows(s):
    N, J, wide = s.N, s.J, STEPS * s.N
    state = lax.broadcasted_iota(jnp.int32, (N, J), 0)
    col = lax.broadcasted_iota(jnp.int32, (N, J), 1)
    mask = jnp.logical_or(col == s.R + state, col == s.R + N + state).astype(F32)
    row = lax.broadcasted_iota(jnp.int32, (J, 256), 0)
    lane = lax.broadcasted_iota(jnp.int32, (J, 256), 1)
    first = jnp.logical_and(row < s.R + N, lane < 128)
    last = jnp.logical_and(row >= s.R + N, lane >= 128)
    ones = jnp.logical_or(first, last).astype(BF16)

    def run(block):
        rows = s.proj[span(block, STEPS), :].astype(F32)
        parts = [(jnp.broadcast_to(rows[i : i + 1], (N, J)) * mask).astype(BF16) for i in range(STEPS)]
        s.spread[span(block, wide), :] = dot(jnp.concatenate(parts, axis=0), ones)

    repeat(s.T // STEPS, run, 4)


def scan_inputs(s):
    wide = STEPS * s.N
    at = row_plan(s)
    s.proj[...] = dot(s.active[...], s.w_xt[...], (1, 1)).astype(BF16)
    row = lax.broadcasted_iota(jnp.int32, (s.J, wide), 0)
    col = lax.broadcasted_iota(jnp.int32, (s.J, wide), 1)
    mask = diagonal(s)
    pick_b = (row == s.R + col % s.N).astype(BF16)
    pick_c = (row == s.R + s.N + col % s.N).astype(BF16)
    s.bmat[...] = (dot(s.proj[...], pick_b) * mask).astype(BF16)
    s.cmat[...] = (dot(s.proj[...], pick_c) * mask).astype(BF16)
    spread_rows(s)

    def run(index):
        cols = span(index, 256)
        pre = dot(s.proj[:, : s.R], s.w_dt[:, cols]) + s.small[pl.ds(at.dt_bias, 1), cols]
        size = jnp.maximum(pre, 0.0) + jnp.log1p(jnp.exp(-jnp.abs(pre)))
        s.step[:, cols] = size
        s.sigp[:, cols] = jax.nn.sigmoid(pre)
        s.drive[:, cols] = size * s.active[:, cols].astype(F32)

    repeat(s.E // 256, run, 6)
    s.decay[...] = -jnp.exp(s.small[pl.ds(0, s.N), :]) * LOG2E


def forward_scan(s):
    N, E, wide = s.N, s.E, STEPS * s.N
    s.states[pl.ds(0, N), :] = jnp.zeros((N, E), BF16)

    def scan_sum(block):
        rows = span(block, STEPS)
        held = s.states[pl.ds(pl.multiple_of(block * wide + N, N), wide), :]
        s.mixed[rows, :] = dot(s.cmat[rows, :], held)

    def run(block, state):
        scan_sum(jnp.maximum(block - 1, 0))
        rows = span(block, STEPS)
        size, push = s.step[rows, :], s.drive[rows, :]
        for i in range(STEPS):
            t = block * STEPS + i
            b_row = s.spread[span(t, N), pl.ds(0, 128)]
            b_row = jnp.concatenate([b_row] * (E // 128), axis=1)
            factor = jnp.exp2(jnp.broadcast_to(size[i : i + 1], (N, E)) * s.decay[...])
            state = factor * state + b_row * jnp.broadcast_to(push[i : i + 1], (N, E))
            s.states[span(t + 1, N), :] = state.astype(BF16)
        return state

    lax.fori_loop(0, s.T // STEPS, run, jnp.zeros((N, E), F32))
    scan_sum(s.T // STEPS - 1)


def mix(s):
    at = row_plan(s)

    def run(index):
        cols = span(index, 128)
        value = s.mixed[pl.ds(0, s.T), cols] + s.small[pl.ds(at.skip, 1), cols] * s.active[:, cols].astype(F32)
        s.mixed[pl.ds(0, s.T), cols] = value
        s.gated[:, cols] = (value * s.gact[:, cols]).astype(BF16)

    repeat(s.E // 128, run, 2)


def back_out(s):
    at = row_plan(s)

    def run(index):
        cols = span(index, 256)
        d_gated = dot(s.d_branch[...], s.w_out[cols, :], (1, 1))
        d_value = d_gated * s.gact[:, cols]
        s.d_mixed[:, cols] = d_value
        s.d_gate[:, cols] = (d_gated * s.mixed[pl.ds(0, s.T), cols] * s.gslope[:, cols]).astype(BF16)
        s.rows[pl.ds(at.skip, 1), cols] = jnp.sum(
            d_value * s.active[:, cols].astype(F32), axis=0, keepdims=True
        )

    repeat(s.E // 256, run, 6)


def project_out(s):
    def run(index):
        cols = span(index, 256)
        branch = dot(s.gated[...], s.w_out[:, cols])
        at = lax.broadcasted_iota(jnp.int32, (s.T, 1), 0)
        live = (at < s.length[0]).astype(F32)
        s.output[:, cols] = (s.tok[:, cols].astype(F32) + live * branch).astype(BF16)

    repeat(s.D // 256, run, 3)


def backward_scan(s, between=None):
    N, E, wide, half = s.N, s.E, STEPS * s.N, s.N // 2
    blocks = s.T // STEPS
    s.carry[...] = jnp.zeros((N, E), F32)
    s.rows[pl.ds(0, N), :] = jnp.zeros((N, E), F32)
    at = lax.broadcasted_iota(jnp.int32, (STEPS, STEPS * half), 0)
    to = lax.broadcasted_iota(jnp.int32, (STEPS, STEPS * half), 1)
    gather = (at == to // half).astype(BF16)

    def run(k):
        block = blocks - 1 - k
        rows = span(block, STEPS)
        for chunk in range(E // CHUNK):
            cols = pl.ds(chunk * CHUNK, CHUNK)
            later, total = s.carry[:, cols], s.rows[pl.ds(0, N), cols]
            size, d_value = s.step[rows, cols], s.d_mixed[rows, cols]
            rate = s.decay[:, cols]
            for i in reversed(range(STEPS)):
                t = block * STEPS + i
                dt = jnp.broadcast_to(size[i : i + 1], (N, CHUNK))
                c_row = s.spread[span(t, N), pl.ds(128, 128)]
                c_row = jnp.concatenate([c_row] * (CHUNK // 128), axis=1)
                lam = c_row * jnp.broadcast_to(d_value[i : i + 1], (N, CHUNK)) + later
                s.lam[pl.ds(i * N, N), cols] = lam.astype(BF16)
                later = jnp.exp2(dt * rate) * lam
                weighted = later * s.states[span(t, N), cols].astype(F32)
                total = total + weighted * dt
                part = weighted * rate
                part = part[:half] + part[half:]
                if i % 2 == 1:
                    odd = part
                else:
                    s.part[pl.ds(i * half, N), cols] = jnp.concatenate([part, odd], axis=0).astype(BF16)
            s.carry[:, cols] = later
            s.rows[pl.ds(0, N), cols] = total
            held = s.lam[:, cols]
            s.gact[rows, cols] = dot(s.bmat[rows, :], held)
            s.gslope[rows, cols] = dot(gather, s.part[:, cols])
            b_part = dot(s.drive[rows, cols].astype(BF16), held, (1, 1))
            after = s.states[pl.ds(pl.multiple_of(block * wide + N, N), wide), cols]
            c_part = dot(d_value.astype(BF16), after, (1, 1))
            if chunk == 0:
                s.db[rows, :] = b_part
                s.dc[rows, :] = c_part
            else:
                s.db[rows, :] += b_part
                s.dc[rows, :] += c_part
        if between is not None:
            between(k)

    repeat(blocks, run)
    s.rows[pl.ds(0, N), :] = s.rows[pl.ds(0, N), :] * s.decay[...] * (1.0 / LOG2E)


def back_step(s):
    at = row_plan(s)

    def run(index):
        cols = span(index, 128)
        wide = s.active[:, cols].astype(F32)
        adjoint = s.gact[:, cols]
        d_pre = (wide * adjoint + s.gslope[:, cols] * (1.0 / LOG2E)) * s.sigp[:, cols]
        s.rows[pl.ds(at.dt_bias, 1), cols] = jnp.sum(d_pre, axis=0, keepdims=True)
        s.lam[:, cols] = d_pre.astype(BF16)
        s.d_mixed[:, cols] = (
            s.d_mixed[:, cols] * s.small[pl.ds(at.skip, 1), cols] + s.step[:, cols] * adjoint
        )

    repeat(s.E // 128, run)


def back_proj(s):
    wide = STEPS * s.N
    row = lax.broadcasted_iota(jnp.int32, (wide, s.N), 0)
    col = lax.broadcasted_iota(jnp.int32, (wide, s.N), 1)
    pick = (row % s.N == col).astype(BF16)
    mask = diagonal(s)
    s.d_proj[:, pl.ds(0, s.R)] = dot(s.lam[...], s.w_dt[...], (1, 1)).astype(BF16)
    s.d_proj[:, pl.ds(s.R, s.N)] = dot((s.db[...] * mask).astype(BF16), pick).astype(BF16)
    s.d_proj[:, pl.ds(s.R + s.N, s.N)] = dot((s.dc[...] * mask).astype(BF16), pick).astype(BF16)


def back_conv(s, part, count):
    at = row_plan(s)
    s.mixed[pl.ds(s.T, PAD), :] = jnp.zeros((PAD, s.E), F32)
    first = at.gain + 1

    def run(index):
        cols = span(part + index, 128)
        s.rows[pl.ds(first, s.R), cols] = dot(s.proj[:, : s.R], s.lam[:, cols], (0, 0))
        s.rows[pl.ds(first + s.R, s.J), cols] = dot(s.d_proj[...], s.active[:, cols], (0, 0))
        d_active = s.d_mixed[:, cols] + dot(s.d_proj[...], s.w_xt[:, cols])
        d_value = d_active * s.cslope[:, cols]
        s.mixed[pl.ds(0, s.T), cols] = d_value
        s.rows[pl.ds(at.bias, 1), cols] = jnp.sum(d_value, axis=0, keepdims=True)
        total = jnp.zeros_like(d_value)
        for k in range(s.K):
            s.rows[pl.ds(at.conv + k, 1), cols] = jnp.sum(
                d_value * s.inner[pl.ds(PAD - s.K + 1 + k, s.T), cols], axis=0, keepdims=True
            )
            taps = s.small[pl.ds(at.conv + k, 1), cols]
            total = total + taps * s.mixed[pl.ds(s.K - 1 - k, s.T), cols]
        s.d_inner[:, cols] = total.astype(BF16)

    repeat(count, run, 3)


def back_in(s):
    def run(index):
        rows = span(index, 256)
        s.step[:, rows] = dot(s.d_inner[...], s.w_in[rows, pl.ds(0, s.E)], (1, 1)) + dot(
            s.d_gate[...], s.w_in[rows, pl.ds(s.E, s.E)], (1, 1)
        )

    repeat(s.D // 256, run, 3)


def back_norm(s):
    s.d_gain[...] = jnp.zeros((1, s.D), F32)

    def run(block):
        rows = span(block, 64)
        x = s.tok[rows, :].astype(F32)
        scale = s.inv[rows, pl.ds(0, 1)]
        d_value = s.step[rows, pl.ds(0, s.D)]
        s.d_gain[...] += jnp.sum(d_value * x * scale, axis=0, keepdims=True)
        d_scaled = d_value * s.gain[...]
        shared = jnp.mean(d_scaled * x, axis=1, keepdims=True)
        s.input_grad[rows, :] = (
            s.cot[rows, :].astype(F32) + scale * d_scaled - x * (scale * scale * scale) * shared
        )

    repeat(s.T // 64, run, 4)


def sizes(tokens, w_out, a_log, w_dt, w_xt, conv_w):
    return dict(
        T=tokens.shape[0], D=tokens.shape[1], E=w_out.shape[0], N=a_log.shape[0],
        R=w_dt.shape[0], J=w_xt.shape[0], K=conv_w.shape[0],
    )


def scratch_plan(z):
    T, D, E, N, R, J, K = (z[n] for n in "TDENRJK")
    wide = STEPS * N
    full, low = ((T, E), F32), ((T, E), BF16)
    padded = ((T + PAD, E), F32)
    count = N + K + 4
    return dict(
        inv=((T, 128), F32), gain=((1, D), F32), small=((count, E), F32), inner=padded, gact=full, gslope=full,
        cslope=full, active=low, proj=((T, J), BF16), bmat=((T, wide), BF16), cmat=((T, wide), BF16),
        spread=((T * N, 256), F32), decay=((N, E), F32), step=full, sigp=full, drive=full,
        mixed=padded, d_mixed=full, states=(((T + 1) * N, E), BF16), carry=((N, E), F32),
        lam=((wide, E), BF16), part=((wide // 2, E), BF16), db=((T, wide), F32), dc=((T, wide), F32),
        d_proj=((T, J), BF16), d_gain=((1, D), F32),
    )


def plain_kernel(z, names, *refs):
    s = types.SimpleNamespace(**z, **dict(zip(names, refs)))
    at = row_plan(s)
    s.small[pl.ds(0, s.N), :] = s.a_log[...].astype(F32)
    s.small[pl.ds(at.conv, s.K), :] = s.conv_w[...].astype(F32)
    s.small[pl.ds(at.bias, 1), :] = s.conv_b[...].astype(F32)
    s.small[pl.ds(at.dt_bias, 1), :] = s.dt_bias[...].astype(F32)
    s.small[pl.ds(at.skip, 1), :] = s.d_skip[...].astype(F32)
    s.gain[...] = s.gain_in[...].astype(F32)
    s.rows[...] = jnp.zeros(s.rows.shape, F32)
    s.inner[pl.ds(0, PAD), :] = jnp.zeros((PAD, s.E), F32)
    for step in (start_norm, norm):
        step(s)
    project_inner(s, 0, s.E // 256)
    project_gate(s, 0, s.E // 256)
    for step in (scan_inputs, forward_scan, mix, project_out, back_out):
        step(s)
    backward_scan(s)
    back_step(s)
    back_proj(s)
    back_conv(s, 0, s.E // 128)
    back_in(s)
    back_norm(s)
    s.g_gain[...] = s.d_gain[...]


def plain_layer(length, tokens, cotangent, gain, w_in, conv_w, conv_b, w_xt, w_dt, dt_bias, a_log, d_skip, w_out):
    z = sizes(tokens, w_out, a_log, w_dt, w_xt, conv_w)
    T, D, E, N, R, J, K = (z[n] for n in "TDENRJK")
    plan = scratch_plan(z)
    ins = ("length", "tok", "cot", "gain_in", "w_in", "conv_w", "conv_b", "w_xt", "w_dt", "dt_bias", "a_log", "d_skip", "w_out")
    outs = dict(
        output=((T, D), BF16), input_grad=((T, D), F32), normed=((T, D), BF16), gated=((T, E), BF16),
        d_branch=((T, D), BF16), d_inner=((T, E), BF16), d_gate=((T, E), BF16), g_gain=((1, D), F32),
        rows=((N + K + 4 + R + J, E), F32),
    )
    names = list(ins) + list(outs) + list(plan)
    return pl.pallas_call(
        functools.partial(plain_kernel, z, names),
        out_shape=[jax.ShapeDtypeStruct(*spec) for spec in outs.values()],
        in_specs=[SMEM] + [VMEM] * 12,
        out_specs=[VMEM] * len(outs),
        scratch_shapes=[pltpu.VMEM(*spec) for spec in plan.values()],
        compiler_params=pltpu.CompilerParams(vmem_limit_bytes=60 * MB),
        name="plain_layer",
    )(length, tokens, cotangent, gain, w_in, conv_w, conv_b, w_xt, w_dt, dt_bias, a_log, d_skip, w_out)


def plain_body(tokens, lengths, cotangent, *shards):
    axes = (0, 0, 1, 0, 0, 1, 0, 1, 0, 0)
    weights = [lax.all_gather(w, "fsdp", axis=a, tiled=True) for w, a in zip(shards, axes)]
    weights = [w.reshape(1, -1) if w.ndim == 1 else w for w in weights]
    weights[4] = weights[4].T
    output, input_grad, normed, gated, d_branch, d_inner, d_gate, g_gain, rows = plain_layer(
        lengths, tokens[0], cotangent[0], *weights
    )
    big_in = dot(normed, jnp.concatenate([d_inner, d_gate], axis=1), (0, 0))
    big_out = dot(gated, d_branch, (0, 0))

    def scatter(value, axis):
        return lax.psum_scatter(value, "fsdp", scatter_dimension=axis, tiled=True)

    own = (
        scatter(big_in.astype(BF16), 0), scatter(big_out.astype(BF16), 0),
        scatter(rows, 1), scatter(g_gain[0], 0),
    )
    own_in, own_out, rows, own_gain = lax.psum(own, "dp")
    N, K, R = shards[7].shape[0], shards[2].shape[0], shards[5].shape[0]
    M = N + K + 4
    return (
        output[None], input_grad[None], own_gain, own_in.astype(F32), rows[N : N + K], rows[N + K],
        rows[M + R :].T, rows[M : M + R], rows[N + K + 1], rows[:N], rows[N + K + 2], own_out.astype(F32),
    )


ORDERS = (
    ((2,), (0,), (3,), (1,)),
    ((0, 1), (2, 3)),
    ((1,), (0,), (2, 3)),
    ((1,), (0,), (2, 3)),
    ((2,), (1,), (0,), (3,)),
    ((0,), (1,), (2, 3)),
    ((0,), (1,), (2, 3)),
    ((1,), (0,), (2, 3)),
    ((2,), (0, 1), (3,)),
    ((0, 1), (3,), (2,)),
)
DURING = {
    6: ((0, 0), (1, 0)),
    9: ((4, 0),),
    10: ((2, 0), (5, 0)),
    11: ((1, 1), (0, 1)),
    13: ((3, 0),),
    14: ((2, 1),),
    15: ((4, 1), (1, 2)),
    16: ((5, 1), (0, 2), (3, 1)),
    18: ((4, 2), (2, 2)),
    19: ((5, 2), (0, 3), (1, 3)),
    20: ((3, 2),),
    21: ((4, 3),),
}
AFTER = (
    (0, 4), (2, 3), (6, 0), (5, 3), (7, 0), (8, 0), (9, 0), (3, 3), (2, 4), (4, 4), (6, 1), (7, 1),
    (0, 5), (5, 4), (9, 1), (8, 1), (3, 4), (6, 2), (4, 5), (9, 2), (7, 2), (8, 2), (0, 6), (2, 5),
    (9, 3), (6, 3), (5, 5), (7, 3), (3, 5), (8, 3), (4, 6), (7, 4), (0, 7), (6, 4), (9, 4), (8, 4),
    (4, 7), (6, 5), (7, 5), (8, 5), (9, 5),
)
PIECES = 16
FIRST, SECOND = 0, 2
GATHERS = 10
SWAPS = 7
COPIES = 12


def packed_rows(s):
    return s.N + s.K + 4


class Sum:
    def __init__(self, s, number, stages, acc, recv, out, result, first, piece):
        self.s, self.stages, self.piece, self.steps = s, stages, piece, 2 * len(stages)
        self.sem = GATHERS + SWAPS + COPIES * number
        self.acc, self.recv, self.out = acc, recv, out
        self.first, self.landed = first * PIECES * piece, first * (PIECES - 1) * piece
        self.bits = [[lax.rem(s.dp // 2**b, 2) for b in stage] for stage in stages]
        whole = pl.ds(self.first, PIECES * piece)
        self.leave = pltpu.make_async_copy(out.at[whole, :], result.at[whole, :], s.local.at[6 + number])
        self.plan = []
        start, count, landing, sem = 0, PIECES, 0, self.sem
        for stage, bits in zip(stages, self.bits):
            group = 2 ** len(stage)
            count //= group
            others = []
            for flip in range(1, group):
                device, place = s.dp, 0
                for j, (b, bit) in enumerate(zip(stage, bits)):
                    flipped = flip // 2**j % 2
                    device = device + flipped * (1 - 2 * bit) * 2**b
                    place = place + (flipped + (1 - 2 * flipped) * bit) * 2**j
                others.append(((device, s.me), start + place * count, landing, sem))
                landing, sem = landing + count, sem + 2
            for j, bit in enumerate(bits):
                start = start + bit * 2**j * count
            self.plan.append((others, start, count))

    def rows(self, start, count):
        return pl.ds(pl.multiple_of(self.first + start * self.piece, 16), count * self.piece)

    def reduce_copies(self, level):
        others, _, count = self.plan[level]
        return [
            self.s.remote(
                self.acc.at[self.rows(theirs, count), :],
                self.recv.at[pl.ds(self.landed + landing * self.piece, count * self.piece), :], sem, device,
            )
            for device, theirs, landing, sem in others
        ]

    def spread_copies(self, level, sent=True):
        others, mine, count = self.plan[level]
        copies = []
        for device, theirs, _, sem in others:
            rows = self.rows(mine if sent else theirs, count)
            copies.append(self.s.remote(self.out.at[rows, :], self.out.at[rows, :], sem + 1, device))
        return copies

    def start(self):
        for copy in self.reduce_copies(0):
            copy.start()

    def carry_on(self, step):
        levels = len(self.stages)
        if step < levels:
            self.reduce(step)
            following = self.spread_copies(step) if step == levels - 1 else self.reduce_copies(step + 1)
        else:
            level = self.steps - 1 - step
            for copy in self.spread_copies(level, False):
                copy.wait_recv()
            following = self.spread_copies(level - 1) if level > 0 else [self.leave]
        for copy in following:
            copy.start()

    def reduce(self, level):
        for copy in self.reduce_copies(level):
            copy.wait_recv()
        others, mine, count = self.plan[level]
        target = self.out if level == len(self.stages) - 1 else self.acc

        def add(index):
            here = self.rows(mine + index, 1)
            total = self.acc[here, :].astype(F32)
            for _, _, landing, _ in others:
                there = pl.ds(pl.multiple_of(self.landed + (landing + index) * self.piece, 16), self.piece)
                total = total + self.recv[there, :].astype(F32)
            target[here, :] = total.astype(BF16)

        repeat(count, add)

    def finish(self):
        for level in range(len(self.stages)):
            for copy in self.reduce_copies(level) + self.spread_copies(level):
                copy.wait_send()
        self.leave.wait()


def fused_kernel(z, names, *refs):
    s = types.SimpleNamespace(**z, **dict(zip(names, refs)))
    D, E = s.D, s.E
    DH, EH = D // 2, E // 2
    at = row_plan(s)
    count = packed_rows(s)
    s.dp, s.me = lax.axis_index("dp"), lax.axis_index("fsdp")
    other = 1 - s.me
    peer = (s.dp, other)

    def remote(src, dst, sem, device):
        return pltpu.make_async_remote_copy(
            src_ref=src, dst_ref=dst, send_sem=s.send.at[sem], recv_sem=s.recv_sem.at[sem],
            device_id=device, device_id_type=MESH,
        )

    s.remote = remote
    units = [Sum(s, i, ORDERS[i], s.acc, s.recv, s.out, s.out_to, i, 16) for i in range(9)]
    units.append(Sum(s, 9, ORDERS[9], s.acc_rows, s.recv_rows, s.out_rows, s.out_rows_to, 0, 32))

    barrier = pltpu.get_barrier_semaphore()
    pl.semaphore_signal(barrier, inc=1, device_id=peer, device_id_type=MESH)
    partners = {}
    for unit in units:
        for stage, (others, _, _) in zip(unit.stages, unit.plan):
            for flip, other_one in enumerate(others):
                partners[(stage, flip)] = other_one[0]
    greeted = {}
    for (stage, flip), device in partners.items():
        greeted[tuple(sorted(b for j, b in enumerate(stage) if (flip + 1) // 2**j % 2))] = device
    for device in greeted.values():
        pl.semaphore_signal(barrier, inc=1, device_id=device, device_id_type=MESH)

    mine_d, mine_e = span(s.me, DH), span(s.me, EH)
    theirs_d, theirs_e = span(other, DH), span(other, EH)
    local_in = pltpu.make_async_copy(s.w_in_own, s.w_in.at[mine_d, :], s.local.at[0])
    local_out = pltpu.make_async_copy(s.w_out_own, s.w_out.at[mine_e, :], s.local.at[1])
    local_tok = pltpu.make_async_copy(s.tok_own, s.tok, s.local.at[2])
    local_cot = pltpu.make_async_copy(s.cot_own, s.cot, s.local.at[3])
    for copy in (local_tok, local_cot, local_in, local_out):
        copy.start()
    s.pack[pl.ds(0, s.N), :] = s.a_log[...].astype(F32)
    s.pack[pl.ds(at.conv, s.K), :] = s.conv_w[...].astype(F32)
    s.pack[pl.ds(at.bias, 1), :] = s.conv_b[...].astype(F32)[None, :]
    s.pack[pl.ds(at.dt_bias, 1), :] = s.dt_bias[...].astype(F32)[None, :]
    s.pack[pl.ds(at.skip, 1), :] = s.d_skip[...].astype(F32)[None, :]
    s.pack[pl.ds(at.gain, 1), :] = jnp.zeros((1, EH), F32)
    s.pack[pl.ds(at.gain, 1), pl.ds(0, DH)] = s.gain_own[...].astype(F32)[None, :]
    pl.semaphore_wait(barrier, len(greeted) + 1)

    width = 2 * E // 6
    gathers = [remote(s.pack, s.pack_in, 0, peer)]
    for j in range(6):
        cols = pl.ds(j * width, width)
        gathers.append(remote(s.w_in_own.at[:, cols], s.w_in.at[mine_d, cols], 1 + j, peer))
    gathers.append(remote(s.w_xt_own, s.w_xt_in, 7, peer))
    gathers.append(remote(s.w_dt_own, s.w_dt_in, 8, peer))
    gathers.append(remote(s.w_out_own, s.w_out.at[mine_e, :], 9, peer))
    for j in (0, 1, 2, 3, 7, 8, 4, 5, 6, 9):
        gathers[j].start()

    swaps = [
        remote(s.normed.at[:, theirs_d], s.normed_in, GATHERS, peer),
        remote(s.d_branch, s.d_branch_in, GATHERS + 1, peer),
        remote(s.gated.at[:, theirs_e], s.gated_in, GATHERS + 2, peer),
        remote(s.d_gate, s.d_gate_in, GATHERS + 3, peer),
        remote(s.d_inner.at[:, pl.ds(0, EH)], s.d_inner_in.at[:, pl.ds(0, EH)], GATHERS + 4, peer),
        remote(s.d_inner.at[:, pl.ds(EH, EH)], s.d_inner_in.at[:, pl.ds(EH, EH)], GATHERS + 5, peer),
        remote(s.rows.at[:, theirs_e], s.rows_in, GATHERS + 6, peer),
    ]

    local_tok.wait()
    local_cot.wait()
    start_norm(s)
    swaps[1].start()
    s.w_xt[:, mine_e] = s.w_xt_own[...]
    s.w_dt[:, mine_e] = s.w_dt_own[...]
    s.small[:, mine_e] = s.pack[...]
    s.gain[:, mine_d] = s.pack[pl.ds(at.gain, 1), pl.ds(0, DH)]
    s.inner[pl.ds(0, PAD), :] = jnp.zeros((PAD, E), F32)
    gathers[0].wait_recv()
    s.small[:, theirs_e] = s.pack_in[...]
    s.gain[:, theirs_d] = s.pack_in[pl.ds(at.gain, 1), pl.ds(0, DH)]
    norm(s)
    swaps[0].start()
    local_in.wait()
    for j in range(3):
        gathers[1 + j].wait_recv()
        project_inner(s, 2 * j, 2)
    gathers[7].wait_recv()
    gathers[8].wait_recv()
    s.w_dt[:, theirs_e] = s.w_dt_in[...]
    s.w_xt[:, theirs_e] = s.w_xt_in[...]
    scan_inputs(s)
    for j in range(3):
        gathers[4 + j].wait_recv()
        project_gate(s, 2 * j, 2)
    forward_scan(s)
    mix(s)
    swaps[2].start()
    local_out.wait()
    gathers[9].wait_recv()
    back_out(s)
    swaps[3].start()
    def product(left, left_in, right, right_in, shift, cols, across):
        own = pl.ds(pl.multiple_of(shift + cols.start, 128), cols.size)
        total = dot(left[:, own], right[:, across], (0, 0)) + dot(left_in[:, cols], right_in[:, across], (0, 0))
        return total.astype(BF16)

    def grad_out(color):
        cols = pl.ds(256 * color, 256)
        s.acc[pl.ds(256 * color, 256), :] = product(
            s.gated, s.gated_in, s.d_branch, s.d_branch_in, s.me * EH, cols, pl.ds(0, D)
        )

    def grad_in(unit, color, right, right_in):
        first = 256 * (3 * unit + color)
        parts = (((0, 256, 0),), ((256, 128, 0), (0, 128, EH)), ((128, 256, EH),))[color]
        for start, size, across in parts:
            s.acc[pl.ds(first, size), :] = product(
                s.normed, s.normed_in, right, right_in, s.me * DH, pl.ds(start, size), pl.ds(across, EH)
            )
            first += size

    def carry_on(events):
        for index, step in events:
            units[index].carry_on(step)

    def first_sums():
        swaps[1].wait_recv()
        swaps[2].wait_recv()
        for color in range(3):
            grad_out(color)
            units[color].start()

    def second_sums():
        swaps[0].wait_recv()
        swaps[3].wait_recv()
        for color in range(3):
            grad_in(1, color, s.d_gate, s.d_gate_in)
            units[3 + color].start()

    def between(k):
        pl.when(k == FIRST)(first_sums)
        pl.when(k == SECOND)(second_sums)
        for when, events in DURING.items():
            if when < s.T // STEPS:
                pl.when(k == when)(functools.partial(carry_on, events))

    def phase(number, step):
        step(s)
        carry_on(DURING.get(number, ()))

    s.rows[pl.ds(at.gain, 1), :] = jnp.zeros((1, E), F32)
    backward_scan(s, between)
    phase(16, back_step)
    phase(17, back_proj)
    back_conv(s, 0, 6)
    swaps[4].start()
    back_conv(s, 6, 6)
    swaps[5].start()
    carry_on(DURING.get(18, ()))
    for color in range(3):
        if color < 2:
            swaps[4 + color].wait_recv()
        grad_in(2, color, s.d_inner, s.d_inner_in)
        units[6 + color].start()
        if color == 0:
            phase(19, back_in)
    carry_on(DURING.get(20, ()))
    back_norm(s)
    s.rows[pl.ds(at.gain, 1), pl.ds(0, DH)] = s.d_gain[:, pl.ds(0, DH)]
    s.rows[pl.ds(at.gain, 1), pl.ds(EH, DH)] = s.d_gain[:, pl.ds(DH, DH)]
    swaps[6].start()
    leaving = [pltpu.make_async_copy(s.input_grad, s.input_grad_to, s.local.at[5])]
    leaving[0].start()
    carry_on(DURING.get(21, ()))
    project_out(s)
    leaving.append(pltpu.make_async_copy(s.output, s.output_to, s.local.at[4]))
    leaving[1].start()
    carry_on(DURING.get(22, ()))
    swaps[6].wait_recv()
    total = s.rows.shape[0]
    s.acc_rows[...] = jnp.zeros(s.acc_rows.shape, BF16)
    for part in range(3):
        own = pl.ds(pl.multiple_of(s.me * EH + 256 * part, 128), 256)
        value = s.rows[:, own] + s.rows_in[:, pl.ds(256 * part, 256)]
        value = jnp.concatenate([value, jnp.zeros((160 - total, 256), F32)], axis=0)
        s.acc_rows[pl.ds(160 * part, 160), :] = value.astype(BF16)
    units[9].start()
    carry_on(AFTER)
    for copy in leaving:
        copy.wait()
    for copy in gathers + swaps:
        copy.wait_send()
    for unit in units:
        unit.finish()


def fused_layer(length, tokens, cotangent, gain, w_in, conv_w, conv_b, w_xt, w_dt, dt_bias, a_log, d_skip, w_out):
    z = sizes(tokens, jax.ShapeDtypeStruct((2 * w_out.shape[0], w_out.shape[1]), BF16), a_log, w_dt, w_xt, conv_w)
    T, D, E, N, R, J, K = (z[n] for n in "TDENRJK")
    DH, EH = D // 2, E // 2
    total = N + K + 4 + R + J
    names = ("length", "tok_own", "cot_own", "gain_own", "w_in_own", "conv_w", "conv_b", "w_xt_own", "w_dt_own", "dt_bias", "a_log", "d_skip", "w_out_own")
    outs = dict(
        output_to=((T, D), BF16), input_grad_to=((T, D), F32), out_to=((9 * 256, D), BF16), out_rows_to=((512, 256), BF16)
    )
    plan = scratch_plan(z)
    plan.update(
        w_in=((D, 2 * E), BF16), w_out=((E, D), BF16), w_xt=((J, E), BF16), w_dt=((R, E), BF16),
        pack=((N + K + 4, EH), F32), pack_in=((N + K + 4, EH), F32), w_dt_in=((R, EH), BF16), w_xt_in=((J, EH), BF16),
        normed=((T, D), BF16), gated=((T, E), BF16), d_branch=((T, D), BF16), d_inner=((T, E), BF16),
        d_gate=((T, E), BF16), rows=((total, E), F32), normed_in=((T, DH), BF16), d_branch_in=((T, D), BF16),
        gated_in=((T, EH), BF16), d_gate_in=((T, E), BF16), d_inner_in=((T, E), BF16), rows_in=((total, EH), F32),
        tok=((T, D), BF16), cot=((T, D), BF16), output=((T, D), BF16), input_grad=((T, D), F32),
        out=((9 * 256, D), BF16), out_rows=((512, 256), BF16),
        acc=((9 * 256, D), BF16), recv=((9 * 240, D), BF16), acc_rows=((512, 256), BF16), recv_rows=((480, 256), BF16),
    )
    sems = GATHERS + SWAPS + COPIES * 10
    names = list(names) + list(outs) + list(plan) + ["local", "send", "recv_sem"]
    specs = [SMEM] + [VMEM] * 12
    specs[1] = specs[2] = specs[4] = specs[12] = ANY
    return pl.pallas_call(
        functools.partial(fused_kernel, z, names),
        out_shape=[jax.ShapeDtypeStruct(*spec) for spec in outs.values()],
        in_specs=specs,
        out_specs=[ANY] * len(outs),
        scratch_shapes=[pltpu.VMEM(*spec) for spec in plan.values()]
        + [pltpu.SemaphoreType.DMA((16,)), pltpu.SemaphoreType.DMA((sems,)), pltpu.SemaphoreType.DMA((sems,))],
        compiler_params=pltpu.CompilerParams(collective_id=0, has_side_effects=True, vmem_limit_bytes=63 * MB),
        name="layer",
    )(length, tokens, cotangent, gain, w_in, conv_w, conv_b, w_xt, w_dt, dt_bias, a_log, d_skip, w_out)


def finish_kernel(N, K, R, J, *refs):
    out, out_rows, output_in, input_grad_in, output, input_grad = refs[:6]
    targets = refs[6:16]
    g_in, g_out = targets[1], targets[9]
    low, wide, rows_low, kept, kept_wide, *small = refs[16:29]
    sem_in, sem_out = refs[29:]
    g_gain, g_conv_w, g_conv_b, g_xt, g_dt, g_dt_bias, g_a_log, g_skip = small
    DH, D = g_in.shape[0], out.shape[1]
    count = out.shape[0] // DH
    reads, writes = [], []

    def through(source, held, held_out, target):
        index = len(reads)
        reads.append(pltpu.make_async_copy(source, held, sem_in.at[index]))
        writes.append(pltpu.make_async_copy(held_out, target, sem_out.at[index]))

    for index in range(count):
        rows = pl.ds(index * DH, DH)
        unit, half = index // 2, index % 2
        if unit == 0:
            target = g_out.at[pl.ds(half * DH, DH), :]
        else:
            target = g_in.at[:, pl.ds(((2 - unit) * 2 + half) * D, D)]
        through(out.at[rows, :], low.at[rows, :], wide.at[rows, :], target)
    through(input_grad_in, kept_wide, kept_wide, input_grad)
    through(output_in, kept, kept, output)
    read_rows = pltpu.make_async_copy(out_rows, rows_low, sem_in.at[count + 2])
    read_rows.start()
    for copy in reads:
        copy.start()
    read_rows.wait()
    M = N + K + 4
    for part in range(3):
        value = rows_low[pl.ds(160 * part, 160), :].astype(F32)
        cols = pl.ds(256 * part, 256)
        g_a_log[:, cols] = value[:N]
        g_conv_w[:, cols] = value[N : N + K]
        g_conv_b[cols] = value[N + K]
        g_dt_bias[cols] = value[N + K + 1]
        g_skip[cols] = value[N + K + 2]
        if part == 0:
            g_gain[pl.ds(0, 256)] = value[N + K + 3]
        elif part == 1:
            g_gain[pl.ds(256, DH - 256)] = value[N + K + 3, : DH - 256]
        g_dt[:, cols] = value[M : M + R]
        g_xt[:, cols] = value[M + R : M + R + J]
    for index, held in enumerate(small):
        target = targets[(0, 2, 3, 4, 5, 6, 7, 8)[index]]
        writes.append(pltpu.make_async_copy(held, target, sem_out.at[count + 2 + index]))
        writes[-1].start()
    for index in range(count + 2):
        reads[index].wait()
        if index < count:
            rows = pl.ds(index * DH, DH)
            wide[rows, :] = low[rows, :].astype(F32)
        writes[index].start()
    for copy in writes:
        copy.wait()


def fused_body(tokens, lengths, cotangent, *shards):
    shards = list(shards)
    shards[4] = shards[4].T
    output, input_grad, out, out_rows = fused_layer(lengths, tokens[0], cotangent[0], *shards)
    gain, w_in, conv_w, conv_b, w_xt, w_dt, dt_bias, a_log, d_skip, w_out = shards
    kept = [out, jax.ShapeDtypeStruct(out.shape, F32), out_rows, output, input_grad]
    grads = [jax.ShapeDtypeStruct(w.shape, F32) for w in shards]
    small = [g for i, g in enumerate(grads) if i not in (1, 9)]
    results = pl.pallas_call(
        functools.partial(finish_kernel, a_log.shape[0], conv_w.shape[0], w_dt.shape[0], w_xt.shape[0]),
        out_shape=[jax.ShapeDtypeStruct(x.shape, x.dtype) for x in (output, input_grad)] + grads,
        in_specs=[ANY] * 4,
        out_specs=[ANY] * 12,
        scratch_shapes=[pltpu.VMEM(x.shape, x.dtype) for x in kept + small]
        + [pltpu.SemaphoreType.DMA((16,)), pltpu.SemaphoreType.DMA((24,))],
        compiler_params=pltpu.CompilerParams(vmem_limit_bytes=60 * MB),
        name="finish",
    )(out, out_rows, output, input_grad)
    output, input_grad, *grads = results
    grads[4] = grads[4].T
    return (output[None], input_grad[None], *grads)


def solution(mesh):
    seq, row, col, one = P(("dp", "fsdp"), None, None), P("fsdp", None), P(None, "fsdp"), P("fsdp")
    fused = mesh.shape["dp"] == PIECES and mesh.shape["fsdp"] == 2
    return jax.shard_map(
        fused_body if fused else plain_body,
        mesh=mesh,
        in_specs=(seq, P(("dp", "fsdp")), seq, one, row, col, one, row, col, one, col, one, row),
        out_specs=(seq, seq, one, row, col, one, row, col, one, col, one, row),
        check_vma=False,
    )
```

```python
import functools
import types

import jax
import jax.numpy as jnp
from jax import lax
from jax.experimental import pallas as pl
from jax.experimental.pallas import tpu as pltpu
from jax.sharding import PartitionSpec as P

F32 = jnp.float32
BF16 = jnp.bfloat16
EPS = 1e-05
STEPS = 16
CHUNK = 256
PAD = 8
LOG2E = 1.4426950408889634
MB = 2**20
VMEM = pl.BlockSpec(memory_space=pltpu.VMEM)
SMEM = pl.BlockSpec(memory_space=pltpu.SMEM)
ANY = pl.BlockSpec(memory_space=pl.ANY)
MESH = pl.DeviceIdType.MESH


def dot(left, right, over=(1, 0)):
    dims = (((over[0],), (over[1],)), ((), ()))
    return lax.dot_general(left, right, dims, preferred_element_type=F32)


def span(index, size):
    return pl.ds(pl.multiple_of(index * size, size), size)


def repeat(count, step, unroll=1):
    def run(index, carry):
        step(index)
        return carry

    lax.fori_loop(0, count, run, 0, unroll=min(unroll, count))


def row_plan(s):
    bias = s.N + s.K
    return types.SimpleNamespace(conv=s.N, bias=bias, dt_bias=bias + 1, skip=bias + 2, gain=bias + 3)


def start_norm(s):
    def run(block):
        rows = span(block, 64)
        x = s.tok[rows, :].astype(F32)
        scale = lax.rsqrt(jnp.mean(x * x, axis=1, keepdims=True) + EPS)
        s.inv[rows, :] = jnp.broadcast_to(scale, (64, 128))
        at = block * 64 + lax.broadcasted_iota(jnp.int32, (64, 1), 0)
        live = (at < s.length[0]).astype(F32)
        s.d_branch[rows, :] = (live * s.cot[rows, :].astype(F32)).astype(BF16)

    repeat(s.T // 64, run, 4)


def norm(s):
    def run(block):
        rows = span(block, 64)
        x = s.tok[rows, :].astype(F32)
        s.normed[rows, :] = (x * s.inv[rows, pl.ds(0, 1)] * s.gain[...]).astype(BF16)

    repeat(s.T // 64, run, 4)


def project_inner(s, first, count):
    at = row_plan(s)

    def run(index):
        cols = span(first + index, 256)
        s.inner[pl.ds(PAD, s.T), cols] = dot(s.normed[...], s.w_in[:, cols])

    repeat(count, run, 6)

    def convolve(index):
        cols = span(2 * first + index, 128)
        value = s.small[pl.ds(at.bias, 1), cols] + sum(
            s.small[pl.ds(at.conv + k, 1), cols] * s.inner[pl.ds(PAD - s.K + 1 + k, s.T), cols]
            for k in range(s.K)
        )
        sigma = jax.nn.sigmoid(value)
        s.active[:, cols] = (value * sigma).astype(BF16)
        s.cslope[:, cols] = sigma * (1.0 + value * (1.0 - sigma))

    repeat(2 * count, convolve, 4)


def project_gate(s, first, count):
    def run(index):
        cols = span(first + index, 256)
        source = pl.ds(pl.multiple_of(s.E + (first + index) * 256, 256), 256)
        value = dot(s.normed[...], s.w_in[:, source])
        sigma = jax.nn.sigmoid(value)
        s.gact[:, cols] = value * sigma
        s.gslope[:, cols] = sigma * (1.0 + value * (1.0 - sigma))

    repeat(count, run, 6)


def diagonal(s):
    wide = STEPS * s.N
    at = lax.broadcasted_iota(jnp.int32, (s.T, wide), 0)
    to = lax.broadcasted_iota(jnp.int32, (s.T, wide), 1)
    return (at % STEPS == to // s.N).astype(F32)


def spread_rows(s):
    N, J, wide = s.N, s.J, STEPS * s.N
    state = lax.broadcasted_iota(jnp.int32, (N, J), 0)
    col = lax.broadcasted_iota(jnp.int32, (N, J), 1)
    mask = jnp.logical_or(col == s.R + state, col == s.R + N + state).astype(F32)
    row = lax.broadcasted_iota(jnp.int32, (J, 256), 0)
    lane = lax.broadcasted_iota(jnp.int32, (J, 256), 1)
    first = jnp.logical_and(row < s.R + N, lane < 128)
    last = jnp.logical_and(row >= s.R + N, lane >= 128)
    ones = jnp.logical_or(first, last).astype(BF16)

    def run(block):
        rows = s.proj[span(block, STEPS), :].astype(F32)
        parts = [(jnp.broadcast_to(rows[i : i + 1], (N, J)) * mask).astype(BF16) for i in range(STEPS)]
        s.spread[span(block, wide), :] = dot(jnp.concatenate(parts, axis=0), ones)

    repeat(s.T // STEPS, run, 4)


def scan_inputs(s):
    wide = STEPS * s.N
    at = row_plan(s)
    s.proj[...] = dot(s.active[...], s.w_xt[...], (1, 1)).astype(BF16)
    row = lax.broadcasted_iota(jnp.int32, (s.J, wide), 0)
    col = lax.broadcasted_iota(jnp.int32, (s.J, wide), 1)
    mask = diagonal(s)
    pick_b = (row == s.R + col % s.N).astype(BF16)
    pick_c = (row == s.R + s.N + col % s.N).astype(BF16)
    s.bmat[...] = (dot(s.proj[...], pick_b) * mask).astype(BF16)
    s.cmat[...] = (dot(s.proj[...], pick_c) * mask).astype(BF16)
    spread_rows(s)

    def run(index):
        cols = span(index, 256)
        pre = dot(s.proj[:, : s.R], s.w_dt[:, cols]) + s.small[pl.ds(at.dt_bias, 1), cols]
        size = jnp.maximum(pre, 0.0) + jnp.log1p(jnp.exp(-jnp.abs(pre)))
        s.step[:, cols] = size
        s.sigp[:, cols] = jax.nn.sigmoid(pre)
        s.drive[:, cols] = size * s.active[:, cols].astype(F32)

    repeat(s.E // 256, run, 6)
    s.decay[...] = -jnp.exp(s.small[pl.ds(0, s.N), :]) * LOG2E


def forward_scan(s):
    N, E, wide = s.N, s.E, STEPS * s.N
    s.states[pl.ds(0, N), :] = jnp.zeros((N, E), BF16)

    def scan_sum(block):
        rows = span(block, STEPS)
        held = s.states[pl.ds(pl.multiple_of(block * wide + N, N), wide), :]
        s.mixed[rows, :] = dot(s.cmat[rows, :], held)

    def run(block, state):
        scan_sum(jnp.maximum(block - 1, 0))
        rows = span(block, STEPS)
        size, push = s.step[rows, :], s.drive[rows, :]
        for i in range(STEPS):
            t = block * STEPS + i
            b_row = s.spread[span(t, N), pl.ds(0, 128)]
            b_row = jnp.concatenate([b_row] * (E // 128), axis=1)
            factor = jnp.exp2(jnp.broadcast_to(size[i : i + 1], (N, E)) * s.decay[...])
            state = factor * state + b_row * jnp.broadcast_to(push[i : i + 1], (N, E))
            s.states[span(t + 1, N), :] = state.astype(BF16)
        return state

    lax.fori_loop(0, s.T // STEPS, run, jnp.zeros((N, E), F32))
    scan_sum(s.T // STEPS - 1)


def mix(s):
    at = row_plan(s)

    def run(index):
        cols = span(index, 128)
        value = s.mixed[pl.ds(0, s.T), cols] + s.small[pl.ds(at.skip, 1), cols] * s.active[:, cols].astype(F32)
        s.mixed[pl.ds(0, s.T), cols] = value
        s.gated[:, cols] = (value * s.gact[:, cols]).astype(BF16)

    repeat(s.E // 128, run, 2)


def back_out(s):
    at = row_plan(s)

    def run(index):
        cols = span(index, 256)
        d_gated = dot(s.d_branch[...], s.w_out[cols, :], (1, 1))
        d_value = d_gated * s.gact[:, cols]
        s.d_mixed[:, cols] = d_value
        s.d_gate[:, cols] = (d_gated * s.mixed[pl.ds(0, s.T), cols] * s.gslope[:, cols]).astype(BF16)
        s.rows[pl.ds(at.skip, 1), cols] = jnp.sum(
            d_value * s.active[:, cols].astype(F32), axis=0, keepdims=True
        )

    repeat(s.E // 256, run, 6)


def project_out(s):
    def run(index):
        cols = span(index, 256)
        branch = dot(s.gated[...], s.w_out[:, cols])
        at = lax.broadcasted_iota(jnp.int32, (s.T, 1), 0)
        live = (at < s.length[0]).astype(F32)
        s.output[:, cols] = (s.tok[:, cols].astype(F32) + live * branch).astype(BF16)

    repeat(s.D // 256, run, 3)


def backward_scan(s, between=None):
    N, E, wide, half = s.N, s.E, STEPS * s.N, s.N // 2
    blocks = s.T // STEPS
    s.carry[...] = jnp.zeros((N, E), F32)
    s.rows[pl.ds(0, N), :] = jnp.zeros((N, E), F32)
    at = lax.broadcasted_iota(jnp.int32, (STEPS, STEPS * half), 0)
    to = lax.broadcasted_iota(jnp.int32, (STEPS, STEPS * half), 1)
    gather = (at == to // half).astype(BF16)

    def run(k):
        block = blocks - 1 - k
        rows = span(block, STEPS)
        for chunk in range(E // CHUNK):
            cols = pl.ds(chunk * CHUNK, CHUNK)
            later, total = s.carry[:, cols], s.rows[pl.ds(0, N), cols]
            size, d_value = s.step[rows, cols], s.d_mixed[rows, cols]
            rate = s.decay[:, cols]
            for i in reversed(range(STEPS)):
                t = block * STEPS + i
                dt = jnp.broadcast_to(size[i : i + 1], (N, CHUNK))
                c_row = s.spread[span(t, N), pl.ds(128, 128)]
                c_row = jnp.concatenate([c_row] * (CHUNK // 128), axis=1)
                lam = c_row * jnp.broadcast_to(d_value[i : i + 1], (N, CHUNK)) + later
                s.lam[pl.ds(i * N, N), cols] = lam.astype(BF16)
                later = jnp.exp2(dt * rate) * lam
                weighted = later * s.states[span(t, N), cols].astype(F32)
                total = total + weighted * dt
                part = weighted * rate
                part = part[:half] + part[half:]
                if i % 2 == 1:
                    odd = part
                else:
                    s.part[pl.ds(i * half, N), cols] = jnp.concatenate([part, odd], axis=0).astype(BF16)
            s.carry[:, cols] = later
            s.rows[pl.ds(0, N), cols] = total
            held = s.lam[:, cols]
            s.gact[rows, cols] = dot(s.bmat[rows, :], held)
            s.gslope[rows, cols] = dot(gather, s.part[:, cols])
            b_part = dot(s.drive[rows, cols].astype(BF16), held, (1, 1))
            after = s.states[pl.ds(pl.multiple_of(block * wide + N, N), wide), cols]
            c_part = dot(d_value.astype(BF16), after, (1, 1))
            if chunk == 0:
                s.db[rows, :] = b_part
                s.dc[rows, :] = c_part
            else:
                s.db[rows, :] += b_part
                s.dc[rows, :] += c_part
        if between is not None:
            between(k)

    repeat(blocks, run)
    s.rows[pl.ds(0, N), :] = s.rows[pl.ds(0, N), :] * s.decay[...] * (1.0 / LOG2E)


def back_step(s):
    at = row_plan(s)

    def run(index):
        cols = span(index, 128)
        wide = s.active[:, cols].astype(F32)
        adjoint = s.gact[:, cols]
        d_pre = (wide * adjoint + s.gslope[:, cols] * (1.0 / LOG2E)) * s.sigp[:, cols]
        s.rows[pl.ds(at.dt_bias, 1), cols] = jnp.sum(d_pre, axis=0, keepdims=True)
        s.lam[:, cols] = d_pre.astype(BF16)
        s.d_mixed[:, cols] = (
            s.d_mixed[:, cols] * s.small[pl.ds(at.skip, 1), cols] + s.step[:, cols] * adjoint
        )

    repeat(s.E // 128, run)


def back_proj(s):
    wide = STEPS * s.N
    row = lax.broadcasted_iota(jnp.int32, (wide, s.N), 0)
    col = lax.broadcasted_iota(jnp.int32, (wide, s.N), 1)
    pick = (row % s.N == col).astype(BF16)
    mask = diagonal(s)
    s.d_proj[:, pl.ds(0, s.R)] = dot(s.lam[...], s.w_dt[...], (1, 1)).astype(BF16)
    s.d_proj[:, pl.ds(s.R, s.N)] = dot((s.db[...] * mask).astype(BF16), pick).astype(BF16)
    s.d_proj[:, pl.ds(s.R + s.N, s.N)] = dot((s.dc[...] * mask).astype(BF16), pick).astype(BF16)


def back_conv(s, part, count):
    at = row_plan(s)
    s.mixed[pl.ds(s.T, PAD), :] = jnp.zeros((PAD, s.E), F32)
    first = at.gain + 1

    def run(index):
        cols = span(part + index, 128)
        s.rows[pl.ds(first, s.R), cols] = dot(s.proj[:, : s.R], s.lam[:, cols], (0, 0))
        s.rows[pl.ds(first + s.R, s.J), cols] = dot(s.d_proj[...], s.active[:, cols], (0, 0))
        d_active = s.d_mixed[:, cols] + dot(s.d_proj[...], s.w_xt[:, cols])
        d_value = d_active * s.cslope[:, cols]
        s.mixed[pl.ds(0, s.T), cols] = d_value
        s.rows[pl.ds(at.bias, 1), cols] = jnp.sum(d_value, axis=0, keepdims=True)
        total = jnp.zeros_like(d_value)
        for k in range(s.K):
            s.rows[pl.ds(at.conv + k, 1), cols] = jnp.sum(
                d_value * s.inner[pl.ds(PAD - s.K + 1 + k, s.T), cols], axis=0, keepdims=True
            )
            taps = s.small[pl.ds(at.conv + k, 1), cols]
            total = total + taps * s.mixed[pl.ds(s.K - 1 - k, s.T), cols]
        s.d_inner[:, cols] = total.astype(BF16)

    repeat(count, run, 3)


def back_in(s):
    def run(index):
        rows = span(index, 256)
        s.step[:, rows] = dot(s.d_inner[...], s.w_in[rows, pl.ds(0, s.E)], (1, 1)) + dot(
            s.d_gate[...], s.w_in[rows, pl.ds(s.E, s.E)], (1, 1)
        )

    repeat(s.D // 256, run, 3)


def back_norm(s):
    s.d_gain[...] = jnp.zeros((1, s.D), F32)

    def run(block):
        rows = span(block, 64)
        x = s.tok[rows, :].astype(F32)
        scale = s.inv[rows, pl.ds(0, 1)]
        d_value = s.step[rows, pl.ds(0, s.D)]
        s.d_gain[...] += jnp.sum(d_value * x * scale, axis=0, keepdims=True)
        d_scaled = d_value * s.gain[...]
        shared = jnp.mean(d_scaled * x, axis=1, keepdims=True)
        s.input_grad[rows, :] = (
            s.cot[rows, :].astype(F32) + scale * d_scaled - x * (scale * scale * scale) * shared
        )

    repeat(s.T // 64, run, 4)


def sizes(tokens, w_out, a_log, w_dt, w_xt, conv_w):
    return dict(
        T=tokens.shape[0], D=tokens.shape[1], E=w_out.shape[0], N=a_log.shape[0],
        R=w_dt.shape[0], J=w_xt.shape[0], K=conv_w.shape[0],
    )


def scratch_plan(z):
    T, D, E, N, R, J, K = (z[n] for n in "TDENRJK")
    wide = STEPS * N
    full, low = ((T, E), F32), ((T, E), BF16)
    padded = ((T + PAD, E), F32)
    count = N + K + 4
    return dict(
        inv=((T, 128), F32), gain=((1, D), F32), small=((count, E), F32), inner=padded, gact=full, gslope=full,
        cslope=full, active=low, proj=((T, J), BF16), bmat=((T, wide), BF16), cmat=((T, wide), BF16),
        spread=((T * N, 256), F32), decay=((N, E), F32), step=full, sigp=full, drive=full,
        mixed=padded, d_mixed=full, states=(((T + 1) * N, E), BF16), carry=((N, E), F32),
        lam=((wide, E), BF16), part=((wide // 2, E), BF16), db=((T, wide), F32), dc=((T, wide), F32),
        d_proj=((T, J), BF16), d_gain=((1, D), F32),
    )


def plain_kernel(z, names, *refs):
    s = types.SimpleNamespace(**z, **dict(zip(names, refs)))
    at = row_plan(s)
    s.small[pl.ds(0, s.N), :] = s.a_log[...].astype(F32)
    s.small[pl.ds(at.conv, s.K), :] = s.conv_w[...].astype(F32)
    s.small[pl.ds(at.bias, 1), :] = s.conv_b[...].astype(F32)
    s.small[pl.ds(at.dt_bias, 1), :] = s.dt_bias[...].astype(F32)
    s.small[pl.ds(at.skip, 1), :] = s.d_skip[...].astype(F32)
    s.gain[...] = s.gain_in[...].astype(F32)
    s.rows[...] = jnp.zeros(s.rows.shape, F32)
    s.inner[pl.ds(0, PAD), :] = jnp.zeros((PAD, s.E), F32)
    for step in (start_norm, norm):
        step(s)
    project_inner(s, 0, s.E // 256)
    project_gate(s, 0, s.E // 256)
    for step in (scan_inputs, forward_scan, mix, project_out, back_out):
        step(s)
    backward_scan(s)
    back_step(s)
    back_proj(s)
    back_conv(s, 0, s.E // 128)
    back_in(s)
    back_norm(s)
    s.g_gain[...] = s.d_gain[...]


def plain_layer(length, tokens, cotangent, gain, w_in, conv_w, conv_b, w_xt, w_dt, dt_bias, a_log, d_skip, w_out):
    z = sizes(tokens, w_out, a_log, w_dt, w_xt, conv_w)
    T, D, E, N, R, J, K = (z[n] for n in "TDENRJK")
    plan = scratch_plan(z)
    ins = ("length", "tok", "cot", "gain_in", "w_in", "conv_w", "conv_b", "w_xt", "w_dt", "dt_bias", "a_log", "d_skip", "w_out")
    outs = dict(
        output=((T, D), BF16), input_grad=((T, D), F32), normed=((T, D), BF16), gated=((T, E), BF16),
        d_branch=((T, D), BF16), d_inner=((T, E), BF16), d_gate=((T, E), BF16), g_gain=((1, D), F32),
        rows=((N + K + 4 + R + J, E), F32),
    )
    names = list(ins) + list(outs) + list(plan)
    return pl.pallas_call(
        functools.partial(plain_kernel, z, names),
        out_shape=[jax.ShapeDtypeStruct(*spec) for spec in outs.values()],
        in_specs=[SMEM] + [VMEM] * 12,
        out_specs=[VMEM] * len(outs),
        scratch_shapes=[pltpu.VMEM(*spec) for spec in plan.values()],
        compiler_params=pltpu.CompilerParams(vmem_limit_bytes=60 * MB),
        name="plain_layer",
    )(length, tokens, cotangent, gain, w_in, conv_w, conv_b, w_xt, w_dt, dt_bias, a_log, d_skip, w_out)


def plain_body(tokens, lengths, cotangent, *shards):
    axes = (0, 0, 1, 0, 0, 1, 0, 1, 0, 0)
    weights = [lax.all_gather(w, "fsdp", axis=a, tiled=True) for w, a in zip(shards, axes)]
    weights = [w.reshape(1, -1) if w.ndim == 1 else w for w in weights]
    weights[4] = weights[4].T
    output, input_grad, normed, gated, d_branch, d_inner, d_gate, g_gain, rows = plain_layer(
        lengths, tokens[0], cotangent[0], *weights
    )
    big_in = dot(normed, jnp.concatenate([d_inner, d_gate], axis=1), (0, 0))
    big_out = dot(gated, d_branch, (0, 0))

    def scatter(value, axis):
        return lax.psum_scatter(value, "fsdp", scatter_dimension=axis, tiled=True)

    own = (
        scatter(big_in.astype(BF16), 0), scatter(big_out.astype(BF16), 0),
        scatter(rows, 1), scatter(g_gain[0], 0),
    )
    own_in, own_out, rows, own_gain = lax.psum(own, "dp")
    N, K, R = shards[7].shape[0], shards[2].shape[0], shards[5].shape[0]
    M = N + K + 4
    return (
        output[None], input_grad[None], own_gain, own_in.astype(F32), rows[N : N + K], rows[N + K],
        rows[M + R :].T, rows[M : M + R], rows[N + K + 1], rows[:N], rows[N + K + 2], own_out.astype(F32),
    )


ORDERS = (
    ((2,), (0,), (3,), (1,)),
    ((0, 1), (2, 3)),
    ((1,), (0,), (2, 3)),
    ((1,), (0,), (2, 3)),
    ((2,), (1,), (0,), (3,)),
    ((0,), (1,), (2, 3)),
    ((0,), (1,), (2, 3)),
    ((1,), (0,), (2, 3)),
    ((2,), (0, 1), (3,)),
    ((0, 1), (3,), (2,)),
)
DURING = {
    6: ((0, 0), (1, 0)),
    9: ((4, 0),),
    10: ((2, 0), (5, 0)),
    11: ((1, 1), (0, 1)),
    13: ((3, 0),),
    14: ((2, 1),),
    15: ((4, 1), (1, 2)),
    16: ((5, 1), (0, 2), (3, 1)),
    18: ((4, 2), (2, 2)),
    19: ((5, 2), (0, 3), (1, 3)),
    20: ((3, 2),),
    21: ((4, 3),),
}
AFTER = (
    (6, 0), (0, 4), (2, 3), (7, 0), (8, 0), (5, 3), (9, 0), (3, 3), (6, 1), (2, 4), (7, 1), (4, 4),
    (9, 1), (0, 5), (8, 1), (5, 4), (6, 2), (3, 4), (9, 2), (7, 2), (4, 5), (8, 2), (9, 3), (0, 6),
    (6, 3), (2, 5), (7, 3), (5, 5), (8, 3), (3, 5), (7, 4), (4, 6), (6, 4), (9, 4), (0, 7), (8, 4),
    (6, 5), (7, 5), (4, 7), (8, 5), (9, 5),
)
PIECES = 16
FIRST, SECOND = 0, 2
GATHERS = 10
SWAPS = 7
COPIES = 12


def packed_rows(s):
    return s.N + s.K + 4


class Sum:
    def __init__(self, s, number, stages, acc, recv, out, result, first, piece):
        self.s, self.stages, self.piece, self.steps = s, stages, piece, 2 * len(stages)
        self.sem = GATHERS + SWAPS + COPIES * number
        self.acc, self.recv, self.out = acc, recv, out
        self.first, self.landed = first * PIECES * piece, first * (PIECES - 1) * piece
        self.bits = [[lax.rem(s.dp // 2**b, 2) for b in stage] for stage in stages]
        whole = pl.ds(self.first, PIECES * piece)
        self.leave = pltpu.make_async_copy(out.at[whole, :], result.at[whole, :], s.local.at[6 + number])
        self.plan = []
        start, count, landing, sem = 0, PIECES, 0, self.sem
        for stage, bits in zip(stages, self.bits):
            group = 2 ** len(stage)
            count //= group
            others = []
            for flip in range(1, group):
                device, place = s.dp, 0
                for j, (b, bit) in enumerate(zip(stage, bits)):
                    flipped = flip // 2**j % 2
                    device = device + flipped * (1 - 2 * bit) * 2**b
                    place = place + (flipped + (1 - 2 * flipped) * bit) * 2**j
                others.append(((device, s.me), start + place * count, landing, sem))
                landing, sem = landing + count, sem + 2
            for j, bit in enumerate(bits):
                start = start + bit * 2**j * count
            self.plan.append((others, start, count))

    def rows(self, start, count):
        return pl.ds(pl.multiple_of(self.first + start * self.piece, 16), count * self.piece)

    def reduce_copies(self, level):
        others, _, count = self.plan[level]
        return [
            self.s.remote(
                self.acc.at[self.rows(theirs, count), :],
                self.recv.at[pl.ds(self.landed + landing * self.piece, count * self.piece), :], sem, device,
            )
            for device, theirs, landing, sem in others
        ]

    def spread_copies(self, level, sent=True):
        others, mine, count = self.plan[level]
        copies = []
        for device, theirs, _, sem in others:
            rows = self.rows(mine if sent else theirs, count)
            copies.append(self.s.remote(self.out.at[rows, :], self.out.at[rows, :], sem + 1, device))
        return copies

    def start(self):
        for copy in self.reduce_copies(0):
            copy.start()

    def carry_on(self, step):
        levels = len(self.stages)
        if step < levels:
            self.reduce(step)
            following = self.spread_copies(step) if step == levels - 1 else self.reduce_copies(step + 1)
        else:
            level = self.steps - 1 - step
            for copy in self.spread_copies(level, False):
                copy.wait_recv()
            following = self.spread_copies(level - 1) if level > 0 else [self.leave]
        for copy in following:
            copy.start()

    def reduce(self, level):
        for copy in self.reduce_copies(level):
            copy.wait_recv()
        others, mine, count = self.plan[level]
        target = self.out if level == len(self.stages) - 1 else self.acc

        def add(index):
            here = self.rows(mine + index, 1)
            total = self.acc[here, :].astype(F32)
            for _, _, landing, _ in others:
                there = pl.ds(pl.multiple_of(self.landed + (landing + index) * self.piece, 16), self.piece)
                total = total + self.recv[there, :].astype(F32)
            target[here, :] = total.astype(BF16)

        repeat(count, add)

    def finish(self):
        for level in range(len(self.stages)):
            for copy in self.reduce_copies(level) + self.spread_copies(level):
                copy.wait_send()
        self.leave.wait()


def fused_kernel(z, names, *refs):
    s = types.SimpleNamespace(**z, **dict(zip(names, refs)))
    D, E = s.D, s.E
    DH, EH = D // 2, E // 2
    at = row_plan(s)
    count = packed_rows(s)
    s.dp, s.me = lax.axis_index("dp"), lax.axis_index("fsdp")
    other = 1 - s.me
    peer = (s.dp, other)

    def remote(src, dst, sem, device):
        return pltpu.make_async_remote_copy(
            src_ref=src, dst_ref=dst, send_sem=s.send.at[sem], recv_sem=s.recv_sem.at[sem],
            device_id=device, device_id_type=MESH,
        )

    s.remote = remote
    units = [Sum(s, i, ORDERS[i], s.acc, s.recv, s.out, s.out_to, i, 16) for i in range(9)]
    units.append(Sum(s, 9, ORDERS[9], s.acc_rows, s.recv_rows, s.out_rows, s.out_rows_to, 0, 32))

    barrier = pltpu.get_barrier_semaphore()
    pl.semaphore_signal(barrier, inc=1, device_id=peer, device_id_type=MESH)
    partners = {}
    for unit in units:
        for stage, (others, _, _) in zip(unit.stages, unit.plan):
            for flip, other_one in enumerate(others):
                partners[(stage, flip)] = other_one[0]
    greeted = {}
    for (stage, flip), device in partners.items():
        greeted[tuple(sorted(b for j, b in enumerate(stage) if (flip + 1) // 2**j % 2))] = device
    for device in greeted.values():
        pl.semaphore_signal(barrier, inc=1, device_id=device, device_id_type=MESH)

    mine_d, mine_e = span(s.me, DH), span(s.me, EH)
    theirs_d, theirs_e = span(other, DH), span(other, EH)
    local_in = pltpu.make_async_copy(s.w_in_own, s.w_in.at[mine_d, :], s.local.at[0])
    local_out = pltpu.make_async_copy(s.w_out_own, s.w_out.at[mine_e, :], s.local.at[1])
    local_tok = pltpu.make_async_copy(s.tok_own, s.tok, s.local.at[2])
    local_cot = pltpu.make_async_copy(s.cot_own, s.cot, s.local.at[3])
    for copy in (local_tok, local_cot, local_in, local_out):
        copy.start()
    s.pack[pl.ds(0, s.N), :] = s.a_log[...].astype(F32)
    s.pack[pl.ds(at.conv, s.K), :] = s.conv_w[...].astype(F32)
    s.pack[pl.ds(at.bias, 1), :] = s.conv_b[...].astype(F32)[None, :]
    s.pack[pl.ds(at.dt_bias, 1), :] = s.dt_bias[...].astype(F32)[None, :]
    s.pack[pl.ds(at.skip, 1), :] = s.d_skip[...].astype(F32)[None, :]
    s.pack[pl.ds(at.gain, 1), :] = jnp.zeros((1, EH), F32)
    s.pack[pl.ds(at.gain, 1), pl.ds(0, DH)] = s.gain_own[...].astype(F32)[None, :]
    pl.semaphore_wait(barrier, len(greeted) + 1)

    width = 2 * E // 6
    gathers = [remote(s.pack, s.pack_in, 0, peer)]
    for j in range(6):
        cols = pl.ds(j * width, width)
        gathers.append(remote(s.w_in_own.at[:, cols], s.w_in.at[mine_d, cols], 1 + j, peer))
    gathers.append(remote(s.w_xt_own, s.w_xt_in, 7, peer))
    gathers.append(remote(s.w_dt_own, s.w_dt_in, 8, peer))
    gathers.append(remote(s.w_out_own, s.w_out.at[mine_e, :], 9, peer))
    for j in (0, 1, 2, 3, 7, 8, 4, 5, 6, 9):
        gathers[j].start()

    swaps = [
        remote(s.normed.at[:, theirs_d], s.normed_in, GATHERS, peer),
        remote(s.d_branch, s.d_branch_in, GATHERS + 1, peer),
        remote(s.gated.at[:, theirs_e], s.gated_in, GATHERS + 2, peer),
        remote(s.d_gate, s.d_gate_in, GATHERS + 3, peer),
        remote(s.d_inner.at[:, pl.ds(0, EH)], s.d_inner_in.at[:, pl.ds(0, EH)], GATHERS + 4, peer),
        remote(s.d_inner.at[:, pl.ds(EH, EH)], s.d_inner_in.at[:, pl.ds(EH, EH)], GATHERS + 5, peer),
        remote(s.rows.at[:, theirs_e], s.rows_in, GATHERS + 6, peer),
    ]

    local_tok.wait()
    local_cot.wait()
    start_norm(s)
    swaps[1].start()
    s.w_xt[:, mine_e] = s.w_xt_own[...]
    s.w_dt[:, mine_e] = s.w_dt_own[...]
    s.small[:, mine_e] = s.pack[...]
    s.gain[:, mine_d] = s.pack[pl.ds(at.gain, 1), pl.ds(0, DH)]
    s.inner[pl.ds(0, PAD), :] = jnp.zeros((PAD, E), F32)
    gathers[0].wait_recv()
    s.small[:, theirs_e] = s.pack_in[...]
    s.gain[:, theirs_d] = s.pack_in[pl.ds(at.gain, 1), pl.ds(0, DH)]
    norm(s)
    swaps[0].start()
    local_in.wait()
    for j in range(3):
        gathers[1 + j].wait_recv()
        project_inner(s, 2 * j, 2)
    gathers[7].wait_recv()
    gathers[8].wait_recv()
    s.w_dt[:, theirs_e] = s.w_dt_in[...]
    s.w_xt[:, theirs_e] = s.w_xt_in[...]
    scan_inputs(s)
    for j in range(3):
        gathers[4 + j].wait_recv()
        project_gate(s, 2 * j, 2)
    forward_scan(s)
    mix(s)
    swaps[2].start()
    local_out.wait()
    gathers[9].wait_recv()
    back_out(s)
    swaps[3].start()
    def product(left, left_in, right, right_in, shift, cols, across):
        own = pl.ds(pl.multiple_of(shift + cols.start, 128), cols.size)
        total = dot(left[:, own], right[:, across], (0, 0)) + dot(left_in[:, cols], right_in[:, across], (0, 0))
        return total.astype(BF16)

    def grad_out(color):
        cols = pl.ds(256 * color, 256)
        s.acc[pl.ds(256 * color, 256), :] = product(
            s.gated, s.gated_in, s.d_branch, s.d_branch_in, s.me * EH, cols, pl.ds(0, D)
        )

    def grad_in(unit, color, right, right_in):
        first = 256 * (3 * unit + color)
        parts = (((0, 256, 0),), ((256, 128, 0), (0, 128, EH)), ((128, 256, EH),))[color]
        for start, size, across in parts:
            s.acc[pl.ds(first, size), :] = product(
                s.normed, s.normed_in, right, right_in, s.me * DH, pl.ds(start, size), pl.ds(across, EH)
            )
            first += size

    def carry_on(events):
        for index, step in events:
            units[index].carry_on(step)

    def first_sums():
        swaps[1].wait_recv()
        swaps[2].wait_recv()
        for color in range(3):
            grad_out(color)
            units[color].start()

    def second_sums():
        swaps[0].wait_recv()
        swaps[3].wait_recv()
        for color in range(3):
            grad_in(1, color, s.d_gate, s.d_gate_in)
            units[3 + color].start()

    def between(k):
        pl.when(k == FIRST)(first_sums)
        pl.when(k == SECOND)(second_sums)
        for when, events in DURING.items():
            if when < s.T // STEPS:
                pl.when(k == when)(functools.partial(carry_on, events))

    def phase(number, step):
        step(s)
        carry_on(DURING.get(number, ()))

    s.rows[pl.ds(at.gain, 1), :] = jnp.zeros((1, E), F32)
    backward_scan(s, between)
    phase(16, back_step)
    phase(17, back_proj)
    back_conv(s, 0, 6)
    swaps[4].start()
    back_conv(s, 6, 6)
    swaps[5].start()
    carry_on(DURING.get(18, ()))
    for color in range(3):
        if color < 2:
            swaps[4 + color].wait_recv()
        grad_in(2, color, s.d_inner, s.d_inner_in)
        units[6 + color].start()
        if color == 0:
            phase(19, back_in)
    carry_on(DURING.get(20, ()))
    back_norm(s)
    s.rows[pl.ds(at.gain, 1), pl.ds(0, DH)] = s.d_gain[:, pl.ds(0, DH)]
    s.rows[pl.ds(at.gain, 1), pl.ds(EH, DH)] = s.d_gain[:, pl.ds(DH, DH)]
    swaps[6].start()
    leaving = [pltpu.make_async_copy(s.input_grad, s.input_grad_to, s.local.at[5])]
    leaving[0].start()
    carry_on(DURING.get(21, ()))
    project_out(s)
    leaving.append(pltpu.make_async_copy(s.output, s.output_to, s.local.at[4]))
    leaving[1].start()
    carry_on(DURING.get(22, ()))
    swaps[6].wait_recv()
    total = s.rows.shape[0]
    s.acc_rows[...] = jnp.zeros(s.acc_rows.shape, BF16)
    for part in range(3):
        own = pl.ds(pl.multiple_of(s.me * EH + 256 * part, 128), 256)
        value = s.rows[:, own] + s.rows_in[:, pl.ds(256 * part, 256)]
        value = jnp.concatenate([value, jnp.zeros((160 - total, 256), F32)], axis=0)
        s.acc_rows[pl.ds(160 * part, 160), :] = value.astype(BF16)
    units[9].start()
    carry_on(AFTER)
    for copy in leaving:
        copy.wait()
    for copy in gathers + swaps:
        copy.wait_send()
    for unit in units:
        unit.finish()


def fused_layer(length, tokens, cotangent, gain, w_in, conv_w, conv_b, w_xt, w_dt, dt_bias, a_log, d_skip, w_out):
    z = sizes(tokens, jax.ShapeDtypeStruct((2 * w_out.shape[0], w_out.shape[1]), BF16), a_log, w_dt, w_xt, conv_w)
    T, D, E, N, R, J, K = (z[n] for n in "TDENRJK")
    DH, EH = D // 2, E // 2
    total = N + K + 4 + R + J
    names = ("length", "tok_own", "cot_own", "gain_own", "w_in_own", "conv_w", "conv_b", "w_xt_own", "w_dt_own", "dt_bias", "a_log", "d_skip", "w_out_own")
    outs = dict(
        output_to=((T, D), BF16), input_grad_to=((T, D), F32), out_to=((9 * 256, D), BF16), out_rows_to=((512, 256), BF16)
    )
    plan = scratch_plan(z)
    plan.update(
        w_in=((D, 2 * E), BF16), w_out=((E, D), BF16), w_xt=((J, E), BF16), w_dt=((R, E), BF16),
        pack=((N + K + 4, EH), F32), pack_in=((N + K + 4, EH), F32), w_dt_in=((R, EH), BF16), w_xt_in=((J, EH), BF16),
        normed=((T, D), BF16), gated=((T, E), BF16), d_branch=((T, D), BF16), d_inner=((T, E), BF16),
        d_gate=((T, E), BF16), rows=((total, E), F32), normed_in=((T, DH), BF16), d_branch_in=((T, D), BF16),
        gated_in=((T, EH), BF16), d_gate_in=((T, E), BF16), d_inner_in=((T, E), BF16), rows_in=((total, EH), F32),
        tok=((T, D), BF16), cot=((T, D), BF16), output=((T, D), BF16), input_grad=((T, D), F32),
        out=((9 * 256, D), BF16), out_rows=((512, 256), BF16),
        acc=((9 * 256, D), BF16), recv=((9 * 240, D), BF16), acc_rows=((512, 256), BF16), recv_rows=((480, 256), BF16),
    )
    sems = GATHERS + SWAPS + COPIES * 10
    names = list(names) + list(outs) + list(plan) + ["local", "send", "recv_sem"]
    specs = [SMEM] + [VMEM] * 12
    specs[1] = specs[2] = specs[4] = specs[12] = ANY
    return pl.pallas_call(
        functools.partial(fused_kernel, z, names),
        out_shape=[jax.ShapeDtypeStruct(*spec) for spec in outs.values()],
        in_specs=specs,
        out_specs=[ANY] * len(outs),
        scratch_shapes=[pltpu.VMEM(*spec) for spec in plan.values()]
        + [pltpu.SemaphoreType.DMA((16,)), pltpu.SemaphoreType.DMA((sems,)), pltpu.SemaphoreType.DMA((sems,))],
        compiler_params=pltpu.CompilerParams(collective_id=0, has_side_effects=True, vmem_limit_bytes=63 * MB),
        name="layer",
    )(length, tokens, cotangent, gain, w_in, conv_w, conv_b, w_xt, w_dt, dt_bias, a_log, d_skip, w_out)


def finish_kernel(N, K, R, J, *refs):
    out, out_rows, output_in, input_grad_in, output, input_grad = refs[:6]
    targets = refs[6:16]
    g_in, g_out = targets[1], targets[9]
    low, wide, rows_low, kept, kept_wide, *small = refs[16:29]
    sem_in, sem_out = refs[29:]
    g_gain, g_conv_w, g_conv_b, g_xt, g_dt, g_dt_bias, g_a_log, g_skip = small
    DH, D = g_in.shape[0], out.shape[1]
    count = out.shape[0] // DH
    reads, writes = [], []

    def through(source, held, held_out, target):
        index = len(reads)
        reads.append(pltpu.make_async_copy(source, held, sem_in.at[index]))
        writes.append(pltpu.make_async_copy(held_out, target, sem_out.at[index]))

    for index in range(count):
        rows = pl.ds(index * DH, DH)
        unit, half = index // 2, index % 2
        if unit == 0:
            target = g_out.at[pl.ds(half * DH, DH), :]
        else:
            target = g_in.at[:, pl.ds(((2 - unit) * 2 + half) * D, D)]
        through(out.at[rows, :], low.at[rows, :], wide.at[rows, :], target)
    through(input_grad_in, kept_wide, kept_wide, input_grad)
    through(output_in, kept, kept, output)
    read_rows = pltpu.make_async_copy(out_rows, rows_low, sem_in.at[count + 2])
    read_rows.start()
    for copy in reads:
        copy.start()
    read_rows.wait()
    M = N + K + 4
    for part in range(3):
        value = rows_low[pl.ds(160 * part, 160), :].astype(F32)
        cols = pl.ds(256 * part, 256)
        g_a_log[:, cols] = value[:N]
        g_conv_w[:, cols] = value[N : N + K]
        g_conv_b[cols] = value[N + K]
        g_dt_bias[cols] = value[N + K + 1]
        g_skip[cols] = value[N + K + 2]
        if part == 0:
            g_gain[pl.ds(0, 256)] = value[N + K + 3]
        elif part == 1:
            g_gain[pl.ds(256, DH - 256)] = value[N + K + 3, : DH - 256]
        g_dt[:, cols] = value[M : M + R]
        g_xt[:, cols] = value[M + R : M + R + J]
    for index, held in enumerate(small):
        target = targets[(0, 2, 3, 4, 5, 6, 7, 8)[index]]
        writes.append(pltpu.make_async_copy(held, target, sem_out.at[count + 2 + index]))
        writes[-1].start()
    for index in range(count + 2):
        reads[index].wait()
        if index < count:
            rows = pl.ds(index * DH, DH)
            wide[rows, :] = low[rows, :].astype(F32)
        writes[index].start()
    for copy in writes:
        copy.wait()


def fused_body(tokens, lengths, cotangent, *shards):
    shards = list(shards)
    shards[4] = shards[4].T
    output, input_grad, out, out_rows = fused_layer(lengths, tokens[0], cotangent[0], *shards)
    gain, w_in, conv_w, conv_b, w_xt, w_dt, dt_bias, a_log, d_skip, w_out = shards
    kept = [out, jax.ShapeDtypeStruct(out.shape, F32), out_rows, output, input_grad]
    grads = [jax.ShapeDtypeStruct(w.shape, F32) for w in shards]
    small = [g for i, g in enumerate(grads) if i not in (1, 9)]
    results = pl.pallas_call(
        functools.partial(finish_kernel, a_log.shape[0], conv_w.shape[0], w_dt.shape[0], w_xt.shape[0]),
        out_shape=[jax.ShapeDtypeStruct(x.shape, x.dtype) for x in (output, input_grad)] + grads,
        in_specs=[ANY] * 4,
        out_specs=[ANY] * 12,
        scratch_shapes=[pltpu.VMEM(x.shape, x.dtype) for x in kept + small]
        + [pltpu.SemaphoreType.DMA((16,)), pltpu.SemaphoreType.DMA((24,))],
        compiler_params=pltpu.CompilerParams(vmem_limit_bytes=60 * MB),
        name="finish",
    )(out, out_rows, output, input_grad)
    output, input_grad, *grads = results
    grads[4] = grads[4].T
    return (output[None], input_grad[None], *grads)


def solution(mesh):
    seq, row, col, one = P(("dp", "fsdp"), None, None), P("fsdp", None), P(None, "fsdp"), P("fsdp")
    fused = mesh.shape["dp"] == PIECES and mesh.shape["fsdp"] == 2
    return jax.shard_map(
        fused_body if fused else plain_body,
        mesh=mesh,
        in_specs=(seq, P(("dp", "fsdp")), seq, one, row, col, one, row, col, one, col, one, row),
        out_specs=(seq, seq, one, row, col, one, row, col, one, col, one, row),
        check_vma=False,
    )
```
